32 devices in a mesh: leaf: 8 (over z, y), rhs: 4 (over x, core).
Axes of the slice: x: 2, y: 2, z: 4, core: 2. Of those that a mesh axis runs over, the one named last changes fastest.
Arguments:
- right_side: bfloat16 [64, 32768], P(None, ('leaf', 'rhs')), may hold values from -6 to 6
- point_order: int32 [32768], P('leaf'), may hold values from 0 to 4095, as said below
- leaf_inverse: bfloat16 [64, 512, 512], P('leaf', 'rhs')
- leaf_basis: bfloat16 [64, 512, 256], P('leaf', 'rhs'), may hold values from -0.25 to 0.25
- leaf_coupling: bfloat16 [64, 512, 256], P('leaf', 'rhs'), may hold values from -0.1875 to 0.1875
- node_inverse: bfloat16 [64, 512, 512], P('leaf', 'rhs')
- node_basis: bfloat16 [64, 512, 256], P('leaf', 'rhs'), may hold values from -0.25 to 0.25
- node_coupling: bfloat16 [64, 512, 256], P('leaf', 'rhs'), may hold values from -0.375 to 0.375
Outputs:
- coefficients: float32 [64, 64, 512], P('leaf', None, 'rhs')
The draws below stay inside these ranges and needn't reach their ends.
Inputs may be any that keep to these rules, and one draw needn't show every extreme that they name: `point_order`: within each block of 4096 entries that one index of leaf holds, every number from 0 to 4095 stands once.
All inputs are finite; a program needn't handle non-finite values.
Results may differ from the reference program's by a relative error of at most 0.03.
Values may be sent and summed in bfloat16 or wider, within the bound.
No kernel may reach another device: no remote copies, remote signals or barrier semaphores. Data moves between devices by JAX's collectives and lax.ppermute only.
A program may use at most 64 MiB of HBM per device.

```python
import jax
import jax.numpy as jnp
import numpy as np
from jax import lax

LEAF = 512
RANK = 256
NRHS = 64
LPD = 8
NODE = 512
NL = 64
NPOINTS = 32768
LOCAL = 3
KX = 3
N_LEAF = 8


def with_diagonal(diag_key, off_values, size):
    diagonal = jnp.exp(jax.random.uniform(diag_key, off_values.shape[:2], jnp.float32, jnp.log(0.4), jnp.log(1.6)))
    identity = jnp.eye(size, dtype=jnp.float32)
    return off_values * (1.0 - identity) + identity * diagonal[:, :, None]


def group_order(group_key):
    return jax.random.permutation(group_key, LPD * LEAF)


def draw_point_order(key, part):
    key = jax.random.fold_in(key, 1)
    group_keys = jax.random.split(key, NL // LPD)
    orders = jax.vmap(group_order)(group_keys)
    return orders.reshape(-1).astype(jnp.int32)


def draw_leaf_inverse(key, part):
    key = jax.random.fold_in(key, 2)
    diag_key, off_key = jax.random.split(key)
    off_values = 0.4 * jax.random.truncated_normal(off_key, -4.0, 4.0, (NL, LEAF, LEAF), jnp.float32) / LEAF ** 0.5
    return with_diagonal(diag_key, off_values, LEAF).astype(jnp.bfloat16)


def draw_node_inverse(key, part):
    key = jax.random.fold_in(key, 3)
    diag_key, off_key = jax.random.split(key)
    off_values = 0.4 * jax.random.truncated_normal(off_key, -4.0, 4.0, (NL, NODE, NODE), jnp.float32) / NODE ** 0.5
    return with_diagonal(diag_key, off_values, NODE).astype(jnp.bfloat16)


def block_scale(rng, dims, pieces, least, largest):
    gain = 1.0
    for dim, shards_of in pieces:
        steps = jax.random.uniform(jax.random.fold_in(jax.random.fold_in(rng, 6), dim), (shards_of,), jnp.float32, least / len(pieces), largest / len(pieces))
        gain = gain * jnp.repeat(jnp.exp(steps), dims[dim] // shards_of).reshape((-1,) + (1,) * (len(dims) - 1 - dim))
    return gain


def normal_values(key, shape, width, most, cuts=(), kind=jnp.bfloat16):
    result = width * jax.random.normal(key, shape, jnp.float32)
    if cuts:
        result = result * block_scale(key, shape, cuts, -0.22, 0.18)
    return jnp.clip(result, -most, most).astype(kind)


def setup_inputs(seed: int = 0) -> dict:
    key_list = jax.random.split(jax.random.key(seed), 9)
    return {
        "right_side": normal_values(key_list[0], (NRHS, NPOINTS), 1.0, 6.0, ((1, 32),)),
        "point_order": draw_point_order(jax.random.fold_in(key_list[8], 71), 0),
        "leaf_inverse": draw_leaf_inverse(jax.random.fold_in(key_list[8], 71), 0),
        "leaf_basis": normal_values(key_list[3], (NL, LEAF, RANK), LEAF ** -0.5, 0.25, ((0, 8), (1, 4))),
        "leaf_coupling": normal_values(key_list[4], (NL, LEAF, RANK), (4 * RANK) ** -0.5, 0.1875, ((0, 8), (1, 4))),
        "node_inverse": draw_node_inverse(jax.random.fold_in(key_list[8], 71), 0),
        "node_basis": normal_values(key_list[6], (NL, NODE, RANK), NODE ** -0.5, 0.25, ((0, 8), (1, 4))),
        "node_coupling": normal_values(key_list[7], (NL, NODE, RANK), RANK ** -0.5, 0.375, ((0, 8), (1, 4))),
    }


def product(left_side, right_side_mat, form):
    return jnp.einsum(form, left_side.astype(jnp.float32), right_side_mat.astype(jnp.float32))


def rounded(values):
    return lax.optimization_barrier(values.astype(jnp.bfloat16))


def pair_up(values):
    return jnp.concatenate([values[0::2], values[1::2]], axis=-1)


def split_down(values, rank_size):
    joined = jnp.stack([values[..., :rank_size], values[..., rank_size:]], axis=1)
    return joined.reshape((-1,) + values.shape[1:-1] + (rank_size,))


def owner_list(height):
    return (2 * np.arange(N_LEAF >> height) + 1) * (1 << (height - 1))


def group_up(arguments):
    ordered, inverse, basis, node_inv, node_bas = arguments
    leaf_values = product(ordered, inverse, "lsj,lij->lsi")
    compressed = product(rounded(leaf_values), basis, "lsi,lik->lsk").astype(jnp.bfloat16)
    solved_all = []
    for height in range(1, LOCAL + 1):
        node_count = LPD >> height
        offset = LPD - 2 * node_count
        solved = product(pair_up(compressed), node_inv[offset:offset + node_count], "nsj,nij->nsi")
        solved_all.append(solved)
        compressed = product(rounded(solved), node_bas[offset:offset + node_count], "nsi,nik->nsk").astype(jnp.bfloat16)
    return leaf_values, compressed[0], solved_all


def group_down(arguments):
    incoming, solved_all, node_cou, leaf_values, coupling = arguments
    current = incoming[None]
    for height in range(LOCAL, 0, -1):
        node_count = LPD >> height
        offset = LPD - 2 * node_count
        node_value = solved_all[height - 1] - product(current, node_cou[offset:offset + node_count], "nsk,nik->nsi")
        current = split_down(node_value.astype(jnp.bfloat16), RANK)
    return leaf_values - product(current, coupling, "lsk,lik->lsi")


def reference(right_side, point_order, leaf_inverse, leaf_basis, leaf_coupling, node_inverse, node_basis, node_coupling):
    blocks = right_side.reshape(NRHS, N_LEAF, LPD * LEAF)
    order_rows = jnp.broadcast_to(point_order.reshape(1, N_LEAF, LPD * LEAF), blocks.shape)
    ordered = jnp.take_along_axis(blocks, order_rows, axis=2)
    ordered = ordered.reshape(NRHS, N_LEAF, LPD, LEAF).transpose(1, 2, 0, 3)
    node_inv = node_inverse.reshape(N_LEAF, LPD, NODE, NODE)
    node_bas = node_basis.reshape(N_LEAF, LPD, NODE, RANK)
    node_cou = node_coupling.reshape(N_LEAF, LPD, NODE, RANK)
    leaf_values, compressed, solved_all = lax.map(group_up, (
        ordered,
        leaf_inverse.reshape(N_LEAF, LPD, LEAF, LEAF),
        leaf_basis.reshape(N_LEAF, LPD, LEAF, RANK),
        node_inv, node_bas))
    cross_inv = node_inv[:, LPD - 1]
    cross_bas = node_bas[:, LPD - 1]
    cross_cou = node_cou[:, LPD - 1]
    cross_solved = []
    for height in range(1, KX + 1):
        owners = owner_list(height)
        solved = product(pair_up(compressed), cross_inv[owners], "nsj,nij->nsi")
        cross_solved.append(solved)
        if height < KX:
            compressed = product(rounded(solved), cross_bas[owners], "nsi,nik->nsk").astype(jnp.bfloat16)
    node_value = cross_solved[KX - 1]
    incoming = split_down(node_value.astype(jnp.bfloat16), RANK)
    for height in range(KX, 0, -1):
        incoming = split_down(node_value.astype(jnp.bfloat16), RANK)
        if height > 1:
            owners = owner_list(height - 1)
            node_value = cross_solved[height - 2] - product(incoming, cross_cou[owners], "nsk,nik->nsi")
    coefficients = lax.map(group_down, (
        incoming, solved_all, node_cou, leaf_values,
        leaf_coupling.reshape(N_LEAF, LPD, LEAF, RANK)))
    return coefficients.reshape(NL, NRHS, LEAF)
```

```python
import functools

import jax
import jax.numpy as jnp
from jax import lax
from jax.experimental import pallas as pl
from jax.experimental.pallas import tpu as pltpu
from jax.sharding import PartitionSpec as P

LANES = 256
PIECES = (0, 2, 1, 3)
CORES = 2


def params(mebibytes=12):
    return pltpu.CompilerParams(vmem_limit_bytes=mebibytes * 1024 * 1024)


def cost(flops, moved):
    return pl.CostEstimate(flops=flops // 1000, bytes_accessed=moved // 1000, transcendentals=0)


def dot_rows(left, right):
    return lax.dot_general(
        left, right, (((1,), (1,)), ((), ())), preferred_element_type=jnp.float32
    )


def half_levels(per_dev):
    levels = []
    base = 0
    for height in range(1, per_dev.bit_length() - 1):
        node_count = per_dev >> height
        levels.append((base, node_count // 2, per_dev - 2 * node_count))
        base += node_count // 2
    return levels, base


def pack_kernel(per_dev, inverse, basis, coupling, *refs):
    targets, buffers, (sems, out_sems) = refs[:4], refs[4:8], refs[8:]
    factors, couplings, keep, cross = buffers
    levels, total = half_levels(per_dev)
    high = lax.axis_index("rhs") // CORES
    node_size = inverse.shape[2]
    rank = basis.shape[2]
    parts = (
        (inverse, 0, node_size),
        (basis, node_size, rank),
        (coupling, node_size + rank, rank),
    )
    copies = []
    for source, start, width in parts:
        columns = pl.ds(start, width)
        for base, count, offset in levels:
            mine = source.at[pl.ds(offset + high * count, count)]
            other = source.at[pl.ds(offset + (1 - high) * count, count)]
            if source is coupling:
                for n in range(count):
                    sent = couplings.at[:, pl.ds((base + n) * rank, rank)]
                    copies.append((other.at[n], sent))
            else:
                copies.append((other, factors.at[pl.ds(base, count), :, columns]))
            copies.append((mine, keep.at[pl.ds(base, count), :, columns]))
        copies.append((source.at[per_dev - 2], keep.at[total, :, columns]))
        copies.append((source.at[per_dev - 1], cross.at[:, columns]))
    started = []
    for i, (source, target) in enumerate(copies):
        copy = pltpu.make_async_copy(source, target, sems.at[i])
        copy.start()
        started.append(copy)
    for copy in started:
        copy.wait()
    started = []
    for i, (buffer, target) in enumerate(zip(buffers, targets)):
        copy = pltpu.make_async_copy(buffer, target, out_sems.at[i])
        copy.start()
        started.append(copy)
    for copy in started:
        copy.wait()


def pack(inverse, basis, coupling):
    per_dev, rows, node_size = inverse.shape
    rank = basis.shape[2]
    width = node_size + 2 * rank
    levels, total = half_levels(per_dev)
    shapes = [
        (total, rows, node_size + rank),
        (rows, total * rank),
        (total + 1, rows, width),
        (rows, width),
    ]
    return pl.pallas_call(
        functools.partial(pack_kernel, per_dev),
        in_specs=[pl.BlockSpec(memory_space=pl.ANY)] * 3,
        out_specs=[pl.BlockSpec(memory_space=pl.ANY)] * 4,
        out_shape=[jax.ShapeDtypeStruct(shape, inverse.dtype) for shape in shapes],
        scratch_shapes=[pltpu.VMEM(shape, inverse.dtype) for shape in shapes]
        + [pltpu.SemaphoreType.DMA((6 + 5 * len(levels) + total,)), pltpu.SemaphoreType.DMA((4,))],
        compiler_params=params(63),
        cost_estimate=cost(0, 4 * per_dev * rows * width),
    )(inverse, basis, coupling)


def climb_kernel(level, mine_ref, other_ref, ancestor_ref, carrier_ref):
    right = (lax.axis_index("leaf") // (1 << level)) % 2 == 1
    keep = carrier_ref.shape[1]

    @pl.when(right)
    def _():
        ancestor_ref[...] = mine_ref[...]
        carrier_ref[...] = other_ref[:, :keep]

    @pl.when(jnp.logical_not(right))
    def _():
        ancestor_ref[...] = other_ref[...]
        carrier_ref[...] = mine_ref[:, :keep]


def climb(level, mine, other, keep):
    return pl.pallas_call(
        functools.partial(climb_kernel, level),
        out_shape=[
            pltpu.VMEM(mine.shape, mine.dtype),
            pltpu.VMEM((mine.shape[0], keep), mine.dtype),
        ],
        compiler_params=params(),
        cost_estimate=cost(0, 4 * mine.size),
    )(mine, other)


def join_kernel(*refs):
    *blocks, _, out_ref = refs
    start = 0
    for ref in blocks:
        width = ref.shape[1]
        out_ref[:, start : start + width] = ref[...]
        start += width


def join(blocks, anchor):
    rows = blocks[0].shape[0]
    width = sum(block.shape[1] for block in blocks)
    return pl.pallas_call(
        join_kernel,
        out_shape=pltpu.VMEM((rows, width), blocks[0].dtype),
        compiler_params=params(),
        cost_estimate=cost(0, 4 * rows * width),
    )(*blocks, anchor)


def leaf_kernel(count, side_ref, *refs):
    points, refs = refs[:count], refs[count:]
    order_ref, inverse_ref, basis_ref, values_ref, same_ref, cross_ref, *rest = refs
    targets = values_ref.shape[1]
    stacked = rest[0] if rest else points[0]
    chunks, pieces = stacked.shape[:2]

    if rest:

        @pl.when(pl.program_id(0) == 0)
        def _():
            place = lax.axis_index("rhs")
            for flip, points_ref in zip(PIECES, points):
                for w in range(pieces):
                    stacked[place ^ flip, w] = points_ref[:, w * LANES : (w + 1) * LANES]

    order = order_ref[...]
    high = order // LANES
    low = order % LANES
    rows = lax.broadcasted_iota(jnp.int32, (LANES, order.shape[1]), 0)
    pick = jnp.where(rows == low, 1.0, 0.0).astype(jnp.bfloat16)
    spread = jnp.dot(
        stacked[...].reshape(-1, LANES), pick, preferred_element_type=jnp.float32
    )
    ordered = jnp.zeros((targets, order.shape[1]), jnp.float32)
    for k in range(chunks * pieces):
        ordered = jnp.where(high == k, spread[k * targets : (k + 1) * targets, :], ordered)
    values = dot_rows(ordered.astype(jnp.bfloat16), inverse_ref[0])
    values_ref[0] = values
    partial = jnp.dot(
        values.astype(jnp.bfloat16), basis_ref[0], preferred_element_type=jnp.float32
    ).astype(jnp.bfloat16)
    share = targets // CORES
    for core in range(CORES):

        @pl.when(side_ref[1] == core)
        def _():
            same_ref[0] = partial[core * share : (core + 1) * share]
            cross_ref[0] = partial[(1 - core) * share : (2 - core) * share]


def leaf_up(side, points, point_order, leaf_inverse, leaf_basis):
    leaves, rows, leaf_size = leaf_inverse.shape
    rank = leaf_basis.shape[2]
    half = leaves // 2
    joined = points[0].ndim == 4
    if joined:
        shape = points[0].shape
    else:
        targets, width = points[0].shape
        shape = (len(points), width // LANES, targets, LANES)
    targets = shape[2]
    share = targets // CORES
    sent = jax.ShapeDtypeStruct((half, share, rank), jnp.bfloat16)
    out_specs = [
        pl.BlockSpec((1, targets, rows), lambda i, side: (i, 0, 0)),
        pl.BlockSpec((1, share, rank), lambda i, side: (i, 0, 0)),
        pl.BlockSpec((1, share, rank), lambda i, side: (i, 0, 0)),
    ]
    out_shape = [jax.ShapeDtypeStruct((half, targets, rows), jnp.float32), sent, sent]
    if not joined:
        out_specs.append(pl.BlockSpec(shape, lambda i, side: (0, 0, 0, 0)))
        out_shape.append(pltpu.VMEM(shape, jnp.bfloat16))
    point_specs = [
        pl.BlockSpec(block.shape, lambda i, side, rank=block.ndim: (0,) * rank) for block in points
    ]
    return pl.pallas_call(
        functools.partial(leaf_kernel, len(points)),
        grid_spec=pltpu.PrefetchScalarGridSpec(
            num_scalar_prefetch=1,
            grid=(half,),
            in_specs=[
                *point_specs,
                pl.BlockSpec((1, leaf_size), lambda i, side: (0, side[0] * half + i)),
                pl.BlockSpec((1, rows, leaf_size), lambda i, side: (side[0] * half + i, 0, 0)),
                pl.BlockSpec((1, rows, rank), lambda i, side: (side[0] * half + i, 0, 0)),
            ],
            out_specs=out_specs,
        ),
        out_shape=out_shape,
        compiler_params=params(),
        cost_estimate=cost(
            leaves * targets * leaf_size * (shape[0] * shape[1] * LANES + 2 * rows),
            leaves * rows * (leaf_size + rank + 3 * targets),
        ),
    )(side, *points, point_order.reshape(1, -1), leaf_inverse, leaf_basis)


def solve_node(stacked, inverses, bases, solved_ref):
    mine = lax.axis_index("rhs")
    total = None
    for flip, inverse, basis in zip(PIECES, inverses, bases):
        solved = dot_rows(stacked, inverse)
        solved_ref[mine ^ flip] = solved
        term = jnp.dot(solved.astype(jnp.bfloat16), basis, preferred_element_type=jnp.float32)
        total = term if total is None else total + term
    return total


def group_up_kernel(per_dev, *refs):
    *refs, solved_ref, out_ref = refs
    parts, packs = refs[: 2 * CORES], refs[2 * CORES :]
    levels, _ = half_levels(per_dev)
    rank = parts[0].shape[2]

    def pieces(node, start, width):
        return [ref[node, :, pl.ds(start, width)] for ref in packs]

    sums = sum(ref[...].astype(jnp.float32) for ref in parts).astype(jnp.bfloat16)
    current = [sums[i] for i in range(sums.shape[0])]
    for base, count, _ in levels:
        following = []
        for n in range(count):
            node = base + n
            compressed = solve_node(
                jnp.concatenate([current[2 * n], current[2 * n + 1]], axis=1),
                pieces(node, 0, 2 * rank),
                pieces(node, 2 * rank, rank),
                solved_ref.at[node],
            )
            following.append(compressed.astype(jnp.bfloat16))
        current = following
    out_ref[...] = current[0]


def group_up(per_dev, parts, packs):
    leaves, share, rank = parts[0].shape
    _, total = half_levels(per_dev)
    _, rows, width = packs[0].shape
    return pl.pallas_call(
        functools.partial(group_up_kernel, per_dev),
        out_shape=[
            jax.ShapeDtypeStruct((total, 2 * CORES, share, rows), jnp.float32),
            jax.ShapeDtypeStruct((share, rank), jnp.bfloat16),
        ],
        compiler_params=params(),
        cost_estimate=cost(24 * total * share * rows * rank, 8 * total * rows * width),
    )(*parts, *packs)


def order_pair(right, mine, other):
    return jnp.concatenate([jnp.where(right, other, mine), jnp.where(right, mine, other)], axis=1)


def half_up_kernel(mine_ref, other_ref, own_ref, near_ref, solved_ref, out_ref):
    rank = mine_ref.shape[1]
    place = lax.axis_index("rhs")
    stacked = order_pair(place // CORES == 1, mine_ref[...], other_ref[...])
    total = 0.0
    for flip, ref in enumerate((own_ref, near_ref)):
        solved = dot_rows(stacked, ref[0, :, : 2 * rank])
        solved_ref[(place ^ flip) % CORES] = solved
        total += jnp.dot(
            solved.astype(jnp.bfloat16),
            ref[0, :, 2 * rank : 3 * rank],
            preferred_element_type=jnp.float32,
        )
    out_ref[...] = total.astype(jnp.bfloat16)


def half_up(mine, other, own, near):
    share, rank = mine.shape
    nodes, rows, width = own.shape
    last = pl.BlockSpec((1, rows, width), lambda i: (nodes - 1, 0, 0))
    whole = pl.BlockSpec((share, rank), lambda i: (0, 0))
    return pl.pallas_call(
        half_up_kernel,
        grid=(1,),
        in_specs=[whole, whole, last, last],
        out_specs=[pl.BlockSpec((CORES, share, rows), lambda i: (0, 0, 0)), whole],
        out_shape=[
            jax.ShapeDtypeStruct((CORES, share, rows), jnp.float32),
            jax.ShapeDtypeStruct((share, rank), jnp.bfloat16),
        ],
        compiler_params=params(),
        cost_estimate=cost(12 * share * rows * rank, 4 * rows * width),
    )(mine, other, own, near)


def total_of(refs):
    if len(refs) == 1:
        return refs[0][...]
    return sum(ref[...].astype(jnp.float32) for ref in refs).astype(jnp.bfloat16)


def cross_pair(level, refs):
    half = len(refs) // 2
    is_right = (lax.axis_index("leaf") // (1 << level)) % 2 == 1
    return order_pair(is_right, total_of(refs[:half]), total_of(refs[half:]))


def cross_up_kernel(level, *refs):
    *refs, solved_ref, out_ref = refs
    inputs, packs = refs[: -2 * CORES], refs[-2 * CORES :]
    rank = out_ref.shape[1]
    compressed = solve_node(
        cross_pair(level, inputs),
        [ref[:, : 2 * rank] for ref in packs],
        [ref[:, 2 * rank : 3 * rank] for ref in packs],
        solved_ref,
    )
    out_ref[...] = compressed.astype(jnp.bfloat16)


def cross_up(level, inputs, packs):
    share, rank = inputs[0].shape[-2:]
    rows, width = packs[0].shape
    return pl.pallas_call(
        functools.partial(cross_up_kernel, level),
        out_shape=[
            jax.ShapeDtypeStruct((2 * CORES, share, rows), jnp.float32),
            jax.ShapeDtypeStruct((share, rank), jnp.bfloat16),
        ],
        compiler_params=params(),
        cost_estimate=cost(24 * share * rows * rank, 8 * rows * width),
    )(*inputs, *packs)


def down_kernel(per_dev, cross_levels, input_count, *refs):
    *refs, out_ref, value = refs
    inputs, refs = refs[:input_count], refs[input_count:]
    solved_cross, refs = refs[: cross_levels - 1], refs[cross_levels - 1 :]
    solved_top, solved_half, refs = refs[0], refs[1], refs[2:]
    count = 2 * CORES * (cross_levels - 1)
    cross_packs, (own_top, tail, near_tail, keep, keep_near) = refs[:count], refs[count:]
    levels, total = half_levels(per_dev)
    rank = out_ref.shape[2]
    node_size = 2 * rank
    place = lax.axis_index("rhs")

    def pieces(level):
        return zip(PIECES, cross_packs[2 * CORES * level : 2 * CORES * (level + 1)])

    def choose(which):
        return jnp.concatenate([value[2 * which], value[2 * which + 1]], axis=1)

    def side(level):
        return (lax.axis_index("leaf") // (1 << level)) % 2

    def columns(ref):
        width = ref.shape[-1]
        return pl.ds(width - rank, rank)

    stacked = cross_pair(cross_levels - 1, inputs)
    tops = (
        own_top[...],
        tail[:, :node_size],
        near_tail[:, :node_size],
        near_tail[:, node_size : 2 * node_size],
    )
    for flip, block in zip(PIECES, tops):
        value[place ^ flip] = dot_rows(stacked, block).astype(jnp.bfloat16)
    incoming = choose(side(cross_levels - 1))
    for level in range(cross_levels - 2, -1, -1):
        for flip, ref in pieces(level):
            piece = place ^ flip
            solved = solved_cross[level][piece]
            value[piece] = (solved - dot_rows(incoming, ref[:, columns(ref)])).astype(jnp.bfloat16)
        incoming = choose(side(level))

    for flip, ref in ((0, keep), (1, keep_near)):
        piece = (place ^ flip) % CORES
        coupling = ref[total, :, columns(ref)]
        value[piece] = (solved_top[piece] - dot_rows(incoming, coupling)).astype(jnp.bfloat16)
    current = [choose(0)]
    for base, count, _ in reversed(levels):
        following = []
        for n in range(count):
            node = base + n
            start = node_size + node * rank
            couplings = (
                keep[node, :, columns(keep)],
                tail[:, start : start + rank],
                keep_near[node, :, columns(keep)],
                near_tail[:, node_size + start : node_size + start + rank],
            )
            for flip, coupling in zip(PIECES, couplings):
                piece = place ^ flip
                value[piece] = (
                    solved_half[node, piece] - dot_rows(current[n], coupling)
                ).astype(jnp.bfloat16)
            following += [choose(0), choose(1)]
        current = following
    for i, block in enumerate(current):
        out_ref[i] = block


def way_down(per_dev, inputs, solved_cross, solved_top, solved_half, cross_packs, others):
    share, rank = inputs[0].shape[-2:]
    rows = solved_half.shape[3]
    operands = [*inputs, *solved_cross, solved_top, solved_half]
    for packs in cross_packs:
        operands += packs
    operands += others
    return pl.pallas_call(
        functools.partial(down_kernel, per_dev, len(cross_packs) + 1, len(inputs)),
        out_shape=jax.ShapeDtypeStruct((per_dev // 2, share, rank), jnp.bfloat16),
        scratch_shapes=[pltpu.VMEM((2 * CORES, share, rows), jnp.bfloat16)],
        compiler_params=params(18),
        cost_estimate=cost(8 * share * rows * rank * per_dev, 4 * 1024 * 1024),
    )(*operands)


def finish_kernel(far_ref, own_ref, incoming_ref, coupling_ref, out_ref):
    half = own_ref.shape[0]
    high = lax.axis_index("rhs") // CORES
    for values_ref, side in ((far_ref, 1 - high), (own_ref, high)):
        for i in range(half):
            leaf = side * half + i
            incoming = jnp.concatenate(
                [incoming_ref[side * CORES + core, i] for core in range(CORES)], axis=0
            )
            out_ref[leaf] = values_ref[i] - dot_rows(incoming, coupling_ref[leaf])


def finish(far, own, incoming, coupling):
    half, targets, rows = own.shape
    return pl.pallas_call(
        finish_kernel,
        out_shape=jax.ShapeDtypeStruct((2 * half, targets, rows), jnp.float32),
        compiler_params=params(),
        cost_estimate=cost(4 * half * targets * rows * coupling.shape[2], 16 * own.size),
    )(far, own, incoming, coupling)


def swap(block, axis, bit):
    return lax.ppermute(block, axis, [(i, i ^ bit) for i in range(lax.axis_size(axis))])


def far_swap(block, leaf_bit, rhs_bit):
    shares = lax.axis_size("rhs")
    flip = leaf_bit * shares + rhs_bit
    count = lax.axis_size("leaf") * shares
    return lax.ppermute(block, ("leaf", "rhs"), [(i, i ^ flip) for i in range(count)])


def after(value, anchor):
    return lax.optimization_barrier((value, anchor))[0]


def body(
    right_side,
    point_order,
    leaf_inverse,
    leaf_basis,
    leaf_coupling,
    node_inverse,
    node_basis,
    node_coupling,
):
    devices = lax.axis_size("leaf")
    per_dev = leaf_inverse.shape[0]
    node_size = node_inverse.shape[2]
    cross_levels = devices.bit_length() - 1
    place = lax.axis_index("rhs")
    high, low = place // CORES, place % CORES

    def rise(carrier, level, anchor):
        other = after(swap(carrier, "leaf", 1 << level), anchor)
        width = node_size if level >= cross_levels - 2 else carrier.shape[1]
        return climb(level, carrier, other, width)

    send, send_coupling, keep, carrier = pack(node_inverse, node_basis, node_coupling)
    across, beside = after(
        [swap(right_side, "rhs", CORES), swap(right_side, "rhs", 1)], send
    )
    points = [across, beside, swap(after(across, beside), "rhs", 1)]
    half_far = swap(send, "rhs", CORES)
    keep_near = swap(after(keep, points), "rhs", 1)
    carrier = after(carrier, points)
    points = [right_side, *points]

    leaves = (point_order, leaf_inverse, leaf_basis)
    far_values, far_same, far_cross, joined = leaf_up(
        jnp.stack([1 - high, low]), points, *leaves
    )
    keep_near = after(keep_near, far_same)
    own_values, own_same, own_cross = leaf_up(
        jnp.stack([high, low]), [after(joined, keep_near)], *leaves
    )
    ancestor, carrier = rise(carrier, 0, own_same)
    ancestors = [ancestor]
    far_same = after(swap(far_same, "rhs", CORES), own_same)
    far_cross = after(swap(far_cross, "rhs", CORES + 1), own_same)
    parts = [own_same, far_same, swap(own_cross, "rhs", 1), far_cross]
    half_far = after(half_far, (parts, carrier))
    half_near = swap(half_far, "rhs", 1)
    fars = [swap(after(ancestors[0], half_far), "rhs", CORES)]
    nears = [swap(after(ancestors[0], half_far), "rhs", 1)]

    solved_half, current = group_up(per_dev, parts, [keep, half_far, keep_near, half_near])
    other = swap(after(current, nears[0]), "rhs", CORES)
    ancestor, carrier = rise(carrier, 1, other)
    ancestors.append(ancestor)
    solved_top, current = half_up(current, other, keep, keep_near)
    fars[0] = after(fars[0], other)
    near_far = swap(fars[0], "rhs", 1)
    cross_packs = [[ancestors[0], fars[0], nears[0], near_far]]
    fars.append(swap(join([ancestors[1]], current), "rhs", CORES))
    current = after(current, near_far)
    inputs = [
        current,
        swap(current, "rhs", CORES),
        swap(current, "leaf", 1),
        far_swap(current, 1, CORES),
    ]

    solved_cross = []
    for level in range(cross_levels - 1):
        if level > 0:
            own, far = ancestors[level], fars[level]
            own_near = swap(join([own], current), "rhs", 1)
            far_near = swap(join([far], current), "rhs", 1)
            cross_packs.append([own, far, own_near, far_near])
        solved, current = cross_up(level, inputs, cross_packs[level])
        solved_cross.append(solved)
        inputs = [current, swap(current, "leaf", 2 << level)]
        if level == 0:
            for later in range(2, cross_levels):
                ancestor, carrier = rise(carrier, later, current)
                ancestors.append(ancestor)
            for later in range(2, cross_levels - 1):
                fars.append(swap(join([ancestors[later]], current), "rhs", CORES))
            tail = swap(join([ancestors[-1], send_coupling], current), "rhs", CORES)

    near_tail = swap(join([ancestors[-1], tail], inputs[1]), "rhs", 1)
    others = [ancestors[-1], tail, near_tail, keep, keep_near]
    shares = way_down(per_dev, inputs, solved_cross, solved_top, solved_half, cross_packs, others)
    incoming = lax.all_gather(shares, "rhs", axis=0)
    return finish(far_values, own_values, incoming, leaf_coupling)


def solution(mesh):
    placed = (P(None, ("leaf", "rhs")), P("leaf")) + (P("leaf", "rhs", None),) * 6
    return jax.shard_map(
        body, mesh=mesh, in_specs=placed, out_specs=P("leaf", None, "rhs"), check_vma=False
    )
```

```python
import functools

import jax
import jax.numpy as jnp
from jax import lax
from jax.experimental import pallas as pl
from jax.experimental.pallas import tpu as pltpu
from jax.sharding import PartitionSpec as P

LANES = 256
PIECES = (0, 2, 1, 3)
CORES = 2


def params(mebibytes=12):
    return pltpu.CompilerParams(vmem_limit_bytes=mebibytes * 1024 * 1024)


def cost(flops, moved):
    return pl.CostEstimate(flops=flops // 1000, bytes_accessed=moved // 1000, transcendentals=0)


def dot_rows(left, right):
    return lax.dot_general(
        left, right, (((1,), (1,)), ((), ())), preferred_element_type=jnp.float32
    )


def half_levels(per_dev):
    levels = []
    base = 0
    for height in range(1, per_dev.bit_length() - 1):
        node_count = per_dev >> height
        levels.append((base, node_count // 2, per_dev - 2 * node_count))
        base += node_count // 2
    return levels, base


def pack_kernel(per_dev, inverse, basis, coupling, *refs):
    targets, buffers, (sems, out_sems) = refs[:4], refs[4:8], refs[8:]
    factors, couplings, keep, cross = buffers
    levels, total = half_levels(per_dev)
    high = lax.axis_index("rhs") // CORES
    node_size = inverse.shape[2]
    rank = basis.shape[2]
    parts = (
        (inverse, 0, node_size),
        (basis, node_size, rank),
        (coupling, node_size + rank, rank),
    )
    copies = []
    for source, start, width in parts:
        columns = pl.ds(start, width)
        for base, count, offset in levels:
            mine = source.at[pl.ds(offset + high * count, count)]
            other = source.at[pl.ds(offset + (1 - high) * count, count)]
            if source is coupling:
                for n in range(count):
                    sent = couplings.at[:, pl.ds((base + n) * rank, rank)]
                    copies.append((other.at[n], sent))
            else:
                copies.append((other, factors.at[pl.ds(base, count), :, columns]))
            copies.append((mine, keep.at[pl.ds(base, count), :, columns]))
        copies.append((source.at[per_dev - 2], keep.at[total, :, columns]))
        copies.append((source.at[per_dev - 1], cross.at[:, columns]))
    started = []
    for i, (source, target) in enumerate(copies):
        copy = pltpu.make_async_copy(source, target, sems.at[i])
        copy.start()
        started.append(copy)
    for copy in started:
        copy.wait()
    started = []
    for i, (buffer, target) in enumerate(zip(buffers, targets)):
        copy = pltpu.make_async_copy(buffer, target, out_sems.at[i])
        copy.start()
        started.append(copy)
    for copy in started:
        copy.wait()


def pack(inverse, basis, coupling):
    per_dev, rows, node_size = inverse.shape
    rank = basis.shape[2]
    width = node_size + 2 * rank
    levels, total = half_levels(per_dev)
    shapes = [
        (total, rows, node_size + rank),
        (rows, total * rank),
        (total + 1, rows, width),
        (rows, width),
    ]
    return pl.pallas_call(
        functools.partial(pack_kernel, per_dev),
        in_specs=[pl.BlockSpec(memory_space=pl.ANY)] * 3,
        out_specs=[pl.BlockSpec(memory_space=pl.ANY)] * 4,
        out_shape=[jax.ShapeDtypeStruct(shape, inverse.dtype) for shape in shapes],
        scratch_shapes=[pltpu.VMEM(shape, inverse.dtype) for shape in shapes]
        + [pltpu.SemaphoreType.DMA((6 + 5 * len(levels) + total,)), pltpu.SemaphoreType.DMA((4,))],
        compiler_params=params(63),
        cost_estimate=cost(0, 4 * per_dev * rows * width),
    )(inverse, basis, coupling)


def climb_kernel(level, mine_ref, other_ref, ancestor_ref, *carrier_refs):
    right = (lax.axis_index("leaf") // (1 << level)) % 2 == 1

    @pl.when(right)
    def _():
        ancestor_ref[...] = mine_ref[...]
        for ref in carrier_refs:
            ref[...] = other_ref[:, : ref.shape[1]]

    @pl.when(jnp.logical_not(right))
    def _():
        ancestor_ref[...] = other_ref[...]
        for ref in carrier_refs:
            ref[...] = mine_ref[:, : ref.shape[1]]


def climb(level, mine, other, keep):
    return pl.pallas_call(
        functools.partial(climb_kernel, level),
        out_shape=[pltpu.VMEM(mine.shape, mine.dtype)]
        + [pltpu.VMEM((mine.shape[0], size), mine.dtype) for size in keep],
        compiler_params=params(),
        cost_estimate=cost(0, 4 * mine.size),
    )(mine, other)


def join_kernel(cuts, *refs):
    *blocks, _, out_ref = refs
    start = 0
    for ref, (first, width) in zip(blocks, cuts):
        out_ref[:, start : start + width] = ref[:, first : first + width]
        start += width


def join(blocks, anchor, cuts=None):
    rows = blocks[0].shape[0]
    cuts = cuts or [(0, block.shape[1]) for block in blocks]
    width = sum(size for _, size in cuts)
    return pl.pallas_call(
        functools.partial(join_kernel, cuts),
        out_shape=pltpu.VMEM((rows, width), blocks[0].dtype),
        compiler_params=params(),
        cost_estimate=cost(0, 4 * rows * width),
    )(*blocks, anchor)


def hop_kernel(level, top_ref, tail_ref, _, out_ref):
    node_size = top_ref.shape[1]
    side = (lax.axis_index("leaf") // (1 << level)) % 2
    here = lax.axis_index("rhs") // CORES == side
    out_ref[:, node_size:] = tail_ref[:, node_size:]

    @pl.when(here)
    def _():
        out_ref[:, :node_size] = top_ref[...]

    @pl.when(jnp.logical_not(here))
    def _():
        out_ref[:, :node_size] = tail_ref[:, :node_size]


def hop(level, top, tail, anchor):
    return pl.pallas_call(
        functools.partial(hop_kernel, level),
        out_shape=pltpu.VMEM(tail.shape, tail.dtype),
        compiler_params=params(),
        cost_estimate=cost(0, 4 * tail.size),
    )(top, tail, anchor)


def leaf_kernel(count, side_ref, *refs):
    points, refs = refs[:count], refs[count:]
    order_ref, inverse_ref, basis_ref, values_ref, same_ref, cross_ref, *rest = refs
    targets = values_ref.shape[1]
    stacked = rest[0] if rest else points[0]
    chunks, pieces = stacked.shape[:2]

    if rest:

        @pl.when(pl.program_id(0) == 0)
        def _():
            place = lax.axis_index("rhs")
            for flip, points_ref in zip(PIECES, points):
                for w in range(pieces):
                    stacked[place ^ flip, w] = points_ref[:, w * LANES : (w + 1) * LANES]

    order = order_ref[...]
    high = order // LANES
    low = order % LANES
    rows = lax.broadcasted_iota(jnp.int32, (LANES, order.shape[1]), 0)
    pick = jnp.where(rows == low, 1.0, 0.0).astype(jnp.bfloat16)
    spread = jnp.dot(
        stacked[...].reshape(-1, LANES), pick, preferred_element_type=jnp.float32
    )
    ordered = jnp.zeros((targets, order.shape[1]), jnp.float32)
    for k in range(chunks * pieces):
        ordered = jnp.where(high == k, spread[k * targets : (k + 1) * targets, :], ordered)
    values = dot_rows(ordered.astype(jnp.bfloat16), inverse_ref[0])
    values_ref[0] = values
    partial = jnp.dot(
        values.astype(jnp.bfloat16), basis_ref[0], preferred_element_type=jnp.float32
    ).astype(jnp.bfloat16)
    share = targets // CORES
    for core in range(CORES):

        @pl.when(side_ref[1] == core)
        def _():
            same_ref[0] = partial[core * share : (core + 1) * share]
            cross_ref[0] = partial[(1 - core) * share : (2 - core) * share]


def leaf_up(side, points, point_order, leaf_inverse, leaf_basis):
    leaves, rows, leaf_size = leaf_inverse.shape
    rank = leaf_basis.shape[2]
    half = leaves // 2
    joined = points[0].ndim == 4
    if joined:
        shape = points[0].shape
    else:
        targets, width = points[0].shape
        shape = (len(points), width // LANES, targets, LANES)
    targets = shape[2]
    share = targets // CORES
    sent = jax.ShapeDtypeStruct((half, share, rank), jnp.bfloat16)
    out_specs = [
        pl.BlockSpec((1, targets, rows), lambda i, side: (i, 0, 0)),
        pl.BlockSpec((1, share, rank), lambda i, side: (i, 0, 0)),
        pl.BlockSpec((1, share, rank), lambda i, side: (i, 0, 0)),
    ]
    out_shape = [jax.ShapeDtypeStruct((half, targets, rows), jnp.float32), sent, sent]
    if not joined:
        out_specs.append(pl.BlockSpec(shape, lambda i, side: (0, 0, 0, 0)))
        out_shape.append(pltpu.VMEM(shape, jnp.bfloat16))
    point_specs = [
        pl.BlockSpec(block.shape, lambda i, side, rank=block.ndim: (0,) * rank) for block in points
    ]
    return pl.pallas_call(
        functools.partial(leaf_kernel, len(points)),
        grid_spec=pltpu.PrefetchScalarGridSpec(
            num_scalar_prefetch=1,
            grid=(half,),
            in_specs=[
                *point_specs,
                pl.BlockSpec((1, leaf_size), lambda i, side: (0, side[0] * half + i)),
                pl.BlockSpec((1, rows, leaf_size), lambda i, side: (side[0] * half + i, 0, 0)),
                pl.BlockSpec((1, rows, rank), lambda i, side: (side[0] * half + i, 0, 0)),
            ],
            out_specs=out_specs,
        ),
        out_shape=out_shape,
        compiler_params=params(),
        cost_estimate=cost(
            leaves * targets * leaf_size * (shape[0] * shape[1] * LANES + 2 * rows),
            leaves * rows * (leaf_size + rank + 3 * targets),
        ),
    )(side, *points, point_order.reshape(1, -1), leaf_inverse, leaf_basis)


def solve_node(stacked, inverses, bases, solved_ref):
    mine = lax.axis_index("rhs")
    total = None
    for flip, inverse, basis in zip(PIECES, inverses, bases):
        solved = dot_rows(stacked, inverse)
        solved_ref[mine ^ flip] = solved
        term = jnp.dot(solved.astype(jnp.bfloat16), basis, preferred_element_type=jnp.float32)
        total = term if total is None else total + term
    return total


def group_up_kernel(per_dev, *refs):
    *refs, solved_ref, out_ref = refs
    parts, packs = refs[: 2 * CORES], refs[2 * CORES :]
    levels, _ = half_levels(per_dev)
    rank = parts[0].shape[2]

    def pieces(node, start, width):
        return [ref[node, :, pl.ds(start, width)] for ref in packs]

    sums = sum(ref[...].astype(jnp.float32) for ref in parts).astype(jnp.bfloat16)
    current = [sums[i] for i in range(sums.shape[0])]
    for base, count, _ in levels:
        following = []
        for n in range(count):
            node = base + n
            compressed = solve_node(
                jnp.concatenate([current[2 * n], current[2 * n + 1]], axis=1),
                pieces(node, 0, 2 * rank),
                pieces(node, 2 * rank, rank),
                solved_ref.at[node],
            )
            following.append(compressed.astype(jnp.bfloat16))
        current = following
    out_ref[...] = current[0]


def group_up(per_dev, parts, packs):
    leaves, share, rank = parts[0].shape
    _, total = half_levels(per_dev)
    _, rows, width = packs[0].shape
    return pl.pallas_call(
        functools.partial(group_up_kernel, per_dev),
        out_shape=[
            jax.ShapeDtypeStruct((total, 2 * CORES, share, rows), jnp.float32),
            jax.ShapeDtypeStruct((share, rank), jnp.bfloat16),
        ],
        compiler_params=params(),
        cost_estimate=cost(24 * total * share * rows * rank, 8 * total * rows * width),
    )(*parts, *packs)


def order_pair(right, mine, other):
    return jnp.concatenate([jnp.where(right, other, mine), jnp.where(right, mine, other)], axis=1)


def half_up_kernel(mine_ref, other_ref, own_ref, near_ref, solved_ref, out_ref):
    rank = mine_ref.shape[1]
    place = lax.axis_index("rhs")
    stacked = order_pair(place // CORES == 1, mine_ref[...], other_ref[...])
    total = 0.0
    for flip, ref in enumerate((own_ref, near_ref)):
        solved = dot_rows(stacked, ref[0, :, : 2 * rank])
        solved_ref[(place ^ flip) % CORES] = solved
        total += jnp.dot(
            solved.astype(jnp.bfloat16),
            ref[0, :, 2 * rank : 3 * rank],
            preferred_element_type=jnp.float32,
        )
    out_ref[...] = total.astype(jnp.bfloat16)


def half_up(mine, other, own, near):
    share, rank = mine.shape
    nodes, rows, width = own.shape
    last = pl.BlockSpec((1, rows, width), lambda i: (nodes - 1, 0, 0))
    whole = pl.BlockSpec((share, rank), lambda i: (0, 0))
    return pl.pallas_call(
        half_up_kernel,
        grid=(1,),
        in_specs=[whole, whole, last, last],
        out_specs=[pl.BlockSpec((CORES, share, rows), lambda i: (0, 0, 0)), whole],
        out_shape=[
            jax.ShapeDtypeStruct((CORES, share, rows), jnp.float32),
            jax.ShapeDtypeStruct((share, rank), jnp.bfloat16),
        ],
        compiler_params=params(),
        cost_estimate=cost(12 * share * rows * rank, 4 * rows * width),
    )(mine, other, own, near)


def total_of(refs):
    if len(refs) == 1:
        return refs[0][...]
    return sum(ref[...].astype(jnp.float32) for ref in refs).astype(jnp.bfloat16)


def cross_pair(level, refs):
    half = len(refs) // 2
    is_right = (lax.axis_index("leaf") // (1 << level)) % 2 == 1
    return order_pair(is_right, total_of(refs[:half]), total_of(refs[half:]))


def cross_up_kernel(level, *refs):
    *refs, solved_ref, out_ref = refs
    inputs, packs = refs[: -2 * CORES], refs[-2 * CORES :]
    rank = out_ref.shape[1]
    compressed = solve_node(
        cross_pair(level, inputs),
        [ref[:, : 2 * rank] for ref in packs],
        [ref[:, 2 * rank : 3 * rank] for ref in packs],
        solved_ref,
    )
    out_ref[...] = compressed.astype(jnp.bfloat16)


def cross_up(level, inputs, packs):
    share, rank = inputs[0].shape[-2:]
    rows, width = packs[0].shape
    return pl.pallas_call(
        functools.partial(cross_up_kernel, level),
        out_shape=[
            jax.ShapeDtypeStruct((2 * CORES, share, rows), jnp.float32),
            jax.ShapeDtypeStruct((share, rank), jnp.bfloat16),
        ],
        compiler_params=params(),
        cost_estimate=cost(24 * share * rows * rank, 8 * rows * width),
    )(*inputs, *packs)


def down_kernel(per_dev, cross_levels, input_count, *refs):
    *refs, out_ref, value = refs
    inputs, refs = refs[:input_count], refs[input_count:]
    solved_cross, refs = refs[: cross_levels - 1], refs[cross_levels - 1 :]
    solved_top, solved_half, refs = refs[0], refs[1], refs[2:]
    count = 2 * CORES * (cross_levels - 1)
    cross_packs, (tail, near_tail, keep, keep_near) = refs[:count], refs[count:]
    levels, total = half_levels(per_dev)
    rank = out_ref.shape[2]
    node_size = 2 * rank
    place = lax.axis_index("rhs")

    def choose(which):
        return jnp.concatenate([value[2 * which], value[2 * which + 1]], axis=1)

    def side(level):
        return (lax.axis_index("leaf") // (1 << level)) % 2

    def columns(ref):
        width = ref.shape[-1]
        return pl.ds(width - rank, rank)

    stacked = cross_pair(cross_levels - 1, inputs)
    half = side(cross_levels - 1)
    for flip, ref in ((0, tail), (1, near_tail)):
        core = (place ^ flip) % CORES
        value[2 * half + core] = dot_rows(stacked, ref[:, :node_size]).astype(jnp.bfloat16)
    incoming = choose(half)
    for level in range(cross_levels - 2, -1, -1):
        packs = cross_packs[2 * CORES * level : 2 * CORES * (level + 1)]
        own, far, near, far_near = packs
        if level == 0:
            couplings = [ref[:, columns(ref)] for ref in packs]
        else:
            start = node_size + (total + level - 1) * rank
            couplings = [
                own[:, columns(own)],
                tail[:, start : start + rank],
                near[:, columns(near)],
                near_tail[:, start : start + rank],
            ]
        for flip, coupling in zip(PIECES, couplings):
            piece = place ^ flip
            solved = solved_cross[level][piece]
            value[piece] = (solved - dot_rows(incoming, coupling)).astype(jnp.bfloat16)
        incoming = choose(side(level))

    for flip, ref in ((0, keep), (1, keep_near)):
        piece = (place ^ flip) % CORES
        coupling = ref[total, :, columns(ref)]
        value[piece] = (solved_top[piece] - dot_rows(incoming, coupling)).astype(jnp.bfloat16)
    current = [choose(0)]
    for base, count, _ in reversed(levels):
        following = []
        for n in range(count):
            node = base + n
            start = node_size + node * rank
            couplings = (
                keep[node, :, columns(keep)],
                tail[:, start : start + rank],
                keep_near[node, :, columns(keep)],
                near_tail[:, start : start + rank],
            )
            for flip, coupling in zip(PIECES, couplings):
                piece = place ^ flip
                value[piece] = (
                    solved_half[node, piece] - dot_rows(current[n], coupling)
                ).astype(jnp.bfloat16)
            following += [choose(0), choose(1)]
        current = following
    for i, block in enumerate(current):
        out_ref[i] = block


def way_down(per_dev, inputs, solved_cross, solved_top, solved_half, cross_packs, others):
    share, rank = inputs[0].shape[-2:]
    rows = solved_half.shape[3]
    operands = [*inputs, *solved_cross, solved_top, solved_half]
    for packs in cross_packs:
        operands += packs
    operands += others
    return pl.pallas_call(
        functools.partial(down_kernel, per_dev, len(cross_packs) + 1, len(inputs)),
        out_shape=jax.ShapeDtypeStruct((per_dev // 2, share, rank), jnp.bfloat16),
        scratch_shapes=[pltpu.VMEM((2 * CORES, share, rows), jnp.bfloat16)],
        compiler_params=params(18),
        cost_estimate=cost(8 * share * rows * rank * per_dev, 4 * 1024 * 1024),
    )(*operands)


def finish_kernel(far_ref, own_ref, incoming_ref, coupling_ref, out_ref):
    half = own_ref.shape[0]
    high = lax.axis_index("rhs") // CORES
    for values_ref, side in ((far_ref, 1 - high), (own_ref, high)):
        for i in range(half):
            leaf = side * half + i
            incoming = jnp.concatenate(
                [incoming_ref[side * CORES + core, i] for core in range(CORES)], axis=0
            )
            out_ref[leaf] = values_ref[i] - dot_rows(incoming, coupling_ref[leaf])


def finish(far, own, incoming, coupling):
    half, targets, rows = own.shape
    return pl.pallas_call(
        finish_kernel,
        out_shape=jax.ShapeDtypeStruct((2 * half, targets, rows), jnp.float32),
        compiler_params=params(),
        cost_estimate=cost(4 * half * targets * rows * coupling.shape[2], 16 * own.size),
    )(far, own, incoming, coupling)


def swap(block, axis, bit):
    return lax.ppermute(block, axis, [(i, i ^ bit) for i in range(lax.axis_size(axis))])


def far_swap(block, leaf_bit, rhs_bit):
    shares = lax.axis_size("rhs")
    flip = leaf_bit * shares + rhs_bit
    count = lax.axis_size("leaf") * shares
    return lax.ppermute(block, ("leaf", "rhs"), [(i, i ^ flip) for i in range(count)])


def after(value, anchor):
    return lax.optimization_barrier((value, anchor))[0]


def body(
    right_side,
    point_order,
    leaf_inverse,
    leaf_basis,
    leaf_coupling,
    node_inverse,
    node_basis,
    node_coupling,
):
    devices = lax.axis_size("leaf")
    per_dev = leaf_inverse.shape[0]
    node_size = node_inverse.shape[2]
    rank = leaf_basis.shape[2]
    cross_levels = devices.bit_length() - 1
    place = lax.axis_index("rhs")
    high, low = place // CORES, place % CORES

    def rise(carrier, level, anchor):
        other = after(swap(carrier, "leaf", 1 << level), anchor)
        width = node_size if level == cross_levels - 2 else carrier.shape[1]
        ancestor, *carriers = climb(level, carrier, other, [width] * (level < cross_levels - 1))
        return ancestor, carriers[0] if carriers else None

    send, send_coupling, keep, carrier = pack(node_inverse, node_basis, node_coupling)
    across, beside = after(
        [swap(right_side, "rhs", CORES), swap(right_side, "rhs", 1)], send
    )
    points = [across, beside, swap(after(across, beside), "rhs", 1)]
    half_far = swap(send, "rhs", CORES)
    keep_near = swap(after(keep, points), "rhs", 1)
    carrier = after(carrier, points)
    points = [right_side, *points]

    leaves = (point_order, leaf_inverse, leaf_basis)
    far_values, far_same, far_cross, joined = leaf_up(
        jnp.stack([1 - high, low]), points, *leaves
    )
    keep_near = after(keep_near, far_same)
    own_values, own_same, own_cross = leaf_up(
        jnp.stack([high, low]), [after(joined, keep_near)], *leaves
    )
    ancestor, carrier = rise(carrier, 0, own_same)
    ancestors = [ancestor]
    far_same = after(swap(far_same, "rhs", CORES), own_same)
    far_cross = after(swap(far_cross, "rhs", CORES + 1), own_same)
    parts = [own_same, far_same, swap(own_cross, "rhs", 1), far_cross]
    half_far = after(half_far, (parts, carrier))
    half_near = swap(half_far, "rhs", 1)
    fars = [swap(after(ancestors[0], half_far), "rhs", CORES)]
    nears = [swap(after(ancestors[0], half_far), "rhs", 1)]

    solved_half, current = group_up(per_dev, parts, [keep, half_far, keep_near, half_near])
    other = swap(after(current, nears[0]), "rhs", CORES)
    ancestor, carrier = rise(carrier, 1, other)
    ancestors.append(ancestor)
    solved_top, current = half_up(current, other, keep, keep_near)
    fars[0] = after(fars[0], other)
    near_far = swap(fars[0], "rhs", 1)
    cross_packs = [[ancestors[0], fars[0], nears[0], near_far]]
    factors = [(0, node_size + rank)]
    fars.append(swap(join([ancestors[1]], current, factors), "rhs", CORES))
    current = after(current, near_far)
    inputs = [
        current,
        swap(current, "rhs", CORES),
        swap(current, "leaf", 1),
        far_swap(current, 1, CORES),
    ]

    solved_cross = []
    for level in range(cross_levels - 1):
        if level > 0:
            own, far = ancestors[level], fars[level]
            own_near = swap(join([own], current), "rhs", 1)
            far_near = swap(join([far], current), "rhs", 1)
            cross_packs.append([own, far, own_near, far_near])
        solved, current = cross_up(level, inputs, cross_packs[level])
        solved_cross.append(solved)
        inputs = [current, swap(current, "leaf", 2 << level)]
        if level == 0:
            for later in range(2, cross_levels):
                ancestor, carrier = rise(carrier, later, current)
                ancestors.append(ancestor)
            for later in range(2, cross_levels - 1):
                fars.append(swap(join([ancestors[later]], current, factors), "rhs", CORES))
            blocks = [ancestors[-1], send_coupling, *ancestors[1:-1]]
            cuts = [(0, node_size), (0, send_coupling.shape[1])]
            cuts += [(node_size + rank, rank)] * (cross_levels - 2)
            tail = swap(join(blocks, current, cuts), "rhs", CORES)

    tail = hop(cross_levels - 1, ancestors[-1], tail, inputs[1])
    others = [tail, swap(tail, "rhs", 1), keep, keep_near]
    shares = way_down(per_dev, inputs, solved_cross, solved_top, solved_half, cross_packs, others)
    incoming = lax.all_gather(shares, "rhs", axis=0)
    return finish(far_values, own_values, incoming, leaf_coupling)


def solution(mesh):
    placed = (P(None, ("leaf", "rhs")), P("leaf")) + (P("leaf", "rhs", None),) * 6
    return jax.shard_map(
        body, mesh=mesh, in_specs=placed, out_specs=P("leaf", None, "rhs"), check_vma=False
    )
```

```python
import functools

import jax
import jax.numpy as jnp
from jax import lax
from jax.experimental import pallas as pl
from jax.experimental.pallas import tpu as pltpu
from jax.sharding import PartitionSpec as P

LANES = 256
PIECES = (0, 2, 1, 3)
CORES = 2


def params(mebibytes=12):
    return pltpu.CompilerParams(vmem_limit_bytes=mebibytes * 1024 * 1024)


def cost(flops, moved):
    return pl.CostEstimate(flops=flops // 1000, bytes_accessed=moved // 1000, transcendentals=0)


def dot_rows(left, right):
    return lax.dot_general(
        left, right, (((1,), (1,)), ((), ())), preferred_element_type=jnp.float32
    )


def half_levels(per_dev):
    levels = []
    base = 0
    for height in range(1, per_dev.bit_length() - 1):
        node_count = per_dev >> height
        levels.append((base, node_count // 2, per_dev - 2 * node_count))
        base += node_count // 2
    return levels, base


def pack_kernel(per_dev, inverse, basis, coupling, *refs):
    targets, buffers, (sems, out_sems) = refs[:4], refs[4:8], refs[8:]
    factors, couplings, keep, cross = buffers
    levels, total = half_levels(per_dev)
    high = lax.axis_index("rhs") // CORES
    node_size = inverse.shape[2]
    rank = basis.shape[2]
    parts = (
        (inverse, 0, node_size),
        (basis, node_size, rank),
        (coupling, node_size + rank, rank),
    )
    copies = []
    for source, start, width in parts:
        columns = pl.ds(start, width)
        for base, count, offset in levels:
            mine = source.at[pl.ds(offset + high * count, count)]
            other = source.at[pl.ds(offset + (1 - high) * count, count)]
            if source is coupling:
                for n in range(count):
                    sent = couplings.at[:, pl.ds((base + n) * rank, rank)]
                    copies.append((other.at[n], sent))
            else:
                copies.append((other, factors.at[pl.ds(base, count), :, columns]))
            copies.append((mine, keep.at[pl.ds(base, count), :, columns]))
        copies.append((source.at[per_dev - 2], keep.at[total, :, columns]))
        copies.append((source.at[per_dev - 1], cross.at[:, columns]))
    started = []
    for i, (source, target) in enumerate(copies):
        copy = pltpu.make_async_copy(source, target, sems.at[i])
        copy.start()
        started.append(copy)
    for copy in started:
        copy.wait()
    started = []
    for i, (buffer, target) in enumerate(zip(buffers, targets)):
        copy = pltpu.make_async_copy(buffer, target, out_sems.at[i])
        copy.start()
        started.append(copy)
    for copy in started:
        copy.wait()


def pack(inverse, basis, coupling):
    per_dev, rows, node_size = inverse.shape
    rank = basis.shape[2]
    width = node_size + 2 * rank
    levels, total = half_levels(per_dev)
    shapes = [
        (total, rows, node_size + rank),
        (rows, total * rank),
        (total + 1, rows, width),
        (rows, width),
    ]
    return pl.pallas_call(
        functools.partial(pack_kernel, per_dev),
        in_specs=[pl.BlockSpec(memory_space=pl.ANY)] * 3,
        out_specs=[pl.BlockSpec(memory_space=pl.ANY)] * 4,
        out_shape=[jax.ShapeDtypeStruct(shape, inverse.dtype) for shape in shapes],
        scratch_shapes=[pltpu.VMEM(shape, inverse.dtype) for shape in shapes]
        + [pltpu.SemaphoreType.DMA((6 + 5 * len(levels) + total,)), pltpu.SemaphoreType.DMA((4,))],
        compiler_params=params(63),
        cost_estimate=cost(0, 4 * per_dev * rows * width),
    )(inverse, basis, coupling)


def climb_kernel(level, mine_ref, other_ref, ancestor_ref, *carrier_refs):
    right = (lax.axis_index("leaf") // (1 << level)) % 2 == 1

    @pl.when(right)
    def _():
        ancestor_ref[...] = mine_ref[...]
        for ref in carrier_refs:
            ref[...] = other_ref[:, : ref.shape[1]]

    @pl.when(jnp.logical_not(right))
    def _():
        ancestor_ref[...] = other_ref[...]
        for ref in carrier_refs:
            ref[...] = mine_ref[:, : ref.shape[1]]


def climb(level, mine, other, keep):
    return pl.pallas_call(
        functools.partial(climb_kernel, level),
        out_shape=[pltpu.VMEM(mine.shape, mine.dtype)]
        + [pltpu.VMEM((mine.shape[0], size), mine.dtype) for size in keep],
        compiler_params=params(),
        cost_estimate=cost(0, 4 * mine.size),
    )(mine, other)


def join_kernel(cuts, *refs):
    *blocks, _, out_ref = refs
    start = 0
    for ref, (first, width) in zip(blocks, cuts):
        out_ref[:, start : start + width] = ref[:, first : first + width]
        start += width


def join(blocks, anchor, cuts=None):
    rows = blocks[0].shape[0]
    cuts = cuts or [(0, block.shape[1]) for block in blocks]
    width = sum(size for _, size in cuts)
    return pl.pallas_call(
        functools.partial(join_kernel, cuts),
        out_shape=pltpu.VMEM((rows, width), blocks[0].dtype),
        compiler_params=params(),
        cost_estimate=cost(0, 4 * rows * width),
    )(*blocks, anchor)


def hop_kernel(level, top_ref, tail_ref, _, out_ref):
    node_size = top_ref.shape[1]
    side = (lax.axis_index("leaf") // (1 << level)) % 2
    here = lax.axis_index("rhs") // CORES == side
    out_ref[:, node_size:] = tail_ref[:, node_size:]

    @pl.when(here)
    def _():
        out_ref[:, :node_size] = top_ref[...]

    @pl.when(jnp.logical_not(here))
    def _():
        out_ref[:, :node_size] = tail_ref[:, :node_size]


def hop(level, top, tail, anchor):
    return pl.pallas_call(
        functools.partial(hop_kernel, level),
        out_shape=pltpu.VMEM(tail.shape, tail.dtype),
        compiler_params=params(),
        cost_estimate=cost(0, 4 * tail.size),
    )(top, tail, anchor)


def leaf_kernel(count, side_ref, *refs):
    points, refs = refs[:count], refs[count:]
    order_ref, inverse_ref, basis_ref, values_ref, same_ref, cross_ref, *rest = refs
    targets = values_ref.shape[1]
    stacked = rest[0] if rest else points[0]
    chunks, pieces = stacked.shape[:2]

    if rest:

        @pl.when(pl.program_id(0) == 0)
        def _():
            place = lax.axis_index("rhs")
            for flip, points_ref in zip(PIECES, points):
                for w in range(pieces):
                    stacked[place ^ flip, w] = points_ref[:, w * LANES : (w + 1) * LANES]

    order = order_ref[...]
    high = order // LANES
    low = order % LANES
    rows = lax.broadcasted_iota(jnp.int32, (LANES, order.shape[1]), 0)
    pick = jnp.where(rows == low, 1.0, 0.0).astype(jnp.bfloat16)
    spread = jnp.dot(
        stacked[...].reshape(-1, LANES), pick, preferred_element_type=jnp.float32
    )
    ordered = jnp.zeros((targets, order.shape[1]), jnp.float32)
    for k in range(chunks * pieces):
        ordered = jnp.where(high == k, spread[k * targets : (k + 1) * targets, :], ordered)
    values = dot_rows(ordered.astype(jnp.bfloat16), inverse_ref[0])
    values_ref[0] = values
    partial = jnp.dot(
        values.astype(jnp.bfloat16), basis_ref[0], preferred_element_type=jnp.float32
    ).astype(jnp.bfloat16)
    share = targets // CORES
    for core in range(CORES):

        @pl.when(side_ref[1] == core)
        def _():
            same_ref[0] = partial[core * share : (core + 1) * share]
            cross_ref[0] = partial[(1 - core) * share : (2 - core) * share]


def leaf_up(side, points, point_order, leaf_inverse, leaf_basis):
    leaves, rows, leaf_size = leaf_inverse.shape
    rank = leaf_basis.shape[2]
    half = leaves // 2
    joined = points[0].ndim == 4
    if joined:
        shape = points[0].shape
    else:
        targets, width = points[0].shape
        shape = (len(points), width // LANES, targets, LANES)
    targets = shape[2]
    share = targets // CORES
    sent = jax.ShapeDtypeStruct((half, share, rank), jnp.bfloat16)
    out_specs = [
        pl.BlockSpec((1, targets, rows), lambda i, side: (i, 0, 0)),
        pl.BlockSpec((1, share, rank), lambda i, side: (i, 0, 0)),
        pl.BlockSpec((1, share, rank), lambda i, side: (i, 0, 0)),
    ]
    out_shape = [jax.ShapeDtypeStruct((half, targets, rows), jnp.float32), sent, sent]
    if not joined:
        out_specs.append(pl.BlockSpec(shape, lambda i, side: (0, 0, 0, 0)))
        out_shape.append(pltpu.VMEM(shape, jnp.bfloat16))
    point_specs = [
        pl.BlockSpec(block.shape, lambda i, side, rank=block.ndim: (0,) * rank) for block in points
    ]
    return pl.pallas_call(
        functools.partial(leaf_kernel, len(points)),
        grid_spec=pltpu.PrefetchScalarGridSpec(
            num_scalar_prefetch=1,
            grid=(half,),
            in_specs=[
                *point_specs,
                pl.BlockSpec((1, leaf_size), lambda i, side: (0, side[0] * half + i)),
                pl.BlockSpec((1, rows, leaf_size), lambda i, side: (side[0] * half + i, 0, 0)),
                pl.BlockSpec((1, rows, rank), lambda i, side: (side[0] * half + i, 0, 0)),
            ],
            out_specs=out_specs,
        ),
        out_shape=out_shape,
        compiler_params=params(),
        cost_estimate=cost(
            leaves * targets * leaf_size * (shape[0] * shape[1] * LANES + 2 * rows),
            leaves * rows * (leaf_size + rank + 3 * targets),
        ),
    )(side, *points, point_order.reshape(1, -1), leaf_inverse, leaf_basis)


def solve_node(stacked, inverses, bases, solved_ref):
    mine = lax.axis_index("rhs")
    total = None
    for flip, inverse, basis in zip(PIECES, inverses, bases):
        solved = dot_rows(stacked, inverse)
        solved_ref[mine ^ flip] = solved
        term = jnp.dot(solved.astype(jnp.bfloat16), basis, preferred_element_type=jnp.float32)
        total = term if total is None else total + term
    return total


def group_up_kernel(per_dev, *refs):
    *refs, solved_ref, out_ref = refs
    parts, packs = refs[: 2 * CORES], refs[2 * CORES :]
    levels, _ = half_levels(per_dev)
    rank = parts[0].shape[2]

    def pieces(node, start, width):
        return [ref[node, :, pl.ds(start, width)] for ref in packs]

    sums = sum(ref[...].astype(jnp.float32) for ref in parts).astype(jnp.bfloat16)
    current = [sums[i] for i in range(sums.shape[0])]
    for base, count, _ in levels:
        following = []
        for n in range(count):
            node = base + n
            compressed = solve_node(
                jnp.concatenate([current[2 * n], current[2 * n + 1]], axis=1),
                pieces(node, 0, 2 * rank),
                pieces(node, 2 * rank, rank),
                solved_ref.at[node],
            )
            following.append(compressed.astype(jnp.bfloat16))
        current = following
    out_ref[...] = current[0]


def group_up(per_dev, parts, packs):
    leaves, share, rank = parts[0].shape
    _, total = half_levels(per_dev)
    _, rows, width = packs[0].shape
    return pl.pallas_call(
        functools.partial(group_up_kernel, per_dev),
        out_shape=[
            jax.ShapeDtypeStruct((total, 2 * CORES, share, rows), jnp.float32),
            jax.ShapeDtypeStruct((share, rank), jnp.bfloat16),
        ],
        compiler_params=params(),
        cost_estimate=cost(24 * total * share * rows * rank, 8 * total * rows * width),
    )(*parts, *packs)


def order_pair(right, mine, other):
    return jnp.concatenate([jnp.where(right, other, mine), jnp.where(right, mine, other)], axis=1)


def half_up_kernel(mine_ref, other_ref, own_ref, near_ref, solved_ref, out_ref):
    rank = mine_ref.shape[1]
    place = lax.axis_index("rhs")
    stacked = order_pair(place // CORES == 1, mine_ref[...], other_ref[...])
    total = 0.0
    for flip, ref in enumerate((own_ref, near_ref)):
        solved = dot_rows(stacked, ref[0, :, : 2 * rank])
        solved_ref[(place ^ flip) % CORES] = solved
        total += jnp.dot(
            solved.astype(jnp.bfloat16),
            ref[0, :, 2 * rank : 3 * rank],
            preferred_element_type=jnp.float32,
        )
    out_ref[...] = total.astype(jnp.bfloat16)


def half_up(mine, other, own, near):
    share, rank = mine.shape
    nodes, rows, width = own.shape
    last = pl.BlockSpec((1, rows, width), lambda i: (nodes - 1, 0, 0))
    whole = pl.BlockSpec((share, rank), lambda i: (0, 0))
    return pl.pallas_call(
        half_up_kernel,
        grid=(1,),
        in_specs=[whole, whole, last, last],
        out_specs=[pl.BlockSpec((CORES, share, rows), lambda i: (0, 0, 0)), whole],
        out_shape=[
            jax.ShapeDtypeStruct((CORES, share, rows), jnp.float32),
            jax.ShapeDtypeStruct((share, rank), jnp.bfloat16),
        ],
        compiler_params=params(),
        cost_estimate=cost(12 * share * rows * rank, 4 * rows * width),
    )(mine, other, own, near)


def total_of(refs):
    if len(refs) == 1:
        return refs[0][...]
    return sum(ref[...].astype(jnp.float32) for ref in refs).astype(jnp.bfloat16)


def cross_pair(level, refs):
    half = len(refs) // 2
    is_right = (lax.axis_index("leaf") // (1 << level)) % 2 == 1
    return order_pair(is_right, total_of(refs[:half]), total_of(refs[half:]))


def cross_up_kernel(level, *refs):
    *refs, solved_ref, out_ref = refs
    inputs, packs = refs[: -2 * CORES], refs[-2 * CORES :]
    rank = out_ref.shape[1]
    compressed = solve_node(
        cross_pair(level, inputs),
        [ref[:, : 2 * rank] for ref in packs],
        [ref[:, 2 * rank : 3 * rank] for ref in packs],
        solved_ref,
    )
    out_ref[...] = compressed.astype(jnp.bfloat16)


def cross_up(level, inputs, packs):
    share, rank = inputs[0].shape[-2:]
    rows, width = packs[0].shape
    return pl.pallas_call(
        functools.partial(cross_up_kernel, level),
        out_shape=[
            jax.ShapeDtypeStruct((2 * CORES, share, rows), jnp.float32),
            jax.ShapeDtypeStruct((share, rank), jnp.bfloat16),
        ],
        compiler_params=params(),
        cost_estimate=cost(24 * share * rows * rank, 8 * rows * width),
    )(*inputs, *packs)


def down_kernel(per_dev, cross_levels, input_count, *refs):
    *refs, out_ref, value = refs
    inputs, refs = refs[:input_count], refs[input_count:]
    solved_cross, refs = refs[: cross_levels - 1], refs[cross_levels - 1 :]
    solved_top, solved_half, refs = refs[0], refs[1], refs[2:]
    count = 2 * CORES * (cross_levels - 1)
    cross_packs, others = refs[:count], refs[count:]
    tail, near_tail, half_tail, near_half_tail, keep, keep_near = others
    levels, total = half_levels(per_dev)
    rank = out_ref.shape[2]
    node_size = 2 * rank
    place = lax.axis_index("rhs")

    def choose(which):
        return jnp.concatenate([value[2 * which], value[2 * which + 1]], axis=1)

    def side(level):
        return (lax.axis_index("leaf") // (1 << level)) % 2

    def columns(ref):
        width = ref.shape[-1]
        return pl.ds(width - rank, rank)

    stacked = cross_pair(cross_levels - 1, inputs)
    half = side(cross_levels - 1)
    for flip, ref in ((0, tail), (1, near_tail)):
        core = (place ^ flip) % CORES
        value[2 * half + core] = dot_rows(stacked, ref[:, :node_size]).astype(jnp.bfloat16)
    incoming = choose(half)
    for level in range(cross_levels - 2, -1, -1):
        packs = cross_packs[2 * CORES * level : 2 * CORES * (level + 1)]
        own, _, near, _ = packs
        start = node_size + level * rank
        couplings = [
            own[:, columns(own)],
            tail[:, start : start + rank],
            near[:, columns(near)],
            near_tail[:, start : start + rank],
        ]
        for flip, coupling in zip(PIECES, couplings):
            piece = place ^ flip
            solved = solved_cross[level][piece]
            value[piece] = (solved - dot_rows(incoming, coupling)).astype(jnp.bfloat16)
        incoming = choose(side(level))

    for flip, ref in ((0, keep), (1, keep_near)):
        piece = (place ^ flip) % CORES
        coupling = ref[total, :, columns(ref)]
        value[piece] = (solved_top[piece] - dot_rows(incoming, coupling)).astype(jnp.bfloat16)
    current = [choose(0)]
    for base, count, _ in reversed(levels):
        following = []
        for n in range(count):
            node = base + n
            start = node * rank
            couplings = (
                keep[node, :, columns(keep)],
                half_tail[:, start : start + rank],
                keep_near[node, :, columns(keep)],
                near_half_tail[:, start : start + rank],
            )
            for flip, coupling in zip(PIECES, couplings):
                piece = place ^ flip
                value[piece] = (
                    solved_half[node, piece] - dot_rows(current[n], coupling)
                ).astype(jnp.bfloat16)
            following += [choose(0), choose(1)]
        current = following
    for i, block in enumerate(current):
        out_ref[i] = block


def way_down(per_dev, inputs, solved_cross, solved_top, solved_half, cross_packs, others):
    share, rank = inputs[0].shape[-2:]
    rows = solved_half.shape[3]
    operands = [*inputs, *solved_cross, solved_top, solved_half]
    for packs in cross_packs:
        operands += packs
    operands += others
    return pl.pallas_call(
        functools.partial(down_kernel, per_dev, len(cross_packs) + 1, len(inputs)),
        out_shape=jax.ShapeDtypeStruct((per_dev // 2, share, rank), jnp.bfloat16),
        scratch_shapes=[pltpu.VMEM((2 * CORES, share, rows), jnp.bfloat16)],
        compiler_params=params(18),
        cost_estimate=cost(8 * share * rows * rank * per_dev, 4 * 1024 * 1024),
    )(*operands)


def finish_kernel(far_ref, own_ref, incoming_ref, coupling_ref, out_ref):
    half = own_ref.shape[0]
    high = lax.axis_index("rhs") // CORES
    for values_ref, side in ((far_ref, 1 - high), (own_ref, high)):
        for i in range(half):
            leaf = side * half + i
            incoming = jnp.concatenate(
                [incoming_ref[side * CORES + core, i] for core in range(CORES)], axis=0
            )
            out_ref[leaf] = values_ref[i] - dot_rows(incoming, coupling_ref[leaf])


def finish(far, own, incoming, coupling):
    half, targets, rows = own.shape
    return pl.pallas_call(
        finish_kernel,
        out_shape=jax.ShapeDtypeStruct((2 * half, targets, rows), jnp.float32),
        compiler_params=params(),
        cost_estimate=cost(4 * half * targets * rows * coupling.shape[2], 16 * own.size),
    )(far, own, incoming, coupling)


def swap(block, axis, bit):
    return lax.ppermute(block, axis, [(i, i ^ bit) for i in range(lax.axis_size(axis))])


def far_swap(block, leaf_bit, rhs_bit):
    shares = lax.axis_size("rhs")
    flip = leaf_bit * shares + rhs_bit
    count = lax.axis_size("leaf") * shares
    return lax.ppermute(block, ("leaf", "rhs"), [(i, i ^ flip) for i in range(count)])


def after(value, anchor):
    return lax.optimization_barrier((value, anchor))[0]


def body(
    right_side,
    point_order,
    leaf_inverse,
    leaf_basis,
    leaf_coupling,
    node_inverse,
    node_basis,
    node_coupling,
):
    devices = lax.axis_size("leaf")
    per_dev = leaf_inverse.shape[0]
    node_size = node_inverse.shape[2]
    rank = leaf_basis.shape[2]
    cross_levels = devices.bit_length() - 1
    place = lax.axis_index("rhs")
    high, low = place // CORES, place % CORES

    def rise(carrier, level, anchor):
        other = after(swap(carrier, "leaf", 1 << level), anchor)
        width = node_size if level == cross_levels - 2 else carrier.shape[1]
        ancestor, *carriers = climb(level, carrier, other, [width] * (level < cross_levels - 1))
        return ancestor, carriers[0] if carriers else None

    send, send_coupling, keep, carrier = pack(node_inverse, node_basis, node_coupling)
    across, beside = after(
        [swap(right_side, "rhs", CORES), swap(right_side, "rhs", 1)], send
    )
    points = [across, beside, swap(after(across, beside), "rhs", 1)]
    half_far = swap(send, "rhs", CORES)
    keep_near = swap(after(keep, points), "rhs", 1)
    carrier = after(carrier, points)
    points = [right_side, *points]

    leaves = (point_order, leaf_inverse, leaf_basis)
    far_values, far_same, far_cross, joined = leaf_up(
        jnp.stack([1 - high, low]), points, *leaves
    )
    keep_near = after(keep_near, far_same)
    own_values, own_same, own_cross = leaf_up(
        jnp.stack([high, low]), [after(joined, keep_near)], *leaves
    )
    ancestor, carrier = rise(carrier, 0, own_same)
    ancestors = [ancestor]
    far_same = after(swap(far_same, "rhs", CORES), own_same)
    far_cross = after(swap(far_cross, "rhs", CORES + 1), own_same)
    parts = [own_same, far_same, swap(own_cross, "rhs", 1), far_cross]
    half_far = after(half_far, (parts, carrier))
    half_near = swap(half_far, "rhs", 1)
    factors = [(0, node_size + rank)]
    fars = [swap(join([ancestors[0]], half_far, factors), "rhs", CORES)]

    solved_half, current = group_up(per_dev, parts, [keep, half_far, keep_near, half_near])
    own_near = swap(join([ancestors[0]], current), "rhs", 1)
    other = swap(current, "rhs", CORES)
    half_tail = swap(join([send_coupling], other), "rhs", CORES)
    ancestor, carrier = rise(carrier, 1, other)
    ancestors.append(ancestor)
    solved_top, current = half_up(current, after(other, own_near), keep, keep_near)
    fars[0] = after(fars[0], other)
    near_far = swap(fars[0], "rhs", 1)
    cross_packs = [[ancestors[0], fars[0], own_near, near_far]]
    fars.append(swap(join([ancestors[1]], current, factors), "rhs", CORES))
    current = after(current, near_far)
    inputs = [
        current,
        swap(current, "rhs", CORES),
        swap(current, "leaf", 1),
        far_swap(current, 1, CORES),
    ]
    inputs = after(inputs, half_tail)

    solved_cross = []
    for level in range(cross_levels - 1):
        if level > 0:
            own, far = ancestors[level], fars[level]
            own_near = swap(join([own], current), "rhs", 1)
            far_near = swap(join([far], current), "rhs", 1)
            cross_packs.append([own, far, own_near, far_near])
        solved, current = cross_up(level, inputs, cross_packs[level])
        solved_cross.append(solved)
        inputs = [current, swap(current, "leaf", 2 << level)]
        if level == 0:
            for later in range(2, cross_levels):
                ancestor, carrier = rise(carrier, later, current)
                ancestors.append(ancestor)
            for later in range(2, cross_levels - 1):
                fars.append(swap(join([ancestors[later]], current, factors), "rhs", CORES))
            near_half_tail = swap(join([half_tail], current), "rhs", 1)
            cuts = [(0, node_size)] + [(node_size + rank, rank)] * (cross_levels - 1)
            tail = swap(join([ancestors[-1], *ancestors[:-1]], current, cuts), "rhs", CORES)

    tail = hop(cross_levels - 1, ancestors[-1], tail, inputs[1])
    others = [tail, swap(tail, "rhs", 1), half_tail, near_half_tail, keep, keep_near]
    shares = way_down(per_dev, inputs, solved_cross, solved_top, solved_half, cross_packs, others)
    incoming = lax.all_gather(shares, "rhs", axis=0)
    return finish(far_values, own_values, incoming, leaf_coupling)


def solution(mesh):
    placed = (P(None, ("leaf", "rhs")), P("leaf")) + (P("leaf", "rhs", None),) * 6
    return jax.shard_map(
        body, mesh=mesh, in_specs=placed, out_specs=P("leaf", None, "rhs"), check_vma=False
    )
```

```python
import functools

import jax
import jax.numpy as jnp
from jax import lax
from jax.experimental import pallas as pl
from jax.experimental.pallas import tpu as pltpu
from jax.sharding import PartitionSpec as P

LANES = 256
PIECES = (0, 2, 1, 3)
CORES = 2


def params(mebibytes=12):
    return pltpu.CompilerParams(vmem_limit_bytes=mebibytes * 1024 * 1024)


def cost(flops, moved):
    return pl.CostEstimate(flops=flops // 1000, bytes_accessed=moved // 1000, transcendentals=0)


def dot_rows(left, right):
    return lax.dot_general(
        left, right, (((1,), (1,)), ((), ())), preferred_element_type=jnp.float32
    )


def half_levels(per_dev):
    levels = []
    base = 0
    for height in range(1, per_dev.bit_length() - 1):
        node_count = per_dev >> height
        levels.append((base, node_count // 2, per_dev - 2 * node_count))
        base += node_count // 2
    return levels, base


def pack_kernel(per_dev, inverse, basis, coupling, *refs):
    targets, buffers, (sems, out_sems) = refs[:4], refs[4:8], refs[8:]
    factors, couplings, keep, cross = buffers
    levels, total = half_levels(per_dev)
    high = lax.axis_index("rhs") // CORES
    node_size = inverse.shape[2]
    rank = basis.shape[2]
    parts = (
        (inverse, 0, node_size),
        (basis, node_size, rank),
        (coupling, node_size + rank, rank),
    )
    copies = []
    for source, start, width in parts:
        columns = pl.ds(start, width)
        for base, count, offset in levels:
            mine = source.at[pl.ds(offset + high * count, count)]
            other = source.at[pl.ds(offset + (1 - high) * count, count)]
            if source is coupling:
                for n in range(count):
                    sent = couplings.at[:, pl.ds((base + n) * rank, rank)]
                    copies.append((other.at[n], sent))
            else:
                copies.append((other, factors.at[pl.ds(base, count), :, columns]))
            copies.append((mine, keep.at[pl.ds(base, count), :, columns]))
        copies.append((source.at[per_dev - 2], keep.at[total, :, columns]))
        copies.append((source.at[per_dev - 1], cross.at[:, columns]))
    started = []
    for i, (source, target) in enumerate(copies):
        copy = pltpu.make_async_copy(source, target, sems.at[i])
        copy.start()
        started.append(copy)
    for copy in started:
        copy.wait()
    started = []
    for i, (buffer, target) in enumerate(zip(buffers, targets)):
        copy = pltpu.make_async_copy(buffer, target, out_sems.at[i])
        copy.start()
        started.append(copy)
    for copy in started:
        copy.wait()


def pack(inverse, basis, coupling):
    per_dev, rows, node_size = inverse.shape
    rank = basis.shape[2]
    width = node_size + 2 * rank
    levels, total = half_levels(per_dev)
    shapes = [
        (total, rows, node_size + rank),
        (rows, total * rank),
        (total + 1, rows, width),
        (rows, width),
    ]
    return pl.pallas_call(
        functools.partial(pack_kernel, per_dev),
        in_specs=[pl.BlockSpec(memory_space=pl.ANY)] * 3,
        out_specs=[pl.BlockSpec(memory_space=pl.ANY)] * 4,
        out_shape=[jax.ShapeDtypeStruct(shape, inverse.dtype) for shape in shapes],
        scratch_shapes=[pltpu.VMEM(shape, inverse.dtype) for shape in shapes]
        + [pltpu.SemaphoreType.DMA((6 + 5 * len(levels) + total,)), pltpu.SemaphoreType.DMA((4,))],
        compiler_params=params(63),
        cost_estimate=cost(0, 4 * per_dev * rows * width),
    )(inverse, basis, coupling)


def climb_kernel(level, count, mine_ref, other_ref, *refs):
    extras, (ancestor_ref, *outs) = refs[:count], refs[count:]
    carrier_refs, passed = outs[: len(outs) - count], outs[len(outs) - count :]
    for ref, extra in zip(passed, extras):
        ref[...] = extra[...]
    right = (lax.axis_index("leaf") // (1 << level)) % 2 == 1

    @pl.when(right)
    def _():
        ancestor_ref[...] = mine_ref[...]
        for ref in carrier_refs:
            ref[...] = other_ref[:, : ref.shape[1]]

    @pl.when(jnp.logical_not(right))
    def _():
        ancestor_ref[...] = other_ref[...]
        for ref in carrier_refs:
            ref[...] = mine_ref[:, : ref.shape[1]]


def climb(level, mine, other, keep, extras=()):
    return pl.pallas_call(
        functools.partial(climb_kernel, level, len(extras)),
        out_shape=[pltpu.VMEM(mine.shape, mine.dtype)]
        + [pltpu.VMEM((mine.shape[0], size), mine.dtype) for size in keep]
        + [pltpu.VMEM(extra.shape, extra.dtype) for extra in extras],
        compiler_params=params(),
        cost_estimate=cost(0, 4 * mine.size),
    )(mine, other, *extras)


def join_kernel(cuts, *refs):
    *blocks, _, out_ref = refs
    start = 0
    for ref, (first, width) in zip(blocks, cuts):
        out_ref[:, start : start + width] = ref[:, first : first + width]
        start += width


def join(blocks, anchor, cuts=None):
    rows = blocks[0].shape[0]
    cuts = cuts or [(0, block.shape[1]) for block in blocks]
    width = sum(size for _, size in cuts)
    return pl.pallas_call(
        functools.partial(join_kernel, cuts),
        out_shape=pltpu.VMEM((rows, width), blocks[0].dtype),
        compiler_params=params(),
        cost_estimate=cost(0, 4 * rows * width),
    )(*blocks, anchor)


def hop_kernel(level, top_ref, tail_ref, _, out_ref):
    node_size = top_ref.shape[1]
    side = (lax.axis_index("leaf") // (1 << level)) % 2
    here = lax.axis_index("rhs") // CORES == side
    out_ref[:, node_size:] = tail_ref[:, node_size:]

    @pl.when(here)
    def _():
        out_ref[:, :node_size] = top_ref[...]

    @pl.when(jnp.logical_not(here))
    def _():
        out_ref[:, :node_size] = tail_ref[:, :node_size]


def hop(level, top, tail, anchor):
    return pl.pallas_call(
        functools.partial(hop_kernel, level),
        out_shape=pltpu.VMEM(tail.shape, tail.dtype),
        compiler_params=params(),
        cost_estimate=cost(0, 4 * tail.size),
    )(top, tail, anchor)


def leaf_kernel(count, side_ref, *refs):
    points, refs = refs[:count], refs[count:]
    order_ref, inverse_ref, basis_ref, values_ref, same_ref, cross_ref, *rest = refs
    targets = values_ref.shape[1]
    stacked = rest[0] if rest else points[0]
    chunks, pieces = stacked.shape[:2]

    if rest:

        @pl.when(pl.program_id(0) == 0)
        def _():
            place = lax.axis_index("rhs")
            for flip, points_ref in zip(PIECES, points):
                for w in range(pieces):
                    stacked[place ^ flip, w] = points_ref[:, w * LANES : (w + 1) * LANES]

    order = order_ref[...]
    high = order // LANES
    low = order % LANES
    rows = lax.broadcasted_iota(jnp.int32, (LANES, order.shape[1]), 0)
    pick = jnp.where(rows == low, 1.0, 0.0).astype(jnp.bfloat16)
    spread = jnp.dot(
        stacked[...].reshape(-1, LANES), pick, preferred_element_type=jnp.float32
    )
    ordered = jnp.zeros((targets, order.shape[1]), jnp.float32)
    for k in range(chunks * pieces):
        ordered = jnp.where(high == k, spread[k * targets : (k + 1) * targets, :], ordered)
    values = dot_rows(ordered.astype(jnp.bfloat16), inverse_ref[0])
    values_ref[0] = values
    partial = jnp.dot(
        values.astype(jnp.bfloat16), basis_ref[0], preferred_element_type=jnp.float32
    ).astype(jnp.bfloat16)
    share = targets // CORES
    for core in range(CORES):

        @pl.when(side_ref[1] == core)
        def _():
            same_ref[0] = partial[core * share : (core + 1) * share]
            cross_ref[0] = partial[(1 - core) * share : (2 - core) * share]


def leaf_up(side, points, point_order, leaf_inverse, leaf_basis):
    leaves, rows, leaf_size = leaf_inverse.shape
    rank = leaf_basis.shape[2]
    half = leaves // 2
    joined = points[0].ndim == 4
    if joined:
        shape = points[0].shape
    else:
        targets, width = points[0].shape
        shape = (len(points), width // LANES, targets, LANES)
    targets = shape[2]
    share = targets // CORES
    sent = jax.ShapeDtypeStruct((half, share, rank), jnp.bfloat16)
    out_specs = [
        pl.BlockSpec((1, targets, rows), lambda i, side: (i, 0, 0)),
        pl.BlockSpec((1, share, rank), lambda i, side: (i, 0, 0)),
        pl.BlockSpec((1, share, rank), lambda i, side: (i, 0, 0)),
    ]
    out_shape = [jax.ShapeDtypeStruct((half, targets, rows), jnp.float32), sent, sent]
    if not joined:
        out_specs.append(pl.BlockSpec(shape, lambda i, side: (0, 0, 0, 0)))
        out_shape.append(pltpu.VMEM(shape, jnp.bfloat16))
    point_specs = [
        pl.BlockSpec(block.shape, lambda i, side, rank=block.ndim: (0,) * rank) for block in points
    ]
    return pl.pallas_call(
        functools.partial(leaf_kernel, len(points)),
        grid_spec=pltpu.PrefetchScalarGridSpec(
            num_scalar_prefetch=1,
            grid=(half,),
            in_specs=[
                *point_specs,
                pl.BlockSpec((1, leaf_size), lambda i, side: (0, side[0] * half + i)),
                pl.BlockSpec((1, rows, leaf_size), lambda i, side: (side[0] * half + i, 0, 0)),
                pl.BlockSpec((1, rows, rank), lambda i, side: (side[0] * half + i, 0, 0)),
            ],
            out_specs=out_specs,
        ),
        out_shape=out_shape,
        compiler_params=params(),
        cost_estimate=cost(
            leaves * targets * leaf_size * (shape[0] * shape[1] * LANES + 2 * rows),
            leaves * rows * (leaf_size + rank + 3 * targets),
        ),
    )(side, *points, point_order.reshape(1, -1), leaf_inverse, leaf_basis)


def solve_node(stacked, inverses, bases, solved_ref):
    mine = lax.axis_index("rhs")
    total = None
    for flip, inverse, basis in zip(PIECES, inverses, bases):
        solved = dot_rows(stacked, inverse)
        solved_ref[mine ^ flip] = solved
        term = jnp.dot(solved.astype(jnp.bfloat16), basis, preferred_element_type=jnp.float32)
        total = term if total is None else total + term
    return total


def group_up_kernel(per_dev, *refs):
    *refs, solved_ref, out_ref = refs
    parts, packs = refs[: 2 * CORES], refs[2 * CORES :]
    levels, _ = half_levels(per_dev)
    rank = parts[0].shape[2]

    def pieces(node, start, width):
        return [ref[node, :, pl.ds(start, width)] for ref in packs]

    sums = sum(ref[...].astype(jnp.float32) for ref in parts).astype(jnp.bfloat16)
    current = [sums[i] for i in range(sums.shape[0])]
    for base, count, _ in levels:
        following = []
        for n in range(count):
            node = base + n
            compressed = solve_node(
                jnp.concatenate([current[2 * n], current[2 * n + 1]], axis=1),
                pieces(node, 0, 2 * rank),
                pieces(node, 2 * rank, rank),
                solved_ref.at[node],
            )
            following.append(compressed.astype(jnp.bfloat16))
        current = following
    out_ref[...] = current[0]


def group_up(per_dev, parts, packs):
    leaves, share, rank = parts[0].shape
    _, total = half_levels(per_dev)
    _, rows, width = packs[0].shape
    return pl.pallas_call(
        functools.partial(group_up_kernel, per_dev),
        out_shape=[
            jax.ShapeDtypeStruct((total, 2 * CORES, share, rows), jnp.float32),
            jax.ShapeDtypeStruct((share, rank), jnp.bfloat16),
        ],
        compiler_params=params(),
        cost_estimate=cost(24 * total * share * rows * rank, 8 * total * rows * width),
    )(*parts, *packs)


def order_pair(right, mine, other):
    return jnp.concatenate([jnp.where(right, other, mine), jnp.where(right, mine, other)], axis=1)


def half_up_kernel(mine_ref, other_ref, own_ref, near_ref, solved_ref, out_ref):
    rank = mine_ref.shape[1]
    place = lax.axis_index("rhs")
    stacked = order_pair(place // CORES == 1, mine_ref[...], other_ref[...])
    total = 0.0
    for flip, ref in enumerate((own_ref, near_ref)):
        solved = dot_rows(stacked, ref[0, :, : 2 * rank])
        solved_ref[(place ^ flip) % CORES] = solved
        total += jnp.dot(
            solved.astype(jnp.bfloat16),
            ref[0, :, 2 * rank : 3 * rank],
            preferred_element_type=jnp.float32,
        )
    out_ref[...] = total.astype(jnp.bfloat16)


def half_up(mine, other, own, near):
    share, rank = mine.shape
    nodes, rows, width = own.shape
    last = pl.BlockSpec((1, rows, width), lambda i: (nodes - 1, 0, 0))
    whole = pl.BlockSpec((share, rank), lambda i: (0, 0))
    return pl.pallas_call(
        half_up_kernel,
        grid=(1,),
        in_specs=[whole, whole, last, last],
        out_specs=[pl.BlockSpec((CORES, share, rows), lambda i: (0, 0, 0)), whole],
        out_shape=[
            jax.ShapeDtypeStruct((CORES, share, rows), jnp.float32),
            jax.ShapeDtypeStruct((share, rank), jnp.bfloat16),
        ],
        compiler_params=params(),
        cost_estimate=cost(12 * share * rows * rank, 4 * rows * width),
    )(mine, other, own, near)


def total_of(refs):
    if len(refs) == 1:
        return refs[0][...]
    return sum(ref[...].astype(jnp.float32) for ref in refs).astype(jnp.bfloat16)


def cross_pair(level, refs):
    half = len(refs) // 2
    is_right = (lax.axis_index("leaf") // (1 << level)) % 2 == 1
    return order_pair(is_right, total_of(refs[:half]), total_of(refs[half:]))


def cross_up_kernel(level, *refs):
    *refs, solved_ref, out_ref = refs
    inputs, packs = refs[: -2 * CORES], refs[-2 * CORES :]
    rank = out_ref.shape[1]
    compressed = solve_node(
        cross_pair(level, inputs),
        [ref[:, : 2 * rank] for ref in packs],
        [ref[:, 2 * rank : 3 * rank] for ref in packs],
        solved_ref,
    )
    out_ref[...] = compressed.astype(jnp.bfloat16)


def cross_up(level, inputs, packs):
    share, rank = inputs[0].shape[-2:]
    rows, width = packs[0].shape
    return pl.pallas_call(
        functools.partial(cross_up_kernel, level),
        out_shape=[
            jax.ShapeDtypeStruct((2 * CORES, share, rows), jnp.float32),
            jax.ShapeDtypeStruct((share, rank), jnp.bfloat16),
        ],
        compiler_params=params(),
        cost_estimate=cost(24 * share * rows * rank, 8 * rows * width),
    )(*inputs, *packs)


def down_kernel(per_dev, cross_levels, input_count, *refs):
    *refs, out_ref, value = refs
    inputs, refs = refs[:input_count], refs[input_count:]
    solved_cross, refs = refs[: cross_levels - 1], refs[cross_levels - 1 :]
    solved_top, solved_half, refs = refs[0], refs[1], refs[2:]
    count = 2 * CORES * (cross_levels - 1)
    cross_packs, (tail, near_tail, keep, keep_near) = refs[:count], refs[count:]
    levels, total = half_levels(per_dev)
    rank = out_ref.shape[2]
    node_size = 2 * rank
    place = lax.axis_index("rhs")

    def choose(which):
        return jnp.concatenate([value[2 * which], value[2 * which + 1]], axis=1)

    def side(level):
        return (lax.axis_index("leaf") // (1 << level)) % 2

    def columns(ref):
        width = ref.shape[-1]
        return pl.ds(width - rank, rank)

    stacked = cross_pair(cross_levels - 1, inputs)
    half = side(cross_levels - 1)
    for flip, ref in ((0, tail), (1, near_tail)):
        core = (place ^ flip) % CORES
        value[2 * half + core] = dot_rows(stacked, ref[:, :node_size]).astype(jnp.bfloat16)
    incoming = choose(half)
    for level in range(cross_levels - 2, -1, -1):
        packs = cross_packs[2 * CORES * level : 2 * CORES * (level + 1)]
        own, far, near, far_near = packs
        if level == 0:
            couplings = [ref[:, columns(ref)] for ref in packs]
        else:
            start = node_size + (total + level - 1) * rank
            couplings = [
                own[:, columns(own)],
                tail[:, start : start + rank],
                near[:, columns(near)],
                near_tail[:, start : start + rank],
            ]
        for flip, coupling in zip(PIECES, couplings):
            piece = place ^ flip
            solved = solved_cross[level][piece]
            value[piece] = (solved - dot_rows(incoming, coupling)).astype(jnp.bfloat16)
        incoming = choose(side(level))

    for flip, ref in ((0, keep), (1, keep_near)):
        piece = (place ^ flip) % CORES
        coupling = ref[total, :, columns(ref)]
        value[piece] = (solved_top[piece] - dot_rows(incoming, coupling)).astype(jnp.bfloat16)
    current = [choose(0)]
    for base, count, _ in reversed(levels):
        following = []
        for n in range(count):
            node = base + n
            start = node_size + node * rank
            couplings = (
                keep[node, :, columns(keep)],
                tail[:, start : start + rank],
                keep_near[node, :, columns(keep)],
                near_tail[:, start : start + rank],
            )
            for flip, coupling in zip(PIECES, couplings):
                piece = place ^ flip
                value[piece] = (
                    solved_half[node, piece] - dot_rows(current[n], coupling)
                ).astype(jnp.bfloat16)
            following += [choose(0), choose(1)]
        current = following
    for i, block in enumerate(current):
        out_ref[i] = block


def way_down(per_dev, inputs, solved_cross, solved_top, solved_half, cross_packs, others):
    share, rank = inputs[0].shape[-2:]
    rows = solved_half.shape[3]
    operands = [*inputs, *solved_cross, solved_top, solved_half]
    for packs in cross_packs:
        operands += packs
    operands += others
    return pl.pallas_call(
        functools.partial(down_kernel, per_dev, len(cross_packs) + 1, len(inputs)),
        out_shape=jax.ShapeDtypeStruct((per_dev // 2, share, rank), jnp.bfloat16),
        scratch_shapes=[pltpu.VMEM((2 * CORES, share, rows), jnp.bfloat16)],
        compiler_params=params(18),
        cost_estimate=cost(8 * share * rows * rank * per_dev, 4 * 1024 * 1024),
    )(*operands)


def finish_kernel(far_ref, own_ref, incoming_ref, coupling_ref, out_ref):
    half = own_ref.shape[0]
    high = lax.axis_index("rhs") // CORES
    for values_ref, side in ((far_ref, 1 - high), (own_ref, high)):
        for i in range(half):
            leaf = side * half + i
            incoming = jnp.concatenate(
                [incoming_ref[side * CORES + core, i] for core in range(CORES)], axis=0
            )
            out_ref[leaf] = values_ref[i] - dot_rows(incoming, coupling_ref[leaf])


def finish(far, own, incoming, coupling):
    half, targets, rows = own.shape
    return pl.pallas_call(
        finish_kernel,
        out_shape=jax.ShapeDtypeStruct((2 * half, targets, rows), jnp.float32),
        compiler_params=params(),
        cost_estimate=cost(4 * half * targets * rows * coupling.shape[2], 16 * own.size),
    )(far, own, incoming, coupling)


def swap(block, axis, bit):
    return lax.ppermute(block, axis, [(i, i ^ bit) for i in range(lax.axis_size(axis))])


def far_swap(block, leaf_bit, rhs_bit):
    shares = lax.axis_size("rhs")
    flip = leaf_bit * shares + rhs_bit
    count = lax.axis_size("leaf") * shares
    return lax.ppermute(block, ("leaf", "rhs"), [(i, i ^ flip) for i in range(count)])


def after(value, anchor):
    return lax.optimization_barrier((value, anchor))[0]


def body(
    right_side,
    point_order,
    leaf_inverse,
    leaf_basis,
    leaf_coupling,
    node_inverse,
    node_basis,
    node_coupling,
):
    devices = lax.axis_size("leaf")
    per_dev = leaf_inverse.shape[0]
    node_size = node_inverse.shape[2]
    rank = leaf_basis.shape[2]
    cross_levels = devices.bit_length() - 1
    place = lax.axis_index("rhs")
    high, low = place // CORES, place % CORES

    def rise(carrier, level, anchor, extras=()):
        other = after(swap(carrier, "leaf", 1 << level), anchor)
        width = node_size if level == cross_levels - 2 else carrier.shape[1]
        keep = [width] * (level < cross_levels - 1)
        ancestor, *carriers = climb(level, carrier, other, keep, extras)
        return (ancestor, *(carriers or [None]))

    send, send_coupling, keep, carrier = pack(node_inverse, node_basis, node_coupling)
    across, beside = after(
        [swap(right_side, "rhs", CORES), swap(right_side, "rhs", 1)], send
    )
    points = [across, beside, swap(after(across, beside), "rhs", 1)]
    half_far = swap(send, "rhs", CORES)
    keep_near = swap(after(keep, points), "rhs", 1)
    carrier = after(carrier, points)
    points = [right_side, *points]

    leaves = (point_order, leaf_inverse, leaf_basis)
    far_values, far_same, far_cross, joined = leaf_up(
        jnp.stack([1 - high, low]), points, *leaves
    )
    keep_near = after(keep_near, far_same)
    own_values, own_same, own_cross = leaf_up(
        jnp.stack([high, low]), [after(joined, keep_near)], *leaves
    )
    ancestor, carrier, send_coupling = rise(carrier, 0, own_same, [send_coupling])
    ancestors = [ancestor]
    far_same = after(swap(far_same, "rhs", CORES), own_same)
    far_cross = after(swap(far_cross, "rhs", CORES + 1), own_same)
    parts = [own_same, far_same, swap(own_cross, "rhs", 1), far_cross]
    half_far = after(half_far, (parts, carrier))
    half_near = swap(half_far, "rhs", 1)
    fars = [swap(after(ancestors[0], half_far), "rhs", CORES)]

    solved_half, current = group_up(per_dev, parts, [keep, half_far, keep_near, half_near])
    own_near = swap(join([ancestors[0]], current), "rhs", 1)
    other = swap(current, "rhs", CORES)
    ancestor, carrier = rise(carrier, 1, other)
    ancestors.append(ancestor)
    solved_top, current = half_up(current, after(other, own_near), keep, keep_near)
    fars[0] = after(fars[0], other)
    near_far = swap(fars[0], "rhs", 1)
    cross_packs = [[ancestors[0], fars[0], own_near, near_far]]
    factors = [(0, node_size + rank)]
    fars.append(swap(join([ancestors[1]], current, factors), "rhs", CORES))
    current = after(current, near_far)
    inputs = [
        current,
        swap(current, "rhs", CORES),
        swap(current, "leaf", 1),
        far_swap(current, 1, CORES),
    ]

    solved_cross = []
    for level in range(cross_levels - 1):
        if level > 0:
            own, far = ancestors[level], fars[level]
            own_near = swap(join([own], current), "rhs", 1)
            far_near = swap(join([far], current), "rhs", 1)
            cross_packs.append([own, far, own_near, far_near])
        solved, current = cross_up(level, inputs, cross_packs[level])
        solved_cross.append(solved)
        inputs = [current, swap(current, "leaf", 2 << level)]
        if level == 0:
            for later in range(2, cross_levels):
                ancestor, carrier = rise(carrier, later, current)
                ancestors.append(ancestor)
            for later in range(2, cross_levels - 1):
                fars.append(swap(join([ancestors[later]], current, factors), "rhs", CORES))
            blocks = [ancestors[-1], send_coupling, *ancestors[1:-1]]
            cuts = [(0, node_size), (0, send_coupling.shape[1])]
            cuts += [(node_size + rank, rank)] * (cross_levels - 2)
            tail = swap(join(blocks, current, cuts), "rhs", CORES)

    tail = hop(cross_levels - 1, ancestors[-1], tail, inputs[1])
    others = [tail, swap(tail, "rhs", 1), keep, keep_near]
    shares = way_down(per_dev, inputs, solved_cross, solved_top, solved_half, cross_packs, others)
    incoming = lax.all_gather(shares, "rhs", axis=0)
    return finish(far_values, own_values, incoming, leaf_coupling)


def solution(mesh):
    placed = (P(None, ("leaf", "rhs")), P("leaf")) + (P("leaf", "rhs", None),) * 6
    return jax.shard_map(
        body, mesh=mesh, in_specs=placed, out_specs=P("leaf", None, "rhs"), check_vma=False
    )
```

```python
import functools

import jax
import jax.numpy as jnp
from jax import lax
from jax.experimental import pallas as pl
from jax.experimental.pallas import tpu as pltpu
from jax.sharding import PartitionSpec as P

LANES = 256
PIECES = (0, 2, 1, 3)
CORES = 2


def params(mebibytes=12):
    return pltpu.CompilerParams(vmem_limit_bytes=mebibytes * 1024 * 1024)


def cost(flops, moved):
    return pl.CostEstimate(flops=flops // 1000, bytes_accessed=moved // 1000, transcendentals=0)


def dot_rows(left, right):
    return lax.dot_general(
        left, right, (((1,), (1,)), ((), ())), preferred_element_type=jnp.float32
    )


def half_levels(per_dev):
    levels = []
    base = 0
    for height in range(1, per_dev.bit_length() - 1):
        node_count = per_dev >> height
        levels.append((base, node_count // 2, per_dev - 2 * node_count))
        base += node_count // 2
    return levels, base


def pack_kernel(per_dev, inverse, basis, coupling, *refs):
    targets, buffers, (sems, out_sems) = refs[:4], refs[4:8], refs[8:]
    factors, couplings, keep, cross = buffers
    levels, total = half_levels(per_dev)
    high = lax.axis_index("rhs") // CORES
    node_size = inverse.shape[2]
    rank = basis.shape[2]
    parts = (
        (inverse, 0, node_size),
        (basis, node_size, rank),
        (coupling, node_size + rank, rank),
    )
    copies = []
    for source, start, width in parts:
        columns = pl.ds(start, width)
        for base, count, offset in levels:
            mine = source.at[pl.ds(offset + high * count, count)]
            other = source.at[pl.ds(offset + (1 - high) * count, count)]
            if source is coupling:
                for n in range(count):
                    sent = couplings.at[:, pl.ds((base + n) * rank, rank)]
                    copies.append((other.at[n], sent))
            else:
                copies.append((other, factors.at[pl.ds(base, count), :, columns]))
            copies.append((mine, keep.at[pl.ds(base, count), :, columns]))
        copies.append((source.at[per_dev - 2], keep.at[total, :, columns]))
        copies.append((source.at[per_dev - 1], cross.at[:, columns]))
    started = []
    for i, (source, target) in enumerate(copies):
        copy = pltpu.make_async_copy(source, target, sems.at[i])
        copy.start()
        started.append(copy)
    for copy in started:
        copy.wait()
    started = []
    for i, (buffer, target) in enumerate(zip(buffers, targets)):
        copy = pltpu.make_async_copy(buffer, target, out_sems.at[i])
        copy.start()
        started.append(copy)
    for copy in started:
        copy.wait()


def pack(inverse, basis, coupling):
    per_dev, rows, node_size = inverse.shape
    rank = basis.shape[2]
    width = node_size + 2 * rank
    levels, total = half_levels(per_dev)
    shapes = [
        (total, rows, node_size + rank),
        (rows, total * rank),
        (total + 1, rows, width),
        (rows, width),
    ]
    return pl.pallas_call(
        functools.partial(pack_kernel, per_dev),
        in_specs=[pl.BlockSpec(memory_space=pl.ANY)] * 3,
        out_specs=[pl.BlockSpec(memory_space=pl.ANY)] * 4,
        out_shape=[jax.ShapeDtypeStruct(shape, inverse.dtype) for shape in shapes],
        scratch_shapes=[pltpu.VMEM(shape, inverse.dtype) for shape in shapes]
        + [pltpu.SemaphoreType.DMA((6 + 5 * len(levels) + total,)), pltpu.SemaphoreType.DMA((4,))],
        compiler_params=params(63),
        cost_estimate=cost(0, 4 * per_dev * rows * width),
    )(inverse, basis, coupling)


def climb_kernel(level, count, mine_ref, other_ref, *refs):
    extras, (ancestor_ref, *outs) = refs[:count], refs[count:]
    carrier_refs, passed = outs[: len(outs) - count], outs[len(outs) - count :]
    for ref, extra in zip(passed, extras):
        ref[...] = extra[...]
    right = (lax.axis_index("leaf") // (1 << level)) % 2 == 1

    @pl.when(right)
    def _():
        ancestor_ref[...] = mine_ref[...]
        for ref in carrier_refs:
            ref[...] = other_ref[:, : ref.shape[1]]

    @pl.when(jnp.logical_not(right))
    def _():
        ancestor_ref[...] = other_ref[...]
        for ref in carrier_refs:
            ref[...] = mine_ref[:, : ref.shape[1]]


def climb(level, mine, other, keep, extras=()):
    return pl.pallas_call(
        functools.partial(climb_kernel, level, len(extras)),
        out_shape=[pltpu.VMEM(mine.shape, mine.dtype)]
        + [pltpu.VMEM((mine.shape[0], size), mine.dtype) for size in keep]
        + [pltpu.VMEM(extra.shape, extra.dtype) for extra in extras],
        compiler_params=params(),
        cost_estimate=cost(0, 4 * mine.size),
    )(mine, other, *extras)


def join_kernel(cuts, *refs):
    *blocks, _, out_ref = refs
    start = 0
    for ref, (first, width) in zip(blocks, cuts):
        out_ref[:, start : start + width] = ref[:, first : first + width]
        start += width


def join(blocks, anchor, cuts=None):
    rows = blocks[0].shape[0]
    cuts = cuts or [(0, block.shape[1]) for block in blocks]
    width = sum(size for _, size in cuts)
    return pl.pallas_call(
        functools.partial(join_kernel, cuts),
        out_shape=pltpu.VMEM((rows, width), blocks[0].dtype),
        compiler_params=params(),
        cost_estimate=cost(0, 4 * rows * width),
    )(*blocks, anchor)


def hop_kernel(level, top_ref, tail_ref, _, out_ref):
    side = (lax.axis_index("leaf") // (1 << level)) % 2
    here = lax.axis_index("rhs") // CORES == side

    @pl.when(here)
    def _():
        out_ref[...] = top_ref[...]

    @pl.when(jnp.logical_not(here))
    def _():
        out_ref[...] = tail_ref[...]


def hop(level, top, tail, anchor):
    return pl.pallas_call(
        functools.partial(hop_kernel, level),
        out_shape=pltpu.VMEM(tail.shape, tail.dtype),
        compiler_params=params(),
        cost_estimate=cost(0, 4 * tail.size),
    )(top, tail, anchor)


def leaf_kernel(count, side_ref, *refs):
    points, refs = refs[:count], refs[count:]
    order_ref, inverse_ref, basis_ref, values_ref, same_ref, cross_ref, *rest = refs
    targets = values_ref.shape[1]
    stacked = rest[0] if rest else points[0]
    chunks, pieces = stacked.shape[:2]

    if rest:

        @pl.when(pl.program_id(0) == 0)
        def _():
            place = lax.axis_index("rhs")
            for flip, points_ref in zip(PIECES, points):
                for w in range(pieces):
                    stacked[place ^ flip, w] = points_ref[:, w * LANES : (w + 1) * LANES]

    order = order_ref[...]
    high = order // LANES
    low = order % LANES
    rows = lax.broadcasted_iota(jnp.int32, (LANES, order.shape[1]), 0)
    pick = jnp.where(rows == low, 1.0, 0.0).astype(jnp.bfloat16)
    spread = jnp.dot(
        stacked[...].reshape(-1, LANES), pick, preferred_element_type=jnp.float32
    )
    ordered = jnp.zeros((targets, order.shape[1]), jnp.float32)
    for k in range(chunks * pieces):
        ordered = jnp.where(high == k, spread[k * targets : (k + 1) * targets, :], ordered)
    values = dot_rows(ordered.astype(jnp.bfloat16), inverse_ref[0])
    values_ref[0] = values
    partial = jnp.dot(
        values.astype(jnp.bfloat16), basis_ref[0], preferred_element_type=jnp.float32
    ).astype(jnp.bfloat16)
    share = targets // CORES
    for core in range(CORES):

        @pl.when(side_ref[1] == core)
        def _():
            same_ref[0] = partial[core * share : (core + 1) * share]
            cross_ref[0] = partial[(1 - core) * share : (2 - core) * share]


def leaf_up(side, points, point_order, leaf_inverse, leaf_basis):
    leaves, rows, leaf_size = leaf_inverse.shape
    rank = leaf_basis.shape[2]
    half = leaves // 2
    joined = points[0].ndim == 4
    if joined:
        shape = points[0].shape
    else:
        targets, width = points[0].shape
        shape = (len(points), width // LANES, targets, LANES)
    targets = shape[2]
    share = targets // CORES
    sent = jax.ShapeDtypeStruct((half, share, rank), jnp.bfloat16)
    out_specs = [
        pl.BlockSpec((1, targets, rows), lambda i, side: (i, 0, 0)),
        pl.BlockSpec((1, share, rank), lambda i, side: (i, 0, 0)),
        pl.BlockSpec((1, share, rank), lambda i, side: (i, 0, 0)),
    ]
    out_shape = [jax.ShapeDtypeStruct((half, targets, rows), jnp.float32), sent, sent]
    if not joined:
        out_specs.append(pl.BlockSpec(shape, lambda i, side: (0, 0, 0, 0)))
        out_shape.append(pltpu.VMEM(shape, jnp.bfloat16))
    point_specs = [
        pl.BlockSpec(block.shape, lambda i, side, rank=block.ndim: (0,) * rank) for block in points
    ]
    return pl.pallas_call(
        functools.partial(leaf_kernel, len(points)),
        grid_spec=pltpu.PrefetchScalarGridSpec(
            num_scalar_prefetch=1,
            grid=(half,),
            in_specs=[
                *point_specs,
                pl.BlockSpec((1, leaf_size), lambda i, side: (0, side[0] * half + i)),
                pl.BlockSpec((1, rows, leaf_size), lambda i, side: (side[0] * half + i, 0, 0)),
                pl.BlockSpec((1, rows, rank), lambda i, side: (side[0] * half + i, 0, 0)),
            ],
            out_specs=out_specs,
        ),
        out_shape=out_shape,
        compiler_params=params(),
        cost_estimate=cost(
            leaves * targets * leaf_size * (shape[0] * shape[1] * LANES + 2 * rows),
            leaves * rows * (leaf_size + rank + 3 * targets),
        ),
    )(side, *points, point_order.reshape(1, -1), leaf_inverse, leaf_basis)


def solve_node(stacked, inverses, bases, solved_ref):
    mine = lax.axis_index("rhs")
    total = None
    for flip, inverse, basis in zip(PIECES, inverses, bases):
        solved = dot_rows(stacked, inverse)
        solved_ref[mine ^ flip] = solved
        term = jnp.dot(solved.astype(jnp.bfloat16), basis, preferred_element_type=jnp.float32)
        total = term if total is None else total + term
    return total


def group_up_kernel(per_dev, *refs):
    *refs, solved_ref, out_ref = refs
    parts, (own, far, near, *far_near) = refs[: 2 * CORES], refs[2 * CORES :]
    levels, _ = half_levels(per_dev)
    rank = parts[0].shape[2]

    def pieces(node, start, width):
        columns = pl.ds(start, width)
        return [
            own[node, :, columns],
            far[node, :, columns],
            near[node, :, columns],
            far_near[node][:, columns],
        ]

    sums = sum(ref[...].astype(jnp.float32) for ref in parts).astype(jnp.bfloat16)
    current = [sums[i] for i in range(sums.shape[0])]
    for base, count, _ in levels:
        following = []
        for n in range(count):
            node = base + n
            compressed = solve_node(
                jnp.concatenate([current[2 * n], current[2 * n + 1]], axis=1),
                pieces(node, 0, 2 * rank),
                pieces(node, 2 * rank, rank),
                solved_ref.at[node],
            )
            following.append(compressed.astype(jnp.bfloat16))
        current = following
    out_ref[...] = current[0]


def group_up(per_dev, parts, packs):
    leaves, share, rank = parts[0].shape
    _, total = half_levels(per_dev)
    _, rows, width = packs[0].shape
    return pl.pallas_call(
        functools.partial(group_up_kernel, per_dev),
        out_shape=[
            jax.ShapeDtypeStruct((total, 2 * CORES, share, rows), jnp.float32),
            jax.ShapeDtypeStruct((share, rank), jnp.bfloat16),
        ],
        compiler_params=params(),
        cost_estimate=cost(24 * total * share * rows * rank, 8 * total * rows * width),
    )(*parts, *packs)


def order_pair(right, mine, other):
    return jnp.concatenate([jnp.where(right, other, mine), jnp.where(right, mine, other)], axis=1)


def half_up_kernel(mine_ref, other_ref, own_ref, near_ref, solved_ref, out_ref):
    rank = mine_ref.shape[1]
    place = lax.axis_index("rhs")
    stacked = order_pair(place // CORES == 1, mine_ref[...], other_ref[...])
    total = 0.0
    for flip, ref in enumerate((own_ref, near_ref)):
        solved = dot_rows(stacked, ref[0, :, : 2 * rank])
        solved_ref[(place ^ flip) % CORES] = solved
        total += jnp.dot(
            solved.astype(jnp.bfloat16),
            ref[0, :, 2 * rank : 3 * rank],
            preferred_element_type=jnp.float32,
        )
    out_ref[...] = total.astype(jnp.bfloat16)


def half_up(mine, other, own, near):
    share, rank = mine.shape
    nodes, rows, width = own.shape
    last = pl.BlockSpec((1, rows, width), lambda i: (nodes - 1, 0, 0))
    whole = pl.BlockSpec((share, rank), lambda i: (0, 0))
    return pl.pallas_call(
        half_up_kernel,
        grid=(1,),
        in_specs=[whole, whole, last, last],
        out_specs=[pl.BlockSpec((CORES, share, rows), lambda i: (0, 0, 0)), whole],
        out_shape=[
            jax.ShapeDtypeStruct((CORES, share, rows), jnp.float32),
            jax.ShapeDtypeStruct((share, rank), jnp.bfloat16),
        ],
        compiler_params=params(),
        cost_estimate=cost(12 * share * rows * rank, 4 * rows * width),
    )(mine, other, own, near)


def total_of(refs):
    if len(refs) == 1:
        return refs[0][...]
    return sum(ref[...].astype(jnp.float32) for ref in refs).astype(jnp.bfloat16)


def cross_pair(level, refs):
    half = len(refs) // 2
    is_right = (lax.axis_index("leaf") // (1 << level)) % 2 == 1
    return order_pair(is_right, total_of(refs[:half]), total_of(refs[half:]))


def cross_up_kernel(level, *refs):
    *refs, solved_ref, out_ref = refs
    inputs, packs = refs[: -2 * CORES], refs[-2 * CORES :]
    rank = out_ref.shape[1]
    compressed = solve_node(
        cross_pair(level, inputs),
        [ref[:, : 2 * rank] for ref in packs],
        [ref[:, 2 * rank : 3 * rank] for ref in packs],
        solved_ref,
    )
    out_ref[...] = compressed.astype(jnp.bfloat16)


def cross_up(level, inputs, packs):
    share, rank = inputs[0].shape[-2:]
    rows, width = packs[0].shape
    return pl.pallas_call(
        functools.partial(cross_up_kernel, level),
        out_shape=[
            jax.ShapeDtypeStruct((2 * CORES, share, rows), jnp.float32),
            jax.ShapeDtypeStruct((share, rank), jnp.bfloat16),
        ],
        compiler_params=params(),
        cost_estimate=cost(24 * share * rows * rank, 8 * rows * width),
    )(*inputs, *packs)


def down_kernel(per_dev, cross_levels, input_count, *refs):
    *refs, out_ref, value = refs
    inputs, refs = refs[:input_count], refs[input_count:]
    solved_cross, refs = refs[: cross_levels - 1], refs[cross_levels - 1 :]
    solved_top, solved_half, refs = refs[0], refs[1], refs[2:]
    count = 2 * CORES * (cross_levels - 1)
    cross_packs, others = refs[:count], refs[count:]
    tail, near_tail, half_tail, near_half_tail, keep, keep_near = others
    levels, total = half_levels(per_dev)
    rank = out_ref.shape[2]
    node_size = 2 * rank
    place = lax.axis_index("rhs")

    def choose(which):
        return jnp.concatenate([value[2 * which], value[2 * which + 1]], axis=1)

    def side(level):
        return (lax.axis_index("leaf") // (1 << level)) % 2

    def columns(ref):
        width = ref.shape[-1]
        return pl.ds(width - rank, rank)

    stacked = cross_pair(cross_levels - 1, inputs)
    half = side(cross_levels - 1)
    for flip, ref in ((0, tail), (1, near_tail)):
        core = (place ^ flip) % CORES
        value[2 * half + core] = dot_rows(stacked, ref[:, :node_size]).astype(jnp.bfloat16)
    incoming = choose(half)
    for level in range(cross_levels - 2, -1, -1):
        packs = cross_packs[2 * CORES * level : 2 * CORES * (level + 1)]
        couplings = [ref[:, columns(ref)] for ref in packs]
        for flip, coupling in zip(PIECES, couplings):
            piece = place ^ flip
            solved = solved_cross[level][piece]
            value[piece] = (solved - dot_rows(incoming, coupling)).astype(jnp.bfloat16)
        incoming = choose(side(level))

    for flip, ref in ((0, keep), (1, keep_near)):
        piece = (place ^ flip) % CORES
        coupling = ref[total, :, columns(ref)]
        value[piece] = (solved_top[piece] - dot_rows(incoming, coupling)).astype(jnp.bfloat16)
    current = [choose(0)]
    for base, count, _ in reversed(levels):
        following = []
        for n in range(count):
            node = base + n
            start = node * rank
            couplings = (
                keep[node, :, columns(keep)],
                half_tail[:, start : start + rank],
                keep_near[node, :, columns(keep)],
                near_half_tail[:, start : start + rank],
            )
            for flip, coupling in zip(PIECES, couplings):
                piece = place ^ flip
                value[piece] = (
                    solved_half[node, piece] - dot_rows(current[n], coupling)
                ).astype(jnp.bfloat16)
            following += [choose(0), choose(1)]
        current = following
    for i, block in enumerate(current):
        out_ref[i] = block


def way_down(per_dev, inputs, solved_cross, solved_top, solved_half, cross_packs, others):
    share, rank = inputs[0].shape[-2:]
    rows = solved_half.shape[3]
    operands = [*inputs, *solved_cross, solved_top, solved_half]
    for packs in cross_packs:
        operands += packs
    operands += others
    return pl.pallas_call(
        functools.partial(down_kernel, per_dev, len(cross_packs) + 1, len(inputs)),
        out_shape=jax.ShapeDtypeStruct((per_dev // 2, share, rank), jnp.bfloat16),
        scratch_shapes=[pltpu.VMEM((2 * CORES, share, rows), jnp.bfloat16)],
        compiler_params=params(18),
        cost_estimate=cost(8 * share * rows * rank * per_dev, 4 * 1024 * 1024),
    )(*operands)


def finish_kernel(far_ref, own_ref, incoming_ref, coupling_ref, out_ref):
    half = own_ref.shape[0]
    high = lax.axis_index("rhs") // CORES
    for values_ref, side in ((far_ref, 1 - high), (own_ref, high)):
        for i in range(half):
            leaf = side * half + i
            incoming = jnp.concatenate(
                [incoming_ref[side * CORES + core, i] for core in range(CORES)], axis=0
            )
            out_ref[leaf] = values_ref[i] - dot_rows(incoming, coupling_ref[leaf])


def finish(far, own, incoming, coupling):
    half, targets, rows = own.shape
    return pl.pallas_call(
        finish_kernel,
        out_shape=jax.ShapeDtypeStruct((2 * half, targets, rows), jnp.float32),
        compiler_params=params(),
        cost_estimate=cost(4 * half * targets * rows * coupling.shape[2], 16 * own.size),
    )(far, own, incoming, coupling)


def swap(block, axis, bit):
    return lax.ppermute(block, axis, [(i, i ^ bit) for i in range(lax.axis_size(axis))])


def far_swap(block, leaf_bit, rhs_bit):
    shares = lax.axis_size("rhs")
    flip = leaf_bit * shares + rhs_bit
    count = lax.axis_size("leaf") * shares
    return lax.ppermute(block, ("leaf", "rhs"), [(i, i ^ flip) for i in range(count)])


def after(value, anchor):
    return lax.optimization_barrier((value, anchor))[0]


def body(
    right_side,
    point_order,
    leaf_inverse,
    leaf_basis,
    leaf_coupling,
    node_inverse,
    node_basis,
    node_coupling,
):
    devices = lax.axis_size("leaf")
    per_dev = leaf_inverse.shape[0]
    node_size = node_inverse.shape[2]
    rank = leaf_basis.shape[2]
    cross_levels = devices.bit_length() - 1
    place = lax.axis_index("rhs")
    high, low = place // CORES, place % CORES

    def rise(carrier, level, anchor, extras=()):
        other = after(swap(carrier, "leaf", 1 << level), anchor)
        width = node_size if level == cross_levels - 2 else carrier.shape[1]
        keep = [width] * (level < cross_levels - 1)
        ancestor, *carriers = climb(level, carrier, other, keep, extras)
        return (ancestor, *(carriers or [None]))

    send, send_coupling, keep, carrier = pack(node_inverse, node_basis, node_coupling)
    across, beside = after(
        [swap(right_side, "rhs", CORES), swap(right_side, "rhs", 1)], send
    )
    points = [across, beside, swap(after(across, beside), "rhs", 1)]
    half_far = swap(send, "rhs", CORES)
    keep_near = swap(after(keep, points), "rhs", 1)
    carrier = after(carrier, points)
    points = [right_side, *points]

    leaves = (point_order, leaf_inverse, leaf_basis)
    far_values, far_same, far_cross, joined = leaf_up(
        jnp.stack([1 - high, low]), points, *leaves
    )
    keep_near = after(keep_near, far_same)
    own_values, own_same, own_cross = leaf_up(
        jnp.stack([high, low]), [after(joined, keep_near)], *leaves
    )
    ancestor, carrier, send_coupling = rise(carrier, 0, own_same, [send_coupling])
    ancestors = [ancestor]
    far_same = after(swap(far_same, "rhs", CORES), own_same)
    far_cross = after(swap(far_cross, "rhs", CORES + 1), own_same)
    parts = [own_same, far_same, swap(own_cross, "rhs", 1), far_cross]
    half_far = after(half_far, (parts, carrier))
    half_near = [swap(half_far[n], "rhs", 1) for n in range(half_far.shape[0])]
    ancestor, carrier = rise(carrier, 1, parts)
    ancestors.append(ancestor)
    parts = after(parts, ancestor)
    fars = [swap(after(ancestors[0], half_far), "rhs", CORES)]

    solved_half, current = group_up(per_dev, parts, [keep, half_far, keep_near, *half_near])
    own_near = swap(after(ancestors[0], half_far), "rhs", 1)
    other = swap(after(current, own_near), "rhs", CORES)
    solved_top, current = half_up(current, after(other, own_near), keep, keep_near)
    fars[0] = after(fars[0], other)
    near_far = swap(fars[0], "rhs", 1)
    cross_packs = [[ancestors[0], fars[0], own_near, near_far]]
    anchor = other
    fars.append(swap(join([ancestors[1]], anchor), "rhs", CORES))
    half_tail = swap(join([send_coupling], current), "rhs", CORES)
    current = after(current, near_far)
    inputs = [
        current,
        swap(current, "rhs", CORES),
        swap(current, "leaf", 1),
        far_swap(current, 1, CORES),
    ]

    for level in range(2, cross_levels):
        ancestor, carrier = rise(carrier, level, other)
        ancestors.append(ancestor)
    inputs = after(inputs, ancestors[-1])
    solved_cross = []
    for level in range(cross_levels - 1):
        if level > 0:
            own, far = ancestors[level], fars[level]
            own_near = swap(join([own], current), "rhs", 1)
            far_near = swap(join([far], current), "rhs", 1)
            cross_packs.append([own, far, own_near, far_near])
        solved, current = cross_up(level, inputs, cross_packs[level])
        solved_cross.append(solved)
        inputs = [current, swap(current, "leaf", 2 << level)]
        if level == 0:
            for later in range(2, cross_levels - 1):
                fars.append(swap(join([ancestors[later]], current), "rhs", CORES))
            tail = swap(join([ancestors[-1]], current), "rhs", CORES)

    near_half_tail = swap(join([half_tail], current), "rhs", 1)
    tail = hop(cross_levels - 1, ancestors[-1], tail, inputs[1])
    others = [tail, swap(tail, "rhs", 1), half_tail, near_half_tail, keep, keep_near]
    shares = way_down(per_dev, inputs, solved_cross, solved_top, solved_half, cross_packs, others)
    incoming = lax.all_gather(shares, "rhs", axis=0)
    return finish(far_values, own_values, incoming, leaf_coupling)


def solution(mesh):
    placed = (P(None, ("leaf", "rhs")), P("leaf")) + (P("leaf", "rhs", None),) * 6
    return jax.shard_map(
        body, mesh=mesh, in_specs=placed, out_specs=P("leaf", None, "rhs"), check_vma=False
    )
```

```python
import functools

import jax
import jax.numpy as jnp
from jax import lax
from jax.experimental import pallas as pl
from jax.experimental.pallas import tpu as pltpu
from jax.sharding import PartitionSpec as P

LANES = 256
PIECES = (0, 2, 1, 3)
CORES = 2


def params(mebibytes=12):
    return pltpu.CompilerParams(vmem_limit_bytes=mebibytes * 1024 * 1024)


def cost(flops, moved):
    return pl.CostEstimate(flops=flops // 1000, bytes_accessed=moved // 1000, transcendentals=0)


def dot_rows(left, right):
    return lax.dot_general(
        left, right, (((1,), (1,)), ((), ())), preferred_element_type=jnp.float32
    )


def half_levels(per_dev):
    levels = []
    base = 0
    for height in range(1, per_dev.bit_length() - 1):
        node_count = per_dev >> height
        levels.append((base, node_count // 2, per_dev - 2 * node_count))
        base += node_count // 2
    return levels, base


def pack_kernel(per_dev, inverse, basis, coupling, *refs):
    targets, buffers, (sems, out_sems) = refs[:4], refs[4:8], refs[8:]
    factors, couplings, keep, cross = buffers
    levels, total = half_levels(per_dev)
    high = lax.axis_index("rhs") // CORES
    node_size = inverse.shape[2]
    rank = basis.shape[2]
    parts = (
        (inverse, 0, node_size),
        (basis, node_size, rank),
        (coupling, node_size + rank, rank),
    )
    copies = []
    for source, start, width in parts:
        columns = pl.ds(start, width)
        for base, count, offset in levels:
            mine = source.at[pl.ds(offset + high * count, count)]
            other = source.at[pl.ds(offset + (1 - high) * count, count)]
            if source is coupling:
                for n in range(count):
                    sent = couplings.at[:, pl.ds((base + n) * rank, rank)]
                    copies.append((other.at[n], sent))
            else:
                copies.append((other, factors.at[pl.ds(base, count), :, columns]))
            copies.append((mine, keep.at[pl.ds(base, count), :, columns]))
        copies.append((source.at[per_dev - 2], keep.at[total, :, columns]))
        copies.append((source.at[per_dev - 1], cross.at[:, columns]))
    started = []
    for i, (source, target) in enumerate(copies):
        copy = pltpu.make_async_copy(source, target, sems.at[i])
        copy.start()
        started.append(copy)
    for copy in started:
        copy.wait()
    started = []
    for i, (buffer, target) in enumerate(zip(buffers, targets)):
        copy = pltpu.make_async_copy(buffer, target, out_sems.at[i])
        copy.start()
        started.append(copy)
    for copy in started:
        copy.wait()


def pack(inverse, basis, coupling):
    per_dev, rows, node_size = inverse.shape
    rank = basis.shape[2]
    width = node_size + 2 * rank
    levels, total = half_levels(per_dev)
    shapes = [
        (total, rows, node_size + rank),
        (rows, total * rank),
        (total + 1, rows, width),
        (rows, width),
    ]
    return pl.pallas_call(
        functools.partial(pack_kernel, per_dev),
        in_specs=[pl.BlockSpec(memory_space=pl.ANY)] * 3,
        out_specs=[pl.BlockSpec(memory_space=pl.ANY)] * 4,
        out_shape=[jax.ShapeDtypeStruct(shape, inverse.dtype) for shape in shapes],
        scratch_shapes=[pltpu.VMEM(shape, inverse.dtype) for shape in shapes]
        + [pltpu.SemaphoreType.DMA((6 + 5 * len(levels) + total,)), pltpu.SemaphoreType.DMA((4,))],
        compiler_params=params(63),
        cost_estimate=cost(0, 4 * per_dev * rows * width),
    )(inverse, basis, coupling)


def climb_kernel(level, count, mine_ref, other_ref, *refs):
    extras, (ancestor_ref, *outs) = refs[:count], refs[count:]
    carrier_refs, passed = outs[: len(outs) - count], outs[len(outs) - count :]
    for ref, extra in zip(passed, extras):
        ref[...] = extra[...]
    right = (lax.axis_index("leaf") // (1 << level)) % 2 == 1

    @pl.when(right)
    def _():
        ancestor_ref[...] = mine_ref[...]
        for ref in carrier_refs:
            ref[...] = other_ref[:, : ref.shape[1]]

    @pl.when(jnp.logical_not(right))
    def _():
        ancestor_ref[...] = other_ref[...]
        for ref in carrier_refs:
            ref[...] = mine_ref[:, : ref.shape[1]]


def climb(level, mine, other, keep, extras=()):
    return pl.pallas_call(
        functools.partial(climb_kernel, level, len(extras)),
        out_shape=[pltpu.VMEM(mine.shape, mine.dtype)]
        + [pltpu.VMEM((mine.shape[0], size), mine.dtype) for size in keep]
        + [pltpu.VMEM(extra.shape, extra.dtype) for extra in extras],
        compiler_params=params(),
        cost_estimate=cost(0, 4 * mine.size),
    )(mine, other, *extras)


def join_kernel(cuts, *refs):
    *blocks, _, out_ref = refs
    start = 0
    for ref, (first, width) in zip(blocks, cuts):
        out_ref[:, start : start + width] = ref[:, first : first + width]
        start += width


def join(blocks, anchor, cuts=None):
    rows = blocks[0].shape[0]
    cuts = cuts or [(0, block.shape[1]) for block in blocks]
    width = sum(size for _, size in cuts)
    return pl.pallas_call(
        functools.partial(join_kernel, cuts),
        out_shape=pltpu.VMEM((rows, width), blocks[0].dtype),
        compiler_params=params(),
        cost_estimate=cost(0, 4 * rows * width),
    )(*blocks, anchor)


def hop_kernel(level, top_ref, tail_ref, _, out_ref):
    node_size = top_ref.shape[1]
    side = (lax.axis_index("leaf") // (1 << level)) % 2
    here = lax.axis_index("rhs") // CORES == side
    out_ref[:, node_size:] = tail_ref[:, node_size:]

    @pl.when(here)
    def _():
        out_ref[:, :node_size] = top_ref[...]

    @pl.when(jnp.logical_not(here))
    def _():
        out_ref[:, :node_size] = tail_ref[:, :node_size]


def hop(level, top, tail, anchor):
    return pl.pallas_call(
        functools.partial(hop_kernel, level),
        out_shape=pltpu.VMEM(tail.shape, tail.dtype),
        compiler_params=params(),
        cost_estimate=cost(0, 4 * tail.size),
    )(top, tail, anchor)


def leaf_kernel(count, side_ref, *refs):
    points, refs = refs[:count], refs[count:]
    order_ref, inverse_ref, basis_ref, values_ref, same_ref, cross_ref, *rest = refs
    targets = values_ref.shape[1]
    stacked = rest[0] if rest else points[0]
    chunks, pieces = stacked.shape[:2]

    if rest:

        @pl.when(pl.program_id(0) == 0)
        def _():
            place = lax.axis_index("rhs")
            for flip, points_ref in zip(PIECES, points):
                for w in range(pieces):
                    stacked[place ^ flip, w] = points_ref[:, w * LANES : (w + 1) * LANES]

    order = order_ref[...]
    high = order // LANES
    low = order % LANES
    rows = lax.broadcasted_iota(jnp.int32, (LANES, order.shape[1]), 0)
    pick = jnp.where(rows == low, 1.0, 0.0).astype(jnp.bfloat16)
    spread = jnp.dot(
        stacked[...].reshape(-1, LANES), pick, preferred_element_type=jnp.float32
    )
    ordered = jnp.zeros((targets, order.shape[1]), jnp.float32)
    for k in range(chunks * pieces):
        ordered = jnp.where(high == k, spread[k * targets : (k + 1) * targets, :], ordered)
    values = dot_rows(ordered.astype(jnp.bfloat16), inverse_ref[0])
    values_ref[0] = values
    partial = jnp.dot(
        values.astype(jnp.bfloat16), basis_ref[0], preferred_element_type=jnp.float32
    ).astype(jnp.bfloat16)
    share = targets // CORES
    for core in range(CORES):

        @pl.when(side_ref[1] == core)
        def _():
            same_ref[0] = partial[core * share : (core + 1) * share]
            cross_ref[0] = partial[(1 - core) * share : (2 - core) * share]


def leaf_up(side, points, point_order, leaf_inverse, leaf_basis):
    leaves, rows, leaf_size = leaf_inverse.shape
    rank = leaf_basis.shape[2]
    half = leaves // 2
    joined = points[0].ndim == 4
    if joined:
        shape = points[0].shape
    else:
        targets, width = points[0].shape
        shape = (len(points), width // LANES, targets, LANES)
    targets = shape[2]
    share = targets // CORES
    sent = jax.ShapeDtypeStruct((half, share, rank), jnp.bfloat16)
    out_specs = [
        pl.BlockSpec((1, targets, rows), lambda i, side: (i, 0, 0)),
        pl.BlockSpec((1, share, rank), lambda i, side: (i, 0, 0)),
        pl.BlockSpec((1, share, rank), lambda i, side: (i, 0, 0)),
    ]
    out_shape = [jax.ShapeDtypeStruct((half, targets, rows), jnp.float32), sent, sent]
    if not joined:
        out_specs.append(pl.BlockSpec(shape, lambda i, side: (0, 0, 0, 0)))
        out_shape.append(pltpu.VMEM(shape, jnp.bfloat16))
    point_specs = [
        pl.BlockSpec(block.shape, lambda i, side, rank=block.ndim: (0,) * rank) for block in points
    ]
    return pl.pallas_call(
        functools.partial(leaf_kernel, len(points)),
        grid_spec=pltpu.PrefetchScalarGridSpec(
            num_scalar_prefetch=1,
            grid=(half,),
            in_specs=[
                *point_specs,
                pl.BlockSpec((1, leaf_size), lambda i, side: (0, side[0] * half + i)),
                pl.BlockSpec((1, rows, leaf_size), lambda i, side: (side[0] * half + i, 0, 0)),
                pl.BlockSpec((1, rows, rank), lambda i, side: (side[0] * half + i, 0, 0)),
            ],
            out_specs=out_specs,
        ),
        out_shape=out_shape,
        compiler_params=params(),
        cost_estimate=cost(
            leaves * targets * leaf_size * (shape[0] * shape[1] * LANES + 2 * rows),
            leaves * rows * (leaf_size + rank + 3 * targets),
        ),
    )(side, *points, point_order.reshape(1, -1), leaf_inverse, leaf_basis)


def solve_node(stacked, inverses, bases, solved_ref):
    mine = lax.axis_index("rhs")
    total = None
    for flip, inverse, basis in zip(PIECES, inverses, bases):
        solved = dot_rows(stacked, inverse)
        solved_ref[mine ^ flip] = solved
        term = jnp.dot(solved.astype(jnp.bfloat16), basis, preferred_element_type=jnp.float32)
        total = term if total is None else total + term
    return total


def group_up_kernel(per_dev, *refs):
    *refs, solved_ref, out_ref = refs
    parts, packs = refs[: 2 * CORES], refs[2 * CORES :]
    levels, _ = half_levels(per_dev)
    rank = parts[0].shape[2]

    def pieces(node, start, width):
        return [ref[node, :, pl.ds(start, width)] for ref in packs]

    sums = sum(ref[...].astype(jnp.float32) for ref in parts).astype(jnp.bfloat16)
    current = [sums[i] for i in range(sums.shape[0])]
    for base, count, _ in levels:
        following = []
        for n in range(count):
            node = base + n
            compressed = solve_node(
                jnp.concatenate([current[2 * n], current[2 * n + 1]], axis=1),
                pieces(node, 0, 2 * rank),
                pieces(node, 2 * rank, rank),
                solved_ref.at[node],
            )
            following.append(compressed.astype(jnp.bfloat16))
        current = following
    out_ref[...] = current[0]


def group_up(per_dev, parts, packs):
    leaves, share, rank = parts[0].shape
    _, total = half_levels(per_dev)
    _, rows, width = packs[0].shape
    return pl.pallas_call(
        functools.partial(group_up_kernel, per_dev),
        out_shape=[
            jax.ShapeDtypeStruct((total, 2 * CORES, share, rows), jnp.float32),
            jax.ShapeDtypeStruct((share, rank), jnp.bfloat16),
        ],
        compiler_params=params(),
        cost_estimate=cost(24 * total * share * rows * rank, 8 * total * rows * width),
    )(*parts, *packs)


def order_pair(right, mine, other):
    return jnp.concatenate([jnp.where(right, other, mine), jnp.where(right, mine, other)], axis=1)


def half_up_kernel(mine_ref, other_ref, own_ref, near_ref, solved_ref, out_ref):
    rank = mine_ref.shape[1]
    place = lax.axis_index("rhs")
    stacked = order_pair(place // CORES == 1, mine_ref[...], other_ref[...])
    total = 0.0
    for flip, ref in enumerate((own_ref, near_ref)):
        solved = dot_rows(stacked, ref[0, :, : 2 * rank])
        solved_ref[(place ^ flip) % CORES] = solved
        total += jnp.dot(
            solved.astype(jnp.bfloat16),
            ref[0, :, 2 * rank : 3 * rank],
            preferred_element_type=jnp.float32,
        )
    out_ref[...] = total.astype(jnp.bfloat16)


def half_up(mine, other, own, near):
    share, rank = mine.shape
    nodes, rows, width = own.shape
    last = pl.BlockSpec((1, rows, width), lambda i: (nodes - 1, 0, 0))
    whole = pl.BlockSpec((share, rank), lambda i: (0, 0))
    return pl.pallas_call(
        half_up_kernel,
        grid=(1,),
        in_specs=[whole, whole, last, last],
        out_specs=[pl.BlockSpec((CORES, share, rows), lambda i: (0, 0, 0)), whole],
        out_shape=[
            jax.ShapeDtypeStruct((CORES, share, rows), jnp.float32),
            jax.ShapeDtypeStruct((share, rank), jnp.bfloat16),
        ],
        compiler_params=params(),
        cost_estimate=cost(12 * share * rows * rank, 4 * rows * width),
    )(mine, other, own, near)


def total_of(refs):
    if len(refs) == 1:
        return refs[0][...]
    return sum(ref[...].astype(jnp.float32) for ref in refs).astype(jnp.bfloat16)


def cross_pair(level, refs):
    half = len(refs) // 2
    refs = refs[::-1] if half > 1 else refs
    is_right = (lax.axis_index("leaf") // (1 << level)) % 2 == 1
    return order_pair(is_right, total_of(refs[:half]), total_of(refs[half:]))


def cross_up_kernel(level, *refs):
    *refs, solved_ref, out_ref = refs
    inputs, packs = refs[: -2 * CORES], refs[-2 * CORES :]
    rank = out_ref.shape[1]
    compressed = solve_node(
        cross_pair(level, inputs),
        [ref[:, : 2 * rank] for ref in packs],
        [ref[:, 2 * rank : 3 * rank] for ref in packs],
        solved_ref,
    )
    out_ref[...] = compressed.astype(jnp.bfloat16)


def cross_up(level, inputs, packs):
    share, rank = inputs[0].shape[-2:]
    rows, width = packs[0].shape
    return pl.pallas_call(
        functools.partial(cross_up_kernel, level),
        out_shape=[
            jax.ShapeDtypeStruct((2 * CORES, share, rows), jnp.float32),
            jax.ShapeDtypeStruct((share, rank), jnp.bfloat16),
        ],
        compiler_params=params(),
        cost_estimate=cost(24 * share * rows * rank, 8 * rows * width),
    )(*inputs, *packs)


def down_kernel(per_dev, cross_levels, input_count, *refs):
    *refs, out_ref, value = refs
    inputs, refs = refs[:input_count], refs[input_count:]
    solved_cross, refs = refs[: cross_levels - 1], refs[cross_levels - 1 :]
    solved_top, solved_half, refs = refs[0], refs[1], refs[2:]
    count = 2 * CORES * (cross_levels - 1)
    cross_packs, (tail, near_tail, keep, keep_near) = refs[:count], refs[count:]
    levels, total = half_levels(per_dev)
    rank = out_ref.shape[2]
    node_size = 2 * rank
    place = lax.axis_index("rhs")

    def choose(which):
        return jnp.concatenate([value[2 * which], value[2 * which + 1]], axis=1)

    def side(level):
        return (lax.axis_index("leaf") // (1 << level)) % 2

    def columns(ref):
        width = ref.shape[-1]
        return pl.ds(width - rank, rank)

    stacked = cross_pair(cross_levels - 1, inputs)
    half = side(cross_levels - 1)
    for flip, ref in ((0, tail), (1, near_tail)):
        core = (place ^ flip) % CORES
        value[2 * half + core] = dot_rows(stacked, ref[:, :node_size]).astype(jnp.bfloat16)
    incoming = choose(half)
    for level in range(cross_levels - 2, -1, -1):
        packs = cross_packs[2 * CORES * level : 2 * CORES * (level + 1)]
        couplings = [ref[:, columns(ref)] for ref in packs]
        for flip, coupling in zip(PIECES, couplings):
            piece = place ^ flip
            solved = solved_cross[level][piece]
            value[piece] = (solved - dot_rows(incoming, coupling)).astype(jnp.bfloat16)
        incoming = choose(side(level))

    for flip, ref in ((0, keep), (1, keep_near)):
        piece = (place ^ flip) % CORES
        coupling = ref[total, :, columns(ref)]
        value[piece] = (solved_top[piece] - dot_rows(incoming, coupling)).astype(jnp.bfloat16)
    current = [choose(0)]
    for base, count, _ in reversed(levels):
        following = []
        for n in range(count):
            node = base + n
            start = node_size + node * rank
            couplings = (
                keep[node, :, columns(keep)],
                tail[:, start : start + rank],
                keep_near[node, :, columns(keep)],
                near_tail[:, start : start + rank],
            )
            for flip, coupling in zip(PIECES, couplings):
                piece = place ^ flip
                value[piece] = (
                    solved_half[node, piece] - dot_rows(current[n], coupling)
                ).astype(jnp.bfloat16)
            following += [choose(0), choose(1)]
        current = following
    for i, block in enumerate(current):
        out_ref[i] = block


def way_down(per_dev, inputs, solved_cross, solved_top, solved_half, cross_packs, others):
    share, rank = inputs[0].shape[-2:]
    rows = solved_half.shape[3]
    operands = [*inputs, *solved_cross, solved_top, solved_half]
    for packs in cross_packs:
        operands += packs
    operands += others
    return pl.pallas_call(
        functools.partial(down_kernel, per_dev, len(cross_packs) + 1, len(inputs)),
        out_shape=jax.ShapeDtypeStruct((per_dev // 2, share, rank), jnp.bfloat16),
        scratch_shapes=[pltpu.VMEM((2 * CORES, share, rows), jnp.bfloat16)],
        compiler_params=params(18),
        cost_estimate=cost(8 * share * rows * rank * per_dev, 4 * 1024 * 1024),
    )(*operands)


def finish_kernel(far_ref, own_ref, incoming_ref, coupling_ref, out_ref):
    half = own_ref.shape[0]
    high = lax.axis_index("rhs") // CORES
    for values_ref, side in ((far_ref, 1 - high), (own_ref, high)):
        for i in range(half):
            leaf = side * half + i
            incoming = jnp.concatenate(
                [incoming_ref[side * CORES + core, i] for core in range(CORES)], axis=0
            )
            out_ref[leaf] = values_ref[i] - dot_rows(incoming, coupling_ref[leaf])


def finish(far, own, incoming, coupling):
    half, targets, rows = own.shape
    return pl.pallas_call(
        finish_kernel,
        out_shape=jax.ShapeDtypeStruct((2 * half, targets, rows), jnp.float32),
        compiler_params=params(),
        cost_estimate=cost(4 * half * targets * rows * coupling.shape[2], 16 * own.size),
    )(far, own, incoming, coupling)


def swap(block, axis, bit):
    return lax.ppermute(block, axis, [(i, i ^ bit) for i in range(lax.axis_size(axis))])


def far_swap(block, leaf_bit, rhs_bit):
    shares = lax.axis_size("rhs")
    flip = leaf_bit * shares + rhs_bit
    count = lax.axis_size("leaf") * shares
    return lax.ppermute(block, ("leaf", "rhs"), [(i, i ^ flip) for i in range(count)])


def after(value, anchor):
    return lax.optimization_barrier((value, anchor))[0]


def body(
    right_side,
    point_order,
    leaf_inverse,
    leaf_basis,
    leaf_coupling,
    node_inverse,
    node_basis,
    node_coupling,
):
    devices = lax.axis_size("leaf")
    per_dev = leaf_inverse.shape[0]
    node_size = node_inverse.shape[2]
    rank = leaf_basis.shape[2]
    cross_levels = devices.bit_length() - 1
    place = lax.axis_index("rhs")
    high, low = place // CORES, place % CORES

    def rise(carrier, level, anchor, extras=()):
        other = after(swap(carrier, "leaf", 1 << level), anchor)
        width = node_size if level == cross_levels - 2 else carrier.shape[1]
        keep = [width] * (level < cross_levels - 1)
        ancestor, *carriers = climb(level, carrier, other, keep, extras)
        return (ancestor, *(carriers or [None]))

    send, send_coupling, keep, carrier = pack(node_inverse, node_basis, node_coupling)
    across, beside = after(
        [swap(right_side, "rhs", CORES), swap(right_side, "rhs", 1)], send
    )
    points = [across, beside, swap(after(across, beside), "rhs", 1)]
    half_far = swap(send, "rhs", CORES)
    keep_near = swap(after(keep, points), "rhs", 1)
    carrier = after(carrier, points)
    points = [right_side, *points]

    leaves = (point_order, leaf_inverse, leaf_basis)
    far_values, far_same, far_cross, joined = leaf_up(
        jnp.stack([1 - high, low]), points, *leaves
    )
    keep_near = after(keep_near, far_same)
    own_values, own_same, own_cross = leaf_up(
        jnp.stack([high, low]), [after(joined, keep_near)], *leaves
    )
    ancestor, carrier, send_coupling = rise(carrier, 0, own_same, [send_coupling])
    ancestors = [ancestor]
    far_same = after(swap(far_same, "rhs", CORES), own_same)
    far_cross = after(swap(far_cross, "rhs", CORES + 1), own_same)
    parts = [own_same, far_same, swap(own_cross, "rhs", 1), far_cross]
    half_far = after(half_far, (parts, carrier))
    half_near = swap(half_far, "rhs", 1)
    fars = [swap(after(ancestors[0], half_far), "rhs", CORES)]

    solved_half, current = group_up(per_dev, parts, [keep, half_far, keep_near, half_near])
    own_near = swap(join([ancestors[0]], current), "rhs", 1)
    other = swap(current, "rhs", CORES)
    ancestor, carrier = rise(carrier, 1, other)
    ancestors.append(ancestor)
    solved_top, current = half_up(current, after(other, own_near), keep, keep_near)
    fars[0] = after(fars[0], other)
    near_far = swap(fars[0], "rhs", 1)
    cross_packs = [[ancestors[0], fars[0], own_near, near_far]]
    fars.append(swap(join([ancestors[1]], current), "rhs", CORES))
    current = after(current, near_far)
    diagonal = far_swap(current, 1, CORES)
    beside = swap(current, "leaf", 1)
    across = swap(current, "rhs", CORES)
    inputs = [diagonal, beside, across, current]

    solved_cross = []
    for level in range(cross_levels - 1):
        if level > 0:
            own, far = ancestors[level], fars[level]
            own_near = swap(join([own], current), "rhs", 1)
            far_near = swap(join([far], current), "rhs", 1)
            cross_packs.append([own, far, own_near, far_near])
        solved, current = cross_up(level, inputs, cross_packs[level])
        solved_cross.append(solved)
        inputs = [current, swap(current, "leaf", 2 << level)]
        if level == 0:
            for later in range(2, cross_levels):
                ancestor, carrier = rise(carrier, later, current)
                ancestors.append(ancestor)
            for later in range(2, cross_levels - 1):
                fars.append(swap(join([ancestors[later]], current), "rhs", CORES))
            tail = swap(join([ancestors[-1], send_coupling], current), "rhs", CORES)

    tail = hop(cross_levels - 1, ancestors[-1], tail, inputs[1])
    others = [tail, swap(tail, "rhs", 1), keep, keep_near]
    shares = way_down(per_dev, inputs, solved_cross, solved_top, solved_half, cross_packs, others)
    incoming = lax.all_gather(shares, "rhs", axis=0)
    return finish(far_values, own_values, incoming, leaf_coupling)


def solution(mesh):
    placed = (P(None, ("leaf", "rhs")), P("leaf")) + (P("leaf", "rhs", None),) * 6
    return jax.shard_map(
        body, mesh=mesh, in_specs=placed, out_specs=P("leaf", None, "rhs"), check_vma=False
    )
```

```python
import functools

import jax
import jax.numpy as jnp
from jax import lax
from jax.experimental import pallas as pl
from jax.experimental.pallas import tpu as pltpu
from jax.sharding import PartitionSpec as P

LANES = 256
PIECES = (0, 2, 1, 3)
CORES = 2


def params(mebibytes=12):
    return pltpu.CompilerParams(vmem_limit_bytes=mebibytes * 1024 * 1024)


def cost(flops, moved):
    return pl.CostEstimate(flops=flops // 1000, bytes_accessed=moved // 1000, transcendentals=0)


def dot_rows(left, right):
    return lax.dot_general(
        left, right, (((1,), (1,)), ((), ())), preferred_element_type=jnp.float32
    )


def half_levels(per_dev):
    levels = []
    base = 0
    for height in range(1, per_dev.bit_length() - 1):
        node_count = per_dev >> height
        levels.append((base, node_count // 2, per_dev - 2 * node_count))
        base += node_count // 2
    return levels, base


def pack_kernel(per_dev, inverse, basis, coupling, *refs):
    targets, buffers, (sems, out_sems) = refs[:4], refs[4:8], refs[8:]
    factors, couplings, keep, cross = buffers
    levels, total = half_levels(per_dev)
    high = lax.axis_index("rhs") // CORES
    node_size = inverse.shape[2]
    rank = basis.shape[2]
    parts = (
        (inverse, 0, node_size),
        (basis, node_size, rank),
        (coupling, node_size + rank, rank),
    )
    copies = []
    for source, start, width in parts:
        columns = pl.ds(start, width)
        for base, count, offset in levels:
            mine = source.at[pl.ds(offset + high * count, count)]
            other = source.at[pl.ds(offset + (1 - high) * count, count)]
            if source is coupling:
                for n in range(count):
                    sent = couplings.at[:, pl.ds((base + n) * rank, rank)]
                    copies.append((other.at[n], sent))
            else:
                copies.append((other, factors.at[pl.ds(base, count), :, columns]))
            copies.append((mine, keep.at[pl.ds(base, count), :, columns]))
        copies.append((source.at[per_dev - 2], keep.at[total, :, columns]))
        copies.append((source.at[per_dev - 1], cross.at[:, columns]))
    started = []
    for i, (source, target) in enumerate(copies):
        copy = pltpu.make_async_copy(source, target, sems.at[i])
        copy.start()
        started.append(copy)
    for copy in started:
        copy.wait()
    started = []
    for i, (buffer, target) in enumerate(zip(buffers, targets)):
        copy = pltpu.make_async_copy(buffer, target, out_sems.at[i])
        copy.start()
        started.append(copy)
    for copy in started:
        copy.wait()


def pack(inverse, basis, coupling):
    per_dev, rows, node_size = inverse.shape
    rank = basis.shape[2]
    width = node_size + 2 * rank
    levels, total = half_levels(per_dev)
    shapes = [
        (total, rows, node_size + rank),
        (rows, total * rank),
        (total + 1, rows, width),
        (rows, width),
    ]
    return pl.pallas_call(
        functools.partial(pack_kernel, per_dev),
        in_specs=[pl.BlockSpec(memory_space=pl.ANY)] * 3,
        out_specs=[pl.BlockSpec(memory_space=pl.ANY)] * 4,
        out_shape=[jax.ShapeDtypeStruct(shape, inverse.dtype) for shape in shapes],
        scratch_shapes=[pltpu.VMEM(shape, inverse.dtype) for shape in shapes]
        + [pltpu.SemaphoreType.DMA((6 + 5 * len(levels) + total,)), pltpu.SemaphoreType.DMA((4,))],
        compiler_params=params(63),
        cost_estimate=cost(0, 4 * per_dev * rows * width),
    )(inverse, basis, coupling)


def climb_kernel(level, count, mine_ref, other_ref, *refs):
    extras, (ancestor_ref, *outs) = refs[:count], refs[count:]
    carrier_refs, passed = outs[: len(outs) - count], outs[len(outs) - count :]
    for ref, extra in zip(passed, extras):
        ref[...] = extra[...]
    right = (lax.axis_index("leaf") // (1 << level)) % 2 == 1

    @pl.when(right)
    def _():
        ancestor_ref[...] = mine_ref[...]
        for ref in carrier_refs:
            ref[...] = other_ref[:, : ref.shape[1]]

    @pl.when(jnp.logical_not(right))
    def _():
        ancestor_ref[...] = other_ref[...]
        for ref in carrier_refs:
            ref[...] = mine_ref[:, : ref.shape[1]]


def climb(level, mine, other, keep, extras=()):
    return pl.pallas_call(
        functools.partial(climb_kernel, level, len(extras)),
        out_shape=[pltpu.VMEM(mine.shape, mine.dtype)]
        + [pltpu.VMEM((mine.shape[0], size), mine.dtype) for size in keep]
        + [pltpu.VMEM(extra.shape, extra.dtype) for extra in extras],
        compiler_params=params(),
        cost_estimate=cost(0, 4 * mine.size),
    )(mine, other, *extras)


def join_kernel(cuts, *refs):
    *blocks, _, out_ref = refs
    start = 0
    for ref, (first, width) in zip(blocks, cuts):
        out_ref[:, start : start + width] = ref[:, first : first + width]
        start += width


def join(blocks, anchor, cuts=None):
    rows = blocks[0].shape[0]
    cuts = cuts or [(0, block.shape[1]) for block in blocks]
    width = sum(size for _, size in cuts)
    return pl.pallas_call(
        functools.partial(join_kernel, cuts),
        out_shape=pltpu.VMEM((rows, width), blocks[0].dtype),
        compiler_params=params(),
        cost_estimate=cost(0, 4 * rows * width),
    )(*blocks, anchor)


def hop_kernel(level, top_ref, tail_ref, _, out_ref):
    node_size = top_ref.shape[1]
    side = (lax.axis_index("leaf") // (1 << level)) % 2
    here = lax.axis_index("rhs") // CORES == side
    out_ref[:, node_size:] = tail_ref[:, node_size:]

    @pl.when(here)
    def _():
        out_ref[:, :node_size] = top_ref[...]

    @pl.when(jnp.logical_not(here))
    def _():
        out_ref[:, :node_size] = tail_ref[:, :node_size]


def hop(level, top, tail, anchor):
    return pl.pallas_call(
        functools.partial(hop_kernel, level),
        out_shape=pltpu.VMEM(tail.shape, tail.dtype),
        compiler_params=params(),
        cost_estimate=cost(0, 4 * tail.size),
    )(top, tail, anchor)


def leaf_kernel(count, side_ref, *refs):
    points, refs = refs[:count], refs[count:]
    order_ref, inverse_ref, basis_ref, values_ref, same_ref, cross_ref, *rest = refs
    targets = values_ref.shape[1]
    stacked = rest[0] if rest else points[0]
    chunks, pieces = stacked.shape[:2]

    if rest:

        @pl.when(pl.program_id(0) == 0)
        def _():
            place = lax.axis_index("rhs")
            for flip, points_ref in zip(PIECES, points):
                for w in range(pieces):
                    stacked[place ^ flip, w] = points_ref[:, w * LANES : (w + 1) * LANES]

    order = order_ref[...]
    high = order // LANES
    low = order % LANES
    rows = lax.broadcasted_iota(jnp.int32, (LANES, order.shape[1]), 0)
    pick = jnp.where(rows == low, 1.0, 0.0).astype(jnp.bfloat16)
    spread = jnp.dot(
        stacked[...].reshape(-1, LANES), pick, preferred_element_type=jnp.float32
    )
    ordered = jnp.zeros((targets, order.shape[1]), jnp.float32)
    for k in range(chunks * pieces):
        ordered = jnp.where(high == k, spread[k * targets : (k + 1) * targets, :], ordered)
    values = dot_rows(ordered.astype(jnp.bfloat16), inverse_ref[0])
    values_ref[0] = values
    partial = jnp.dot(
        values.astype(jnp.bfloat16), basis_ref[0], preferred_element_type=jnp.float32
    ).astype(jnp.bfloat16)
    share = targets // CORES
    for core in range(CORES):

        @pl.when(side_ref[1] == core)
        def _():
            same_ref[0] = partial[core * share : (core + 1) * share]
            cross_ref[0] = partial[(1 - core) * share : (2 - core) * share]


def leaf_up(side, points, point_order, leaf_inverse, leaf_basis):
    leaves, rows, leaf_size = leaf_inverse.shape
    rank = leaf_basis.shape[2]
    half = leaves // 2
    joined = points[0].ndim == 4
    if joined:
        shape = points[0].shape
    else:
        targets, width = points[0].shape
        shape = (len(points), width // LANES, targets, LANES)
    targets = shape[2]
    share = targets // CORES
    sent = jax.ShapeDtypeStruct((half, share, rank), jnp.bfloat16)
    out_specs = [
        pl.BlockSpec((1, targets, rows), lambda i, side: (i, 0, 0)),
        pl.BlockSpec((1, share, rank), lambda i, side: (i, 0, 0)),
        pl.BlockSpec((1, share, rank), lambda i, side: (i, 0, 0)),
    ]
    out_shape = [jax.ShapeDtypeStruct((half, targets, rows), jnp.float32), sent, sent]
    if not joined:
        out_specs.append(pl.BlockSpec(shape, lambda i, side: (0, 0, 0, 0)))
        out_shape.append(pltpu.VMEM(shape, jnp.bfloat16))
    point_specs = [
        pl.BlockSpec(block.shape, lambda i, side, rank=block.ndim: (0,) * rank) for block in points
    ]
    return pl.pallas_call(
        functools.partial(leaf_kernel, len(points)),
        grid_spec=pltpu.PrefetchScalarGridSpec(
            num_scalar_prefetch=1,
            grid=(half,),
            in_specs=[
                *point_specs,
                pl.BlockSpec((1, leaf_size), lambda i, side: (0, side[0] * half + i)),
                pl.BlockSpec((1, rows, leaf_size), lambda i, side: (side[0] * half + i, 0, 0)),
                pl.BlockSpec((1, rows, rank), lambda i, side: (side[0] * half + i, 0, 0)),
            ],
            out_specs=out_specs,
        ),
        out_shape=out_shape,
        compiler_params=params(),
        cost_estimate=cost(
            leaves * targets * leaf_size * (shape[0] * shape[1] * LANES + 2 * rows),
            leaves * rows * (leaf_size + rank + 3 * targets),
        ),
    )(side, *points, point_order.reshape(1, -1), leaf_inverse, leaf_basis)


def solve_node(stacked, inverses, bases, solved_ref):
    mine = lax.axis_index("rhs")
    total = None
    for flip, inverse, basis in zip(PIECES, inverses, bases):
        solved = dot_rows(stacked, inverse)
        solved_ref[mine ^ flip] = solved
        term = jnp.dot(solved.astype(jnp.bfloat16), basis, preferred_element_type=jnp.float32)
        total = term if total is None else total + term
    return total


def group_up_kernel(per_dev, *refs):
    *refs, solved_ref, out_ref = refs
    parts, packs = refs[: 2 * CORES], refs[2 * CORES :]
    levels, _ = half_levels(per_dev)
    rank = parts[0].shape[2]

    def pieces(node, start, width):
        return [ref[node, :, pl.ds(start, width)] for ref in packs]

    sums = sum(ref[...].astype(jnp.float32) for ref in parts).astype(jnp.bfloat16)
    current = [sums[i] for i in range(sums.shape[0])]
    for base, count, _ in levels:
        following = []
        for n in range(count):
            node = base + n
            compressed = solve_node(
                jnp.concatenate([current[2 * n], current[2 * n + 1]], axis=1),
                pieces(node, 0, 2 * rank),
                pieces(node, 2 * rank, rank),
                solved_ref.at[node],
            )
            following.append(compressed.astype(jnp.bfloat16))
        current = following
    out_ref[...] = current[0]


def group_up(per_dev, parts, packs):
    leaves, share, rank = parts[0].shape
    _, total = half_levels(per_dev)
    _, rows, width = packs[0].shape
    return pl.pallas_call(
        functools.partial(group_up_kernel, per_dev),
        out_shape=[
            jax.ShapeDtypeStruct((total, 2 * CORES, share, rows), jnp.float32),
            jax.ShapeDtypeStruct((share, rank), jnp.bfloat16),
        ],
        compiler_params=params(),
        cost_estimate=cost(24 * total * share * rows * rank, 8 * total * rows * width),
    )(*parts, *packs)


def order_pair(right, mine, other):
    return jnp.concatenate([jnp.where(right, other, mine), jnp.where(right, mine, other)], axis=1)


def half_up_kernel(mine_ref, other_ref, own_ref, near_ref, solved_ref, out_ref):
    rank = mine_ref.shape[1]
    place = lax.axis_index("rhs")
    stacked = order_pair(place // CORES == 1, mine_ref[...], other_ref[...])
    total = 0.0
    for flip, ref in enumerate((own_ref, near_ref)):
        solved = dot_rows(stacked, ref[0, :, : 2 * rank])
        solved_ref[(place ^ flip) % CORES] = solved
        total += jnp.dot(
            solved.astype(jnp.bfloat16),
            ref[0, :, 2 * rank : 3 * rank],
            preferred_element_type=jnp.float32,
        )
    out_ref[...] = total.astype(jnp.bfloat16)


def half_up(mine, other, own, near):
    share, rank = mine.shape
    nodes, rows, width = own.shape
    last = pl.BlockSpec((1, rows, width), lambda i: (nodes - 1, 0, 0))
    whole = pl.BlockSpec((share, rank), lambda i: (0, 0))
    return pl.pallas_call(
        half_up_kernel,
        grid=(1,),
        in_specs=[whole, whole, last, last],
        out_specs=[pl.BlockSpec((CORES, share, rows), lambda i: (0, 0, 0)), whole],
        out_shape=[
            jax.ShapeDtypeStruct((CORES, share, rows), jnp.float32),
            jax.ShapeDtypeStruct((share, rank), jnp.bfloat16),
        ],
        compiler_params=params(),
        cost_estimate=cost(12 * share * rows * rank, 4 * rows * width),
    )(mine, other, own, near)


def total_of(refs):
    if len(refs) == 1:
        return refs[0][...]
    return sum(ref[...].astype(jnp.float32) for ref in refs).astype(jnp.bfloat16)


def cross_pair(level, refs):
    half = len(refs) // 2
    refs = refs[::-1] if half > 1 else refs
    is_right = (lax.axis_index("leaf") // (1 << level)) % 2 == 1
    return order_pair(is_right, total_of(refs[:half]), total_of(refs[half:]))


def cross_up_kernel(level, *refs):
    *refs, solved_ref, out_ref = refs
    inputs, packs = refs[: -2 * CORES], refs[-2 * CORES :]
    rank = out_ref.shape[1]
    compressed = solve_node(
        cross_pair(level, inputs),
        [ref[:, : 2 * rank] for ref in packs],
        [ref[:, 2 * rank : 3 * rank] for ref in packs],
        solved_ref,
    )
    out_ref[...] = compressed.astype(jnp.bfloat16)


def cross_up(level, inputs, packs):
    share, rank = inputs[0].shape[-2:]
    rows, width = packs[0].shape
    return pl.pallas_call(
        functools.partial(cross_up_kernel, level),
        out_shape=[
            jax.ShapeDtypeStruct((2 * CORES, share, rows), jnp.float32),
            jax.ShapeDtypeStruct((share, rank), jnp.bfloat16),
        ],
        compiler_params=params(),
        cost_estimate=cost(24 * share * rows * rank, 8 * rows * width),
    )(*inputs, *packs)


def down_kernel(per_dev, cross_levels, input_count, *refs):
    *refs, out_ref, value = refs
    inputs, refs = refs[:input_count], refs[input_count:]
    solved_cross, refs = refs[: cross_levels - 1], refs[cross_levels - 1 :]
    solved_top, solved_half, refs = refs[0], refs[1], refs[2:]
    count = 2 * CORES * (cross_levels - 1)
    cross_packs, (both, keep, keep_near) = refs[:count], refs[count:]
    levels, total = half_levels(per_dev)
    rank = out_ref.shape[2]
    node_size = 2 * rank
    place = lax.axis_index("rhs")
    tail, near_tail = both.at[place % CORES], both.at[(place + 1) % CORES]

    def choose(which):
        return jnp.concatenate([value[2 * which], value[2 * which + 1]], axis=1)

    def side(level):
        return (lax.axis_index("leaf") // (1 << level)) % 2

    def columns(ref):
        width = ref.shape[-1]
        return pl.ds(width - rank, rank)

    stacked = cross_pair(cross_levels - 1, inputs)
    half = side(cross_levels - 1)
    for flip, ref in ((0, tail), (1, near_tail)):
        core = (place ^ flip) % CORES
        value[2 * half + core] = dot_rows(stacked, ref[:, :node_size]).astype(jnp.bfloat16)
    incoming = choose(half)
    for level in range(cross_levels - 2, -1, -1):
        packs = cross_packs[2 * CORES * level : 2 * CORES * (level + 1)]
        couplings = [ref[:, columns(ref)] for ref in packs]
        for flip, coupling in zip(PIECES, couplings):
            piece = place ^ flip
            solved = solved_cross[level][piece]
            value[piece] = (solved - dot_rows(incoming, coupling)).astype(jnp.bfloat16)
        incoming = choose(side(level))

    for flip, ref in ((0, keep), (1, keep_near)):
        piece = (place ^ flip) % CORES
        coupling = ref[total, :, columns(ref)]
        value[piece] = (solved_top[piece] - dot_rows(incoming, coupling)).astype(jnp.bfloat16)
    current = [choose(0)]
    for base, count, _ in reversed(levels):
        following = []
        for n in range(count):
            node = base + n
            start = node_size + node * rank
            couplings = (
                keep[node, :, columns(keep)],
                tail[:, start : start + rank],
                keep_near[node, :, columns(keep)],
                near_tail[:, start : start + rank],
            )
            for flip, coupling in zip(PIECES, couplings):
                piece = place ^ flip
                value[piece] = (
                    solved_half[node, piece] - dot_rows(current[n], coupling)
                ).astype(jnp.bfloat16)
            following += [choose(0), choose(1)]
        current = following
    for i, block in enumerate(current):
        out_ref[i] = block


def way_down(per_dev, inputs, solved_cross, solved_top, solved_half, cross_packs, others):
    share, rank = inputs[0].shape[-2:]
    rows = solved_half.shape[3]
    operands = [*inputs, *solved_cross, solved_top, solved_half]
    for packs in cross_packs:
        operands += packs
    operands += others
    return pl.pallas_call(
        functools.partial(down_kernel, per_dev, len(cross_packs) + 1, len(inputs)),
        out_shape=jax.ShapeDtypeStruct((per_dev // 2, share, rank), jnp.bfloat16),
        scratch_shapes=[pltpu.VMEM((2 * CORES, share, rows), jnp.bfloat16)],
        compiler_params=params(18),
        cost_estimate=cost(8 * share * rows * rank * per_dev, 4 * 1024 * 1024),
    )(*operands)


def finish_kernel(far_ref, own_ref, incoming_ref, coupling_ref, out_ref):
    half = own_ref.shape[0]
    high = lax.axis_index("rhs") // CORES
    for values_ref, side in ((far_ref, 1 - high), (own_ref, high)):
        for i in range(half):
            leaf = side * half + i
            incoming = jnp.concatenate(
                [incoming_ref[side * CORES + core, i] for core in range(CORES)], axis=0
            )
            out_ref[leaf] = values_ref[i] - dot_rows(incoming, coupling_ref[leaf])


def finish(far, own, incoming, coupling):
    half, targets, rows = own.shape
    return pl.pallas_call(
        finish_kernel,
        out_shape=jax.ShapeDtypeStruct((2 * half, targets, rows), jnp.float32),
        compiler_params=params(),
        cost_estimate=cost(4 * half * targets * rows * coupling.shape[2], 16 * own.size),
    )(far, own, incoming, coupling)


def swap(block, axis, bit):
    return lax.ppermute(block, axis, [(i, i ^ bit) for i in range(lax.axis_size(axis))])


def far_swap(block, leaf_bit, rhs_bit):
    shares = lax.axis_size("rhs")
    flip = leaf_bit * shares + rhs_bit
    count = lax.axis_size("leaf") * shares
    return lax.ppermute(block, ("leaf", "rhs"), [(i, i ^ flip) for i in range(count)])


def after(value, anchor):
    return lax.optimization_barrier((value, anchor))[0]


def body(
    right_side,
    point_order,
    leaf_inverse,
    leaf_basis,
    leaf_coupling,
    node_inverse,
    node_basis,
    node_coupling,
):
    devices = lax.axis_size("leaf")
    per_dev = leaf_inverse.shape[0]
    node_size = node_inverse.shape[2]
    rank = leaf_basis.shape[2]
    cross_levels = devices.bit_length() - 1
    place = lax.axis_index("rhs")
    high, low = place // CORES, place % CORES

    def rise(carrier, level, anchor, extras=()):
        other = after(swap(carrier, "leaf", 1 << level), anchor)
        width = node_size if level == cross_levels - 2 else carrier.shape[1]
        keep = [width] * (level < cross_levels - 1)
        ancestor, *carriers = climb(level, carrier, other, keep, extras)
        return (ancestor, *(carriers or [None]))

    send, send_coupling, keep, carrier = pack(node_inverse, node_basis, node_coupling)
    across, beside = after(
        [swap(right_side, "rhs", CORES), swap(right_side, "rhs", 1)], send
    )
    points = [across, beside, swap(after(across, beside), "rhs", 1)]
    half_far = swap(send, "rhs", CORES)
    keep_near = swap(after(keep, points), "rhs", 1)
    carrier = after(carrier, points)
    points = [right_side, *points]

    leaves = (point_order, leaf_inverse, leaf_basis)
    far_values, far_same, far_cross, joined = leaf_up(
        jnp.stack([1 - high, low]), points, *leaves
    )
    keep_near = after(keep_near, far_same)
    own_values, own_same, own_cross = leaf_up(
        jnp.stack([high, low]), [after(joined, keep_near)], *leaves
    )
    ancestor, carrier, send_coupling = rise(carrier, 0, own_same, [send_coupling])
    ancestors = [ancestor]
    far_same = after(swap(far_same, "rhs", CORES), own_same)
    far_cross = after(swap(far_cross, "rhs", CORES + 1), own_same)
    parts = [own_same, far_same, swap(own_cross, "rhs", 1), far_cross]
    half_far = after(half_far, (parts, carrier))
    half_near = swap(half_far, "rhs", 1)
    fars = [swap(after(ancestors[0], half_far), "rhs", CORES)]

    solved_half, current = group_up(per_dev, parts, [keep, half_far, keep_near, half_near])
    own_near = swap(join([ancestors[0]], current), "rhs", 1)
    other = swap(current, "rhs", CORES)
    ancestor, carrier = rise(carrier, 1, other)
    ancestors.append(ancestor)
    solved_top, current = half_up(current, after(other, own_near), keep, keep_near)
    fars[0] = after(fars[0], other)
    near_far = swap(fars[0], "rhs", 1)
    cross_packs = [[ancestors[0], fars[0], own_near, near_far]]
    fars.append(swap(join([ancestors[1]], current), "rhs", CORES))
    current = after(current, near_far)
    diagonal = far_swap(current, 1, CORES)
    beside = swap(current, "leaf", 1)
    across = swap(current, "rhs", CORES)
    inputs = [diagonal, beside, across, current]

    solved_cross = []
    for level in range(cross_levels - 1):
        if level > 0:
            own, far = ancestors[level], fars[level]
            own_near = swap(join([own], current), "rhs", 1)
            far_near = swap(join([far], current), "rhs", 1)
            cross_packs.append([own, far, own_near, far_near])
        solved, current = cross_up(level, inputs, cross_packs[level])
        solved_cross.append(solved)
        inputs = [current, swap(current, "leaf", 2 << level)]
        if level == 0:
            for later in range(2, cross_levels):
                ancestor, carrier = rise(carrier, later, current)
                ancestors.append(ancestor)
            for later in range(2, cross_levels - 1):
                fars.append(swap(join([ancestors[later]], current), "rhs", CORES))
            tail = swap(join([ancestors[-1], send_coupling], current), "rhs", CORES)

    tail = hop(cross_levels - 1, ancestors[-1], tail, current)
    shares = lax.axis_size("rhs")
    cores = [[i + core for core in range(CORES)] for i in range(0, shares, CORES)]
    both = lax.all_gather(tail, "rhs", axis_index_groups=cores)
    others = [both, keep, keep_near]
    shares = way_down(per_dev, inputs, solved_cross, solved_top, solved_half, cross_packs, others)
    incoming = lax.all_gather(shares, "rhs", axis=0)
    return finish(far_values, own_values, incoming, leaf_coupling)


def solution(mesh):
    placed = (P(None, ("leaf", "rhs")), P("leaf")) + (P("leaf", "rhs", None),) * 6
    return jax.shard_map(
        body, mesh=mesh, in_specs=placed, out_specs=P("leaf", None, "rhs"), check_vma=False
    )
```

```python
import functools

import jax
import jax.numpy as jnp
from jax import lax
from jax.experimental import pallas as pl
from jax.experimental.pallas import tpu as pltpu
from jax.sharding import PartitionSpec as P

LANES = 256
PIECES = (0, 2, 1, 3)
CORES = 2


def params(mebibytes=12):
    return pltpu.CompilerParams(vmem_limit_bytes=mebibytes * 1024 * 1024)


def cost(flops, moved):
    return pl.CostEstimate(flops=flops // 1000, bytes_accessed=moved // 1000, transcendentals=0)


def dot_rows(left, right):
    return lax.dot_general(
        left, right, (((1,), (1,)), ((), ())), preferred_element_type=jnp.float32
    )


def half_levels(per_dev):
    levels = []
    base = 0
    for height in range(1, per_dev.bit_length() - 1):
        node_count = per_dev >> height
        levels.append((base, node_count // 2, per_dev - 2 * node_count))
        base += node_count // 2
    return levels, base


def pack_kernel(per_dev, inverse, basis, coupling, *refs):
    targets, buffers, (sems, out_sems) = refs[:4], refs[4:8], refs[8:]
    factors, couplings, keep, cross = buffers
    levels, total = half_levels(per_dev)
    high = lax.axis_index("rhs") // CORES
    node_size = inverse.shape[2]
    rank = basis.shape[2]
    parts = (
        (inverse, 0, node_size),
        (basis, node_size, rank),
        (coupling, node_size + rank, rank),
    )
    copies = []
    for source, start, width in parts:
        columns = pl.ds(start, width)
        for base, count, offset in levels:
            mine = source.at[pl.ds(offset + high * count, count)]
            other = source.at[pl.ds(offset + (1 - high) * count, count)]
            if source is coupling:
                for n in range(count):
                    sent = couplings.at[:, pl.ds((base + n) * rank, rank)]
                    copies.append((other.at[n], sent))
            else:
                copies.append((other, factors.at[pl.ds(base, count), :, columns]))
            copies.append((mine, keep.at[pl.ds(base, count), :, columns]))
        copies.append((source.at[per_dev - 2], keep.at[total, :, columns]))
        copies.append((source.at[per_dev - 1], cross.at[:, columns]))
    started = []
    for i, (source, target) in enumerate(copies):
        copy = pltpu.make_async_copy(source, target, sems.at[i])
        copy.start()
        started.append(copy)
    for copy in started:
        copy.wait()
    started = []
    for i, (buffer, target) in enumerate(zip(buffers, targets)):
        copy = pltpu.make_async_copy(buffer, target, out_sems.at[i])
        copy.start()
        started.append(copy)
    for copy in started:
        copy.wait()


def pack(inverse, basis, coupling):
    per_dev, rows, node_size = inverse.shape
    rank = basis.shape[2]
    width = node_size + 2 * rank
    levels, total = half_levels(per_dev)
    shapes = [
        (total, rows, node_size + rank),
        (rows, total * rank),
        (total + 1, rows, width),
        (rows, width),
    ]
    return pl.pallas_call(
        functools.partial(pack_kernel, per_dev),
        in_specs=[pl.BlockSpec(memory_space=pl.ANY)] * 3,
        out_specs=[pl.BlockSpec(memory_space=pl.ANY)] * 4,
        out_shape=[jax.ShapeDtypeStruct(shape, inverse.dtype) for shape in shapes],
        scratch_shapes=[pltpu.VMEM(shape, inverse.dtype) for shape in shapes]
        + [pltpu.SemaphoreType.DMA((6 + 5 * len(levels) + total,)), pltpu.SemaphoreType.DMA((4,))],
        compiler_params=params(63),
        cost_estimate=cost(0, 4 * per_dev * rows * width),
    )(inverse, basis, coupling)


def climb_kernel(level, count, mine_ref, other_ref, *refs):
    extras, (ancestor_ref, *outs) = refs[:count], refs[count:]
    carrier_refs, passed = outs[: len(outs) - count], outs[len(outs) - count :]
    for ref, extra in zip(passed, extras):
        ref[...] = extra[...]
    right = (lax.axis_index("leaf") // (1 << level)) % 2 == 1

    @pl.when(right)
    def _():
        ancestor_ref[...] = mine_ref[...]
        for ref in carrier_refs:
            ref[...] = other_ref[:, : ref.shape[1]]

    @pl.when(jnp.logical_not(right))
    def _():
        ancestor_ref[...] = other_ref[...]
        for ref in carrier_refs:
            ref[...] = mine_ref[:, : ref.shape[1]]


def climb(level, mine, other, keep, extras=()):
    return pl.pallas_call(
        functools.partial(climb_kernel, level, len(extras)),
        out_shape=[pltpu.VMEM(mine.shape, mine.dtype)]
        + [pltpu.VMEM((mine.shape[0], size), mine.dtype) for size in keep]
        + [pltpu.VMEM(extra.shape, extra.dtype) for extra in extras],
        compiler_params=params(),
        cost_estimate=cost(0, 4 * mine.size),
    )(mine, other, *extras)


def join_kernel(cuts, *refs):
    *blocks, _, out_ref = refs
    start = 0
    for ref, (first, width) in zip(blocks, cuts):
        out_ref[:, start : start + width] = ref[:, first : first + width]
        start += width


def join(blocks, anchor, cuts=None):
    rows = blocks[0].shape[0]
    cuts = cuts or [(0, block.shape[1]) for block in blocks]
    width = sum(size for _, size in cuts)
    return pl.pallas_call(
        functools.partial(join_kernel, cuts),
        out_shape=pltpu.VMEM((rows, width), blocks[0].dtype),
        compiler_params=params(),
        cost_estimate=cost(0, 4 * rows * width),
    )(*blocks, anchor)


def hop_kernel(level, top_ref, tail_ref, _, out_ref):
    node_size = top_ref.shape[1]
    side = (lax.axis_index("leaf") // (1 << level)) % 2
    here = lax.axis_index("rhs") // CORES == side
    out_ref[:, node_size:] = tail_ref[:, node_size:]

    @pl.when(here)
    def _():
        out_ref[:, :node_size] = top_ref[...]

    @pl.when(jnp.logical_not(here))
    def _():
        out_ref[:, :node_size] = tail_ref[:, :node_size]


def hop(level, top, tail, anchor):
    return pl.pallas_call(
        functools.partial(hop_kernel, level),
        out_shape=pltpu.VMEM(tail.shape, tail.dtype),
        compiler_params=params(),
        cost_estimate=cost(0, 4 * tail.size),
    )(top, tail, anchor)


def leaf_kernel(count, side_ref, *refs):
    points, refs = refs[:count], refs[count:]
    order_ref, inverse_ref, basis_ref, values_ref, same_ref, cross_ref, *rest = refs
    targets = values_ref.shape[1]
    stacked = rest[0] if rest else points[0]
    chunks, pieces = stacked.shape[:2]

    if rest:

        @pl.when(pl.program_id(0) == 0)
        def _():
            place = lax.axis_index("rhs")
            for flip, points_ref in zip(PIECES, points):
                for w in range(pieces):
                    stacked[place ^ flip, w] = points_ref[:, w * LANES : (w + 1) * LANES]

    order = order_ref[...]
    high = order // LANES
    low = order % LANES
    rows = lax.broadcasted_iota(jnp.int32, (LANES, order.shape[1]), 0)
    pick = jnp.where(rows == low, 1.0, 0.0).astype(jnp.bfloat16)
    spread = jnp.dot(
        stacked[...].reshape(-1, LANES), pick, preferred_element_type=jnp.float32
    )
    ordered = jnp.zeros((targets, order.shape[1]), jnp.float32)
    for k in range(chunks * pieces):
        ordered = jnp.where(high == k, spread[k * targets : (k + 1) * targets, :], ordered)
    values = dot_rows(ordered.astype(jnp.bfloat16), inverse_ref[0])
    values_ref[0] = values
    partial = jnp.dot(
        values.astype(jnp.bfloat16), basis_ref[0], preferred_element_type=jnp.float32
    ).astype(jnp.bfloat16)
    share = targets // CORES
    for core in range(CORES):

        @pl.when(side_ref[1] == core)
        def _():
            same_ref[0] = partial[core * share : (core + 1) * share]
            cross_ref[0] = partial[(1 - core) * share : (2 - core) * share]


def leaf_up(side, points, point_order, leaf_inverse, leaf_basis):
    leaves, rows, leaf_size = leaf_inverse.shape
    rank = leaf_basis.shape[2]
    half = leaves // 2
    joined = points[0].ndim == 4
    if joined:
        shape = points[0].shape
    else:
        targets, width = points[0].shape
        shape = (len(points), width // LANES, targets, LANES)
    targets = shape[2]
    share = targets // CORES
    sent = jax.ShapeDtypeStruct((half, share, rank), jnp.bfloat16)
    out_specs = [
        pl.BlockSpec((1, targets, rows), lambda i, side: (i, 0, 0)),
        pl.BlockSpec((1, share, rank), lambda i, side: (i, 0, 0)),
        pl.BlockSpec((1, share, rank), lambda i, side: (i, 0, 0)),
    ]
    out_shape = [jax.ShapeDtypeStruct((half, targets, rows), jnp.float32), sent, sent]
    if not joined:
        out_specs.append(pl.BlockSpec(shape, lambda i, side: (0, 0, 0, 0)))
        out_shape.append(pltpu.VMEM(shape, jnp.bfloat16))
    point_specs = [
        pl.BlockSpec(block.shape, lambda i, side, rank=block.ndim: (0,) * rank) for block in points
    ]
    return pl.pallas_call(
        functools.partial(leaf_kernel, len(points)),
        grid_spec=pltpu.PrefetchScalarGridSpec(
            num_scalar_prefetch=1,
            grid=(half,),
            in_specs=[
                *point_specs,
                pl.BlockSpec((1, leaf_size), lambda i, side: (0, side[0] * half + i)),
                pl.BlockSpec((1, rows, leaf_size), lambda i, side: (side[0] * half + i, 0, 0)),
                pl.BlockSpec((1, rows, rank), lambda i, side: (side[0] * half + i, 0, 0)),
            ],
            out_specs=out_specs,
        ),
        out_shape=out_shape,
        compiler_params=params(),
        cost_estimate=cost(
            leaves * targets * leaf_size * (shape[0] * shape[1] * LANES + 2 * rows),
            leaves * rows * (leaf_size + rank + 3 * targets),
        ),
    )(side, *points, point_order.reshape(1, -1), leaf_inverse, leaf_basis)


def solve_node(stacked, inverses, bases, solved_ref):
    mine = lax.axis_index("rhs")
    total = None
    for flip, inverse, basis in zip(PIECES, inverses, bases):
        solved = dot_rows(stacked, inverse)
        solved_ref[mine ^ flip] = solved
        term = jnp.dot(solved.astype(jnp.bfloat16), basis, preferred_element_type=jnp.float32)
        total = term if total is None else total + term
    return total


def group_up_kernel(per_dev, *refs):
    *refs, solved_ref, out_ref = refs
    parts, packs = refs[: 2 * CORES], refs[2 * CORES :]
    levels, _ = half_levels(per_dev)
    rank = parts[0].shape[2]

    def pieces(node, start, width):
        return [ref[node, :, pl.ds(start, width)] for ref in packs]

    sums = sum(ref[...].astype(jnp.float32) for ref in parts).astype(jnp.bfloat16)
    current = [sums[i] for i in range(sums.shape[0])]
    for base, count, _ in levels:
        following = []
        for n in range(count):
            node = base + n
            compressed = solve_node(
                jnp.concatenate([current[2 * n], current[2 * n + 1]], axis=1),
                pieces(node, 0, 2 * rank),
                pieces(node, 2 * rank, rank),
                solved_ref.at[node],
            )
            following.append(compressed.astype(jnp.bfloat16))
        current = following
    out_ref[...] = current[0]


def group_up(per_dev, parts, packs):
    leaves, share, rank = parts[0].shape
    _, total = half_levels(per_dev)
    _, rows, width = packs[0].shape
    return pl.pallas_call(
        functools.partial(group_up_kernel, per_dev),
        out_shape=[
            jax.ShapeDtypeStruct((total, 2 * CORES, share, rows), jnp.float32),
            jax.ShapeDtypeStruct((share, rank), jnp.bfloat16),
        ],
        compiler_params=params(),
        cost_estimate=cost(24 * total * share * rows * rank, 8 * total * rows * width),
    )(*parts, *packs)


def order_pair(right, mine, other):
    return jnp.concatenate([jnp.where(right, other, mine), jnp.where(right, mine, other)], axis=1)


def half_up_kernel(mine_ref, other_ref, own_ref, near_ref, solved_ref, out_ref):
    rank = mine_ref.shape[1]
    place = lax.axis_index("rhs")
    stacked = order_pair(place // CORES == 1, mine_ref[...], other_ref[...])
    total = 0.0
    for flip, ref in enumerate((own_ref, near_ref)):
        solved = dot_rows(stacked, ref[0, :, : 2 * rank])
        solved_ref[(place ^ flip) % CORES] = solved
        total += jnp.dot(
            solved.astype(jnp.bfloat16),
            ref[0, :, 2 * rank : 3 * rank],
            preferred_element_type=jnp.float32,
        )
    out_ref[...] = total.astype(jnp.bfloat16)


def half_up(mine, other, own, near):
    share, rank = mine.shape
    nodes, rows, width = own.shape
    last = pl.BlockSpec((1, rows, width), lambda i: (nodes - 1, 0, 0))
    whole = pl.BlockSpec((share, rank), lambda i: (0, 0))
    return pl.pallas_call(
        half_up_kernel,
        grid=(1,),
        in_specs=[whole, whole, last, last],
        out_specs=[pl.BlockSpec((CORES, share, rows), lambda i: (0, 0, 0)), whole],
        out_shape=[
            jax.ShapeDtypeStruct((CORES, share, rows), jnp.float32),
            jax.ShapeDtypeStruct((share, rank), jnp.bfloat16),
        ],
        compiler_params=params(),
        cost_estimate=cost(12 * share * rows * rank, 4 * rows * width),
    )(mine, other, own, near)


def total_of(refs):
    if len(refs) == 1:
        return refs[0][...]
    return sum(ref[...].astype(jnp.float32) for ref in refs).astype(jnp.bfloat16)


def cross_pair(level, refs):
    half = len(refs) // 2
    refs = refs[::-1] if half > 1 else refs
    is_right = (lax.axis_index("leaf") // (1 << level)) % 2 == 1
    return order_pair(is_right, total_of(refs[:half]), total_of(refs[half:]))


def cross_up_kernel(level, *refs):
    *refs, solved_ref, out_ref = refs
    inputs, packs = refs[: -2 * CORES], refs[-2 * CORES :]
    rank = out_ref.shape[1]
    compressed = solve_node(
        cross_pair(level, inputs),
        [ref[:, : 2 * rank] for ref in packs],
        [ref[:, 2 * rank : 3 * rank] for ref in packs],
        solved_ref,
    )
    out_ref[...] = compressed.astype(jnp.bfloat16)


def cross_up(level, inputs, packs):
    share, rank = inputs[0].shape[-2:]
    rows, width = packs[0].shape
    return pl.pallas_call(
        functools.partial(cross_up_kernel, level),
        out_shape=[
            jax.ShapeDtypeStruct((2 * CORES, share, rows), jnp.float32),
            jax.ShapeDtypeStruct((share, rank), jnp.bfloat16),
        ],
        compiler_params=params(),
        cost_estimate=cost(24 * share * rows * rank, 8 * rows * width),
    )(*inputs, *packs)


def down_kernel(per_dev, cross_levels, input_count, *refs):
    *refs, out_ref, value = refs
    inputs, refs = refs[:input_count], refs[input_count:]
    solved_cross, refs = refs[: cross_levels - 1], refs[cross_levels - 1 :]
    solved_top, solved_half, refs = refs[0], refs[1], refs[2:]
    count = 2 * CORES * (cross_levels - 1)
    cross_packs, (both, keep, keep_near) = refs[:count], refs[count:]
    levels, total = half_levels(per_dev)
    rank = out_ref.shape[2]
    node_size = 2 * rank
    place = lax.axis_index("rhs")
    tail, near_tail = both.at[place % CORES], both.at[(place + 1) % CORES]

    def choose(which):
        return jnp.concatenate([value[2 * which], value[2 * which + 1]], axis=1)

    def side(level):
        return (lax.axis_index("leaf") // (1 << level)) % 2

    def columns(ref):
        width = ref.shape[-1]
        return pl.ds(width - rank, rank)

    stacked = cross_pair(cross_levels - 1, inputs)
    half = side(cross_levels - 1)
    for flip, ref in ((0, tail), (1, near_tail)):
        core = (place ^ flip) % CORES
        value[2 * half + core] = dot_rows(stacked, ref[:, :node_size]).astype(jnp.bfloat16)
    incoming = choose(half)
    for level in range(cross_levels - 2, -1, -1):
        packs = cross_packs[2 * CORES * level : 2 * CORES * (level + 1)]
        couplings = [ref[:, columns(ref)] for ref in packs]
        for flip, coupling in zip(PIECES, couplings):
            piece = place ^ flip
            solved = solved_cross[level][piece]
            value[piece] = (solved - dot_rows(incoming, coupling)).astype(jnp.bfloat16)
        incoming = choose(side(level))

    for flip, ref in ((0, keep), (1, keep_near)):
        piece = (place ^ flip) % CORES
        coupling = ref[total, :, columns(ref)]
        value[piece] = (solved_top[piece] - dot_rows(incoming, coupling)).astype(jnp.bfloat16)
    current = [choose(0)]
    for base, count, _ in reversed(levels):
        following = []
        for n in range(count):
            node = base + n
            start = node_size + node * rank
            couplings = (
                keep[node, :, columns(keep)],
                tail[:, start : start + rank],
                keep_near[node, :, columns(keep)],
                near_tail[:, start : start + rank],
            )
            for flip, coupling in zip(PIECES, couplings):
                piece = place ^ flip
                value[piece] = (
                    solved_half[node, piece] - dot_rows(current[n], coupling)
                ).astype(jnp.bfloat16)
            following += [choose(0), choose(1)]
        current = following
    for i, block in enumerate(current):
        out_ref[i] = block


def way_down(per_dev, inputs, solved_cross, solved_top, solved_half, cross_packs, others):
    share, rank = inputs[0].shape[-2:]
    rows = solved_half.shape[3]
    operands = [*inputs, *solved_cross, solved_top, solved_half]
    for packs in cross_packs:
        operands += packs
    operands += others
    return pl.pallas_call(
        functools.partial(down_kernel, per_dev, len(cross_packs) + 1, len(inputs)),
        out_shape=jax.ShapeDtypeStruct((per_dev // 2, share, rank), jnp.bfloat16),
        scratch_shapes=[pltpu.VMEM((2 * CORES, share, rows), jnp.bfloat16)],
        compiler_params=params(18),
        cost_estimate=cost(8 * share * rows * rank * per_dev, 4 * 1024 * 1024),
    )(*operands)


def finish_kernel(far_ref, own_ref, incoming_ref, coupling_ref, out_ref, results, sems):
    half = own_ref.shape[0]
    high = lax.axis_index("rhs") // CORES
    started = []
    for part, (values_ref, side) in enumerate(((own_ref, high), (far_ref, 1 - high))):
        for i in range(half):
            leaf = side * half + i
            slot = part * half + i
            incoming = jnp.concatenate(
                [incoming_ref[side * CORES + core, i] for core in range(CORES)], axis=0
            )
            results[slot] = values_ref[i] - dot_rows(incoming, coupling_ref[leaf])
            copy = pltpu.make_async_copy(results.at[slot], out_ref.at[leaf], sems.at[slot])
            copy.start()
            started.append(copy)
    for copy in started:
        copy.wait()


def finish(far, own, incoming, coupling):
    half, targets, rows = own.shape
    shape = (2 * half, targets, rows)
    vmem = pl.BlockSpec(memory_space=pltpu.VMEM)
    return pl.pallas_call(
        finish_kernel,
        in_specs=[vmem] * 4,
        out_specs=pl.BlockSpec(memory_space=pl.ANY),
        out_shape=jax.ShapeDtypeStruct(shape, jnp.float32),
        scratch_shapes=[pltpu.VMEM(shape, jnp.float32), pltpu.SemaphoreType.DMA((2 * half,))],
        compiler_params=params(),
        cost_estimate=cost(4 * half * targets * rows * coupling.shape[2], 16 * own.size),
    )(far, own, incoming, coupling)


def swap(block, axis, bit):
    return lax.ppermute(block, axis, [(i, i ^ bit) for i in range(lax.axis_size(axis))])


def far_swap(block, leaf_bit, rhs_bit):
    shares = lax.axis_size("rhs")
    flip = leaf_bit * shares + rhs_bit
    count = lax.axis_size("leaf") * shares
    return lax.ppermute(block, ("leaf", "rhs"), [(i, i ^ flip) for i in range(count)])


def after(value, anchor):
    return lax.optimization_barrier((value, anchor))[0]


def body(
    right_side,
    point_order,
    leaf_inverse,
    leaf_basis,
    leaf_coupling,
    node_inverse,
    node_basis,
    node_coupling,
):
    devices = lax.axis_size("leaf")
    per_dev = leaf_inverse.shape[0]
    node_size = node_inverse.shape[2]
    rank = leaf_basis.shape[2]
    cross_levels = devices.bit_length() - 1
    place = lax.axis_index("rhs")
    high, low = place // CORES, place % CORES

    def rise(carrier, level, anchor, extras=()):
        other = after(swap(carrier, "leaf", 1 << level), anchor)
        width = node_size if level == cross_levels - 2 else carrier.shape[1]
        keep = [width] * (level < cross_levels - 1)
        ancestor, *carriers = climb(level, carrier, other, keep, extras)
        return (ancestor, *(carriers or [None]))

    send, send_coupling, keep, carrier = pack(node_inverse, node_basis, node_coupling)
    across, beside = after(
        [swap(right_side, "rhs", CORES), swap(right_side, "rhs", 1)], send
    )
    points = [across, beside, swap(after(across, beside), "rhs", 1)]
    half_far = swap(send, "rhs", CORES)
    keep_near = swap(after(keep, points), "rhs", 1)
    carrier = after(carrier, points)
    points = [right_side, *points]

    leaves = (point_order, leaf_inverse, leaf_basis)
    far_values, far_same, far_cross, joined = leaf_up(
        jnp.stack([1 - high, low]), points, *leaves
    )
    keep_near = after(keep_near, far_same)
    own_values, own_same, own_cross = leaf_up(
        jnp.stack([high, low]), [after(joined, keep_near)], *leaves
    )
    ancestor, carrier, send_coupling = rise(carrier, 0, own_same, [send_coupling])
    ancestors = [ancestor]
    far_same = after(swap(far_same, "rhs", CORES), own_same)
    far_cross = after(swap(far_cross, "rhs", CORES + 1), own_same)
    parts = [own_same, far_same, swap(own_cross, "rhs", 1), far_cross]
    half_far = after(half_far, (parts, carrier))
    half_near = swap(half_far, "rhs", 1)
    fars = [swap(after(ancestors[0], half_far), "rhs", CORES)]

    solved_half, current = group_up(per_dev, parts, [keep, half_far, keep_near, half_near])
    own_near = swap(join([ancestors[0]], current), "rhs", 1)
    other = swap(current, "rhs", CORES)
    ancestor, carrier = rise(carrier, 1, other)
    ancestors.append(ancestor)
    solved_top, current = half_up(current, after(other, own_near), keep, keep_near)
    fars[0] = after(fars[0], other)
    near_far = swap(fars[0], "rhs", 1)
    cross_packs = [[ancestors[0], fars[0], own_near, near_far]]
    fars.append(swap(join([ancestors[1]], current), "rhs", CORES))
    current = after(current, near_far)
    diagonal = far_swap(current, 1, CORES)
    beside = swap(current, "leaf", 1)
    across = swap(current, "rhs", CORES)
    inputs = [diagonal, beside, across, current]

    solved_cross = []
    for level in range(cross_levels - 1):
        if level > 0:
            own, far = ancestors[level], fars[level]
            own_near = swap(join([own], current), "rhs", 1)
            far_near = swap(join([far], current), "rhs", 1)
            cross_packs.append([own, far, own_near, far_near])
        solved, current = cross_up(level, inputs, cross_packs[level])
        solved_cross.append(solved)
        inputs = [current, swap(current, "leaf", 2 << level)]
        if level == 0:
            for later in range(2, cross_levels):
                ancestor, carrier = rise(carrier, later, current)
                ancestors.append(ancestor)
            for later in range(2, cross_levels - 1):
                fars.append(swap(join([ancestors[later]], current), "rhs", CORES))
            tail = swap(join([ancestors[-1], send_coupling], current), "rhs", CORES)

    tail = hop(cross_levels - 1, ancestors[-1], tail, current)
    shares = lax.axis_size("rhs")
    cores = [[i + core for core in range(CORES)] for i in range(0, shares, CORES)]
    both = lax.all_gather(tail, "rhs", axis_index_groups=cores)
    others = [both, keep, keep_near]
    shares = way_down(per_dev, inputs, solved_cross, solved_top, solved_half, cross_packs, others)
    incoming = lax.all_gather(shares, "rhs", axis=0)
    return finish(far_values, own_values, incoming, leaf_coupling)


def solution(mesh):
    placed = (P(None, ("leaf", "rhs")), P("leaf")) + (P("leaf", "rhs", None),) * 6
    return jax.shard_map(
        body, mesh=mesh, in_specs=placed, out_specs=P("leaf", None, "rhs"), check_vma=False
    )
```

```python
import functools

import jax
import jax.numpy as jnp
from jax import lax
from jax.experimental import pallas as pl
from jax.experimental.pallas import tpu as pltpu
from jax.sharding import PartitionSpec as P

LANES = 256
PIECES = (0, 2, 1, 3)
CORES = 2


def params(mebibytes=12):
    return pltpu.CompilerParams(vmem_limit_bytes=mebibytes * 1024 * 1024)


def cost(flops, moved):
    return pl.CostEstimate(flops=flops // 1000, bytes_accessed=moved // 1000, transcendentals=0)


def dot_rows(left, right):
    return lax.dot_general(
        left, right, (((1,), (1,)), ((), ())), preferred_element_type=jnp.float32
    )


def half_levels(per_dev):
    levels = []
    base = 0
    for height in range(1, per_dev.bit_length() - 1):
        node_count = per_dev >> height
        levels.append((base, node_count // 2, per_dev - 2 * node_count))
        base += node_count // 2
    return levels, base


def pack_kernel(per_dev, inverse, basis, coupling, *refs):
    targets, buffers, (sems, out_sems) = refs[:4], refs[4:8], refs[8:]
    factors, couplings, keep, cross = buffers
    levels, total = half_levels(per_dev)
    high = lax.axis_index("rhs") // CORES
    node_size = inverse.shape[2]
    rank = basis.shape[2]
    parts = (
        (inverse, 0, node_size),
        (basis, node_size, rank),
        (coupling, node_size + rank, rank),
    )
    copies = []
    for source, start, width in parts:
        columns = pl.ds(start, width)
        for base, count, offset in levels:
            mine = source.at[pl.ds(offset + high * count, count)]
            other = source.at[pl.ds(offset + (1 - high) * count, count)]
            if source is coupling:
                for n in range(count):
                    sent = couplings.at[:, pl.ds((base + n) * rank, rank)]
                    copies.append((other.at[n], sent))
            else:
                copies.append((other, factors.at[pl.ds(base, count), :, columns]))
            copies.append((mine, keep.at[pl.ds(base, count), :, columns]))
        copies.append((source.at[per_dev - 2], keep.at[total, :, columns]))
        copies.append((source.at[per_dev - 1], cross.at[:, columns]))
    started = []
    for i, (source, target) in enumerate(copies):
        copy = pltpu.make_async_copy(source, target, sems.at[i])
        copy.start()
        started.append(copy)
    for copy in started:
        copy.wait()
    started = []
    for i, (buffer, target) in enumerate(zip(buffers, targets)):
        copy = pltpu.make_async_copy(buffer, target, out_sems.at[i])
        copy.start()
        started.append(copy)
    for copy in started:
        copy.wait()


def pack(inverse, basis, coupling):
    per_dev, rows, node_size = inverse.shape
    rank = basis.shape[2]
    width = node_size + 2 * rank
    levels, total = half_levels(per_dev)
    shapes = [
        (total, rows, node_size + rank),
        (rows, total * rank),
        (total + 1, rows, width),
        (rows, width),
    ]
    return pl.pallas_call(
        functools.partial(pack_kernel, per_dev),
        in_specs=[pl.BlockSpec(memory_space=pl.ANY)] * 3,
        out_specs=[pl.BlockSpec(memory_space=pl.ANY)] * 4,
        out_shape=[jax.ShapeDtypeStruct(shape, inverse.dtype) for shape in shapes],
        scratch_shapes=[pltpu.VMEM(shape, inverse.dtype) for shape in shapes]
        + [pltpu.SemaphoreType.DMA((6 + 5 * len(levels) + total,)), pltpu.SemaphoreType.DMA((4,))],
        compiler_params=params(63),
        cost_estimate=cost(0, 4 * per_dev * rows * width),
    )(inverse, basis, coupling)


def climb_kernel(level, count, mine_ref, other_ref, *refs):
    extras, (ancestor_ref, *outs) = refs[:count], refs[count:]
    carrier_refs, passed = outs[: len(outs) - count], outs[len(outs) - count :]
    for ref, extra in zip(passed, extras):
        ref[...] = extra[...]
    right = (lax.axis_index("leaf") // (1 << level)) % 2 == 1

    @pl.when(right)
    def _():
        ancestor_ref[...] = mine_ref[...]
        for ref in carrier_refs:
            ref[...] = other_ref[:, : ref.shape[1]]

    @pl.when(jnp.logical_not(right))
    def _():
        ancestor_ref[...] = other_ref[...]
        for ref in carrier_refs:
            ref[...] = mine_ref[:, : ref.shape[1]]


def climb(level, mine, other, keep, extras=()):
    return pl.pallas_call(
        functools.partial(climb_kernel, level, len(extras)),
        out_shape=[pltpu.VMEM(mine.shape, mine.dtype)]
        + [pltpu.VMEM((mine.shape[0], size), mine.dtype) for size in keep]
        + [pltpu.VMEM(extra.shape, extra.dtype) for extra in extras],
        compiler_params=params(),
        cost_estimate=cost(0, 4 * mine.size),
    )(mine, other, *extras)


def join_kernel(cuts, *refs):
    *blocks, _, out_ref = refs
    start = 0
    for ref, (first, width) in zip(blocks, cuts):
        out_ref[:, start : start + width] = ref[:, first : first + width]
        start += width


def join(blocks, anchor, cuts=None):
    rows = blocks[0].shape[0]
    cuts = cuts or [(0, block.shape[1]) for block in blocks]
    width = sum(size for _, size in cuts)
    return pl.pallas_call(
        functools.partial(join_kernel, cuts),
        out_shape=pltpu.VMEM((rows, width), blocks[0].dtype),
        compiler_params=params(),
        cost_estimate=cost(0, 4 * rows * width),
    )(*blocks, anchor)


def hop_kernel(level, top_ref, tail_ref, _, out_ref):
    node_size = top_ref.shape[1]
    side = (lax.axis_index("leaf") // (1 << level)) % 2
    here = lax.axis_index("rhs") // CORES == side
    out_ref[:, node_size:] = tail_ref[:, node_size:]

    @pl.when(here)
    def _():
        out_ref[:, :node_size] = top_ref[...]

    @pl.when(jnp.logical_not(here))
    def _():
        out_ref[:, :node_size] = tail_ref[:, :node_size]


def hop(level, top, tail, anchor):
    return pl.pallas_call(
        functools.partial(hop_kernel, level),
        out_shape=pltpu.VMEM(tail.shape, tail.dtype),
        compiler_params=params(),
        cost_estimate=cost(0, 4 * tail.size),
    )(top, tail, anchor)


def leaf_kernel(count, side_ref, *refs):
    points, refs = refs[:count], refs[count:]
    order_ref, inverse_ref, basis_ref, values_ref, same_ref, cross_ref, *rest = refs
    targets = values_ref.shape[1]
    stacked = rest[0] if rest else points[0]
    chunks, pieces = stacked.shape[:2]

    if rest:

        @pl.when(pl.program_id(0) == 0)
        def _():
            place = lax.axis_index("rhs")
            for flip, points_ref in zip(PIECES, points):
                for w in range(pieces):
                    stacked[place ^ flip, w] = points_ref[:, w * LANES : (w + 1) * LANES]

    order = order_ref[...]
    high = order // LANES
    low = order % LANES
    rows = lax.broadcasted_iota(jnp.int32, (LANES, order.shape[1]), 0)
    pick = jnp.where(rows == low, 1.0, 0.0).astype(jnp.bfloat16)
    spread = jnp.dot(
        stacked[...].reshape(-1, LANES), pick, preferred_element_type=jnp.float32
    )
    ordered = jnp.zeros((targets, order.shape[1]), jnp.float32)
    for k in range(chunks * pieces):
        ordered = jnp.where(high == k, spread[k * targets : (k + 1) * targets, :], ordered)
    values = dot_rows(ordered.astype(jnp.bfloat16), inverse_ref[0])
    values_ref[0] = values
    partial = jnp.dot(
        values.astype(jnp.bfloat16), basis_ref[0], preferred_element_type=jnp.float32
    ).astype(jnp.bfloat16)
    share = targets // CORES
    for core in range(CORES):

        @pl.when(side_ref[1] == core)
        def _():
            same_ref[0] = partial[core * share : (core + 1) * share]
            cross_ref[0] = partial[(1 - core) * share : (2 - core) * share]


def leaf_up(side, points, point_order, leaf_inverse, leaf_basis):
    leaves, rows, leaf_size = leaf_inverse.shape
    rank = leaf_basis.shape[2]
    half = leaves // 2
    joined = points[0].ndim == 4
    if joined:
        shape = points[0].shape
    else:
        targets, width = points[0].shape
        shape = (len(points), width // LANES, targets, LANES)
    targets = shape[2]
    share = targets // CORES
    sent = jax.ShapeDtypeStruct((half, share, rank), jnp.bfloat16)
    out_specs = [
        pl.BlockSpec((1, targets, rows), lambda i, side: (i, 0, 0)),
        pl.BlockSpec((1, share, rank), lambda i, side: (i, 0, 0)),
        pl.BlockSpec((1, share, rank), lambda i, side: (i, 0, 0)),
    ]
    out_shape = [jax.ShapeDtypeStruct((half, targets, rows), jnp.float32), sent, sent]
    if not joined:
        out_specs.append(pl.BlockSpec(shape, lambda i, side: (0, 0, 0, 0)))
        out_shape.append(pltpu.VMEM(shape, jnp.bfloat16))
    point_specs = [
        pl.BlockSpec(block.shape, lambda i, side, rank=block.ndim: (0,) * rank) for block in points
    ]
    return pl.pallas_call(
        functools.partial(leaf_kernel, len(points)),
        grid_spec=pltpu.PrefetchScalarGridSpec(
            num_scalar_prefetch=1,
            grid=(half,),
            in_specs=[
                *point_specs,
                pl.BlockSpec((1, leaf_size), lambda i, side: (0, side[0] * half + i)),
                pl.BlockSpec((1, rows, leaf_size), lambda i, side: (side[0] * half + i, 0, 0)),
                pl.BlockSpec((1, rows, rank), lambda i, side: (side[0] * half + i, 0, 0)),
            ],
            out_specs=out_specs,
        ),
        out_shape=out_shape,
        compiler_params=params(),
        cost_estimate=cost(
            leaves * targets * leaf_size * (shape[0] * shape[1] * LANES + 2 * rows),
            leaves * rows * (leaf_size + rank + 3 * targets),
        ),
    )(side, *points, point_order.reshape(1, -1), leaf_inverse, leaf_basis)


def solve_node(stacked, inverses, bases, solved_ref):
    mine = lax.axis_index("rhs")
    total = None
    for flip, inverse, basis in zip(PIECES, inverses, bases):
        solved = dot_rows(stacked, inverse)
        solved_ref[mine ^ flip] = solved
        term = jnp.dot(solved.astype(jnp.bfloat16), basis, preferred_element_type=jnp.float32)
        total = term if total is None else total + term
    return total


def group_up_kernel(per_dev, *refs):
    *refs, solved_ref, out_ref = refs
    parts, packs = refs[: 2 * CORES], refs[2 * CORES :]
    levels, _ = half_levels(per_dev)
    rank = parts[0].shape[2]

    def pieces(node, start, width):
        return [ref[node, :, pl.ds(start, width)] for ref in packs]

    sums = sum(ref[...].astype(jnp.float32) for ref in parts).astype(jnp.bfloat16)
    current = [sums[i] for i in range(sums.shape[0])]
    for base, count, _ in levels:
        following = []
        for n in range(count):
            node = base + n
            compressed = solve_node(
                jnp.concatenate([current[2 * n], current[2 * n + 1]], axis=1),
                pieces(node, 0, 2 * rank),
                pieces(node, 2 * rank, rank),
                solved_ref.at[node],
            )
            following.append(compressed.astype(jnp.bfloat16))
        current = following
    out_ref[...] = current[0]


def group_up(per_dev, parts, packs):
    leaves, share, rank = parts[0].shape
    _, total = half_levels(per_dev)
    _, rows, width = packs[0].shape
    return pl.pallas_call(
        functools.partial(group_up_kernel, per_dev),
        out_shape=[
            jax.ShapeDtypeStruct((total, 2 * CORES, share, rows), jnp.float32),
            jax.ShapeDtypeStruct((share, rank), jnp.bfloat16),
        ],
        compiler_params=params(),
        cost_estimate=cost(24 * total * share * rows * rank, 8 * total * rows * width),
    )(*parts, *packs)


def order_pair(right, mine, other):
    return jnp.concatenate([jnp.where(right, other, mine), jnp.where(right, mine, other)], axis=1)


def half_up_kernel(mine_ref, other_ref, own_ref, near_ref, solved_ref, out_ref):
    rank = mine_ref.shape[1]
    place = lax.axis_index("rhs")
    stacked = order_pair(place // CORES == 1, mine_ref[...], other_ref[...])
    total = 0.0
    for flip, ref in enumerate((own_ref, near_ref)):
        solved = dot_rows(stacked, ref[0, :, : 2 * rank])
        solved_ref[(place ^ flip) % CORES] = solved
        total += jnp.dot(
            solved.astype(jnp.bfloat16),
            ref[0, :, 2 * rank : 3 * rank],
            preferred_element_type=jnp.float32,
        )
    out_ref[...] = total.astype(jnp.bfloat16)


def half_up(mine, other, own, near):
    share, rank = mine.shape
    nodes, rows, width = own.shape
    last = pl.BlockSpec((1, rows, width), lambda i: (nodes - 1, 0, 0))
    whole = pl.BlockSpec((share, rank), lambda i: (0, 0))
    return pl.pallas_call(
        half_up_kernel,
        grid=(1,),
        in_specs=[whole, whole, last, last],
        out_specs=[pl.BlockSpec((CORES, share, rows), lambda i: (0, 0, 0)), whole],
        out_shape=[
            jax.ShapeDtypeStruct((CORES, share, rows), jnp.float32),
            jax.ShapeDtypeStruct((share, rank), jnp.bfloat16),
        ],
        compiler_params=params(),
        cost_estimate=cost(12 * share * rows * rank, 4 * rows * width),
    )(mine, other, own, near)


def total_of(refs):
    if len(refs) == 1:
        return refs[0][...]
    return sum(ref[...].astype(jnp.float32) for ref in refs).astype(jnp.bfloat16)


def cross_pair(level, refs):
    half = len(refs) // 2
    refs = refs[::-1] if half > 1 else refs
    is_right = (lax.axis_index("leaf") // (1 << level)) % 2 == 1
    return order_pair(is_right, total_of(refs[:half]), total_of(refs[half:]))


def from_cores(packs):
    if len(packs[-1].shape) == 2:
        return packs
    return [*packs[:-1], packs[-1].at[(lax.axis_index("rhs") + 1) % CORES]]


def cross_up_kernel(level, *refs):
    *refs, solved_ref, out_ref = refs
    inputs, packs = refs[: -2 * CORES], from_cores(refs[-2 * CORES :])
    rank = out_ref.shape[1]
    compressed = solve_node(
        cross_pair(level, inputs),
        [ref[:, : 2 * rank] for ref in packs],
        [ref[:, 2 * rank : 3 * rank] for ref in packs],
        solved_ref,
    )
    out_ref[...] = compressed.astype(jnp.bfloat16)


def cross_up(level, inputs, packs):
    share, rank = inputs[0].shape[-2:]
    rows, width = packs[0].shape
    return pl.pallas_call(
        functools.partial(cross_up_kernel, level),
        out_shape=[
            jax.ShapeDtypeStruct((2 * CORES, share, rows), jnp.float32),
            jax.ShapeDtypeStruct((share, rank), jnp.bfloat16),
        ],
        compiler_params=params(),
        cost_estimate=cost(24 * share * rows * rank, 8 * rows * width),
    )(*inputs, *packs)


def down_kernel(per_dev, cross_levels, input_count, *refs):
    *refs, out_ref, value = refs
    inputs, refs = refs[:input_count], refs[input_count:]
    solved_cross, refs = refs[: cross_levels - 1], refs[cross_levels - 1 :]
    solved_top, solved_half, refs = refs[0], refs[1], refs[2:]
    count = 2 * CORES * (cross_levels - 1)
    cross_packs, (both, keep, keep_near) = refs[:count], refs[count:]
    levels, total = half_levels(per_dev)
    rank = out_ref.shape[2]
    node_size = 2 * rank
    place = lax.axis_index("rhs")
    tail, near_tail = both.at[place % CORES], both.at[(place + 1) % CORES]

    def choose(which):
        return jnp.concatenate([value[2 * which], value[2 * which + 1]], axis=1)

    def side(level):
        return (lax.axis_index("leaf") // (1 << level)) % 2

    def columns(ref):
        width = ref.shape[-1]
        return pl.ds(width - rank, rank)

    stacked = cross_pair(cross_levels - 1, inputs)
    half = side(cross_levels - 1)
    for flip, ref in ((0, tail), (1, near_tail)):
        core = (place ^ flip) % CORES
        value[2 * half + core] = dot_rows(stacked, ref[:, :node_size]).astype(jnp.bfloat16)
    incoming = choose(half)
    for level in range(cross_levels - 2, -1, -1):
        packs = from_cores(cross_packs[2 * CORES * level : 2 * CORES * (level + 1)])
        couplings = [ref[:, columns(ref)] for ref in packs]
        for flip, coupling in zip(PIECES, couplings):
            piece = place ^ flip
            solved = solved_cross[level][piece]
            value[piece] = (solved - dot_rows(incoming, coupling)).astype(jnp.bfloat16)
        incoming = choose(side(level))

    for flip, ref in ((0, keep), (1, keep_near)):
        piece = (place ^ flip) % CORES
        coupling = ref[total, :, columns(ref)]
        value[piece] = (solved_top[piece] - dot_rows(incoming, coupling)).astype(jnp.bfloat16)
    current = [choose(0)]
    for base, count, _ in reversed(levels):
        following = []
        for n in range(count):
            node = base + n
            start = node_size + node * rank
            couplings = (
                keep[node, :, columns(keep)],
                tail[:, start : start + rank],
                keep_near[node, :, columns(keep)],
                near_tail[:, start : start + rank],
            )
            for flip, coupling in zip(PIECES, couplings):
                piece = place ^ flip
                value[piece] = (
                    solved_half[node, piece] - dot_rows(current[n], coupling)
                ).astype(jnp.bfloat16)
            following += [choose(0), choose(1)]
        current = following
    for i, block in enumerate(current):
        out_ref[i] = block


def way_down(per_dev, inputs, solved_cross, solved_top, solved_half, cross_packs, others):
    share, rank = inputs[0].shape[-2:]
    rows = solved_half.shape[3]
    operands = [*inputs, *solved_cross, solved_top, solved_half]
    for packs in cross_packs:
        operands += packs
    operands += others
    return pl.pallas_call(
        functools.partial(down_kernel, per_dev, len(cross_packs) + 1, len(inputs)),
        out_shape=jax.ShapeDtypeStruct((per_dev // 2, share, rank), jnp.bfloat16),
        scratch_shapes=[pltpu.VMEM((2 * CORES, share, rows), jnp.bfloat16)],
        compiler_params=params(18),
        cost_estimate=cost(8 * share * rows * rank * per_dev, 4 * 1024 * 1024),
    )(*operands)


def finish_kernel(far_ref, own_ref, incoming_ref, coupling_ref, out_ref):
    half = own_ref.shape[0]
    high = lax.axis_index("rhs") // CORES
    for values_ref, side in ((far_ref, 1 - high), (own_ref, high)):
        for i in range(half):
            leaf = side * half + i
            incoming = jnp.concatenate(
                [incoming_ref[side * CORES + core, i] for core in range(CORES)], axis=0
            )
            out_ref[leaf] = values_ref[i] - dot_rows(incoming, coupling_ref[leaf])


def finish(far, own, incoming, coupling):
    half, targets, rows = own.shape
    return pl.pallas_call(
        finish_kernel,
        out_shape=jax.ShapeDtypeStruct((2 * half, targets, rows), jnp.float32),
        compiler_params=params(),
        cost_estimate=cost(4 * half * targets * rows * coupling.shape[2], 16 * own.size),
    )(far, own, incoming, coupling)


def swap(block, axis, bit):
    return lax.ppermute(block, axis, [(i, i ^ bit) for i in range(lax.axis_size(axis))])


def gather_cores(block):
    shares = lax.axis_size("rhs")
    cores = [[i + core for core in range(CORES)] for i in range(0, shares, CORES)]
    return lax.all_gather(block, "rhs", axis_index_groups=cores)


def far_swap(block, leaf_bit, rhs_bit):
    shares = lax.axis_size("rhs")
    flip = leaf_bit * shares + rhs_bit
    count = lax.axis_size("leaf") * shares
    return lax.ppermute(block, ("leaf", "rhs"), [(i, i ^ flip) for i in range(count)])


def after(value, anchor):
    return lax.optimization_barrier((value, anchor))[0]


def body(
    right_side,
    point_order,
    leaf_inverse,
    leaf_basis,
    leaf_coupling,
    node_inverse,
    node_basis,
    node_coupling,
):
    devices = lax.axis_size("leaf")
    per_dev = leaf_inverse.shape[0]
    node_size = node_inverse.shape[2]
    rank = leaf_basis.shape[2]
    cross_levels = devices.bit_length() - 1
    place = lax.axis_index("rhs")
    high, low = place // CORES, place % CORES

    def rise(carrier, level, anchor, extras=()):
        other = after(swap(carrier, "leaf", 1 << level), anchor)
        width = node_size if level == cross_levels - 2 else carrier.shape[1]
        keep = [width] * (level < cross_levels - 1)
        ancestor, *carriers = climb(level, carrier, other, keep, extras)
        return (ancestor, *(carriers or [None]))

    send, send_coupling, keep, carrier = pack(node_inverse, node_basis, node_coupling)
    across, beside = after(
        [swap(right_side, "rhs", CORES), swap(right_side, "rhs", 1)], send
    )
    points = [across, beside, swap(after(across, beside), "rhs", 1)]
    half_far = swap(send, "rhs", CORES)
    keep_near = swap(after(keep, points), "rhs", 1)
    carrier = after(carrier, points)
    points = [right_side, *points]

    leaves = (point_order, leaf_inverse, leaf_basis)
    far_values, far_same, far_cross, joined = leaf_up(
        jnp.stack([1 - high, low]), points, *leaves
    )
    keep_near = after(keep_near, far_same)
    own_values, own_same, own_cross = leaf_up(
        jnp.stack([high, low]), [after(joined, keep_near)], *leaves
    )
    ancestor, carrier, send_coupling = rise(carrier, 0, own_same, [send_coupling])
    ancestors = [ancestor]
    far_same = after(swap(far_same, "rhs", CORES), own_same)
    far_cross = after(swap(far_cross, "rhs", CORES + 1), own_same)
    parts = [own_same, far_same, swap(own_cross, "rhs", 1), far_cross]
    half_far = after(half_far, (parts, carrier))
    half_near = swap(half_far, "rhs", 1)
    fars = [swap(after(ancestors[0], half_far), "rhs", CORES)]

    solved_half, current = group_up(per_dev, parts, [keep, half_far, keep_near, half_near])
    own_near = swap(join([ancestors[0]], current), "rhs", 1)
    other = swap(current, "rhs", CORES)
    ancestor, carrier = rise(carrier, 1, other)
    ancestors.append(ancestor)
    solved_top, current = half_up(current, after(other, own_near), keep, keep_near)
    fars[0] = after(fars[0], other)
    near_far = swap(fars[0], "rhs", 1)
    cross_packs = [[ancestors[0], fars[0], own_near, near_far]]
    fars.append(swap(join([ancestors[1]], current), "rhs", CORES))
    current = after(current, near_far)
    diagonal = far_swap(current, 1, CORES)
    beside = swap(current, "leaf", 1)
    across = swap(current, "rhs", CORES)
    inputs = after([diagonal, beside, across, current], fars[1])

    solved_cross = []
    for level in range(cross_levels - 1):
        if level > 0:
            own, far = ancestors[level], fars[level]
            own_near = swap(join([own], current), "rhs", 1)
            far_near = gather_cores(join([far], current))
            cross_packs.append([own, far, own_near, far_near])
        solved, current = cross_up(level, inputs, cross_packs[level])
        solved_cross.append(solved)
        inputs = [current, swap(current, "leaf", 2 << level)]
        if level == 0:
            for later in range(2, cross_levels):
                ancestor, carrier = rise(carrier, later, current)
                ancestors.append(ancestor)
            for later in range(2, cross_levels - 1):
                fars.append(swap(join([ancestors[later]], current), "rhs", CORES))
            tail = swap(join([ancestors[-1], send_coupling], current), "rhs", CORES)

    tail = hop(cross_levels - 1, ancestors[-1], tail, current)
    others = [gather_cores(tail), keep, keep_near]
    shares = way_down(per_dev, inputs, solved_cross, solved_top, solved_half, cross_packs, others)
    incoming = lax.all_gather(shares, "rhs", axis=0)
    return finish(far_values, own_values, incoming, leaf_coupling)


def solution(mesh):
    placed = (P(None, ("leaf", "rhs")), P("leaf")) + (P("leaf", "rhs", None),) * 6
    return jax.shard_map(
        body, mesh=mesh, in_specs=placed, out_specs=P("leaf", None, "rhs"), check_vma=False
    )
```

```python
import functools

import jax
import jax.numpy as jnp
from jax import lax
from jax.experimental import pallas as pl
from jax.experimental.pallas import tpu as pltpu
from jax.sharding import PartitionSpec as P

LANES = 256
PIECES = (0, 2, 1, 3)
CORES = 2


def params(mebibytes=12):
    return pltpu.CompilerParams(vmem_limit_bytes=mebibytes * 1024 * 1024)


def cost(flops, moved):
    return pl.CostEstimate(flops=flops // 1000, bytes_accessed=moved // 1000, transcendentals=0)


def dot_rows(left, right):
    return lax.dot_general(
        left, right, (((1,), (1,)), ((), ())), preferred_element_type=jnp.float32
    )


def half_levels(per_dev):
    levels = []
    base = 0
    for height in range(1, per_dev.bit_length() - 1):
        node_count = per_dev >> height
        levels.append((base, node_count // 2, per_dev - 2 * node_count))
        base += node_count // 2
    return levels, base


def pack_kernel(per_dev, inverse, basis, coupling, *refs):
    targets, buffers, (sems, out_sems) = refs[:4], refs[4:8], refs[8:]
    factors, couplings, keep, cross = buffers
    levels, total = half_levels(per_dev)
    high = lax.axis_index("rhs") // CORES
    node_size = inverse.shape[2]
    rank = basis.shape[2]
    parts = (
        (inverse, 0, node_size),
        (basis, node_size, rank),
        (coupling, node_size + rank, rank),
    )
    copies = []
    for source, start, width in parts:
        columns = pl.ds(start, width)
        for base, count, offset in levels:
            mine = source.at[pl.ds(offset + high * count, count)]
            other = source.at[pl.ds(offset + (1 - high) * count, count)]
            if source is coupling:
                for n in range(count):
                    sent = couplings.at[:, pl.ds((base + n) * rank, rank)]
                    copies.append((other.at[n], sent))
            else:
                copies.append((other, factors.at[pl.ds(base, count), :, columns]))
            copies.append((mine, keep.at[pl.ds(base, count), :, columns]))
        copies.append((source.at[per_dev - 2], keep.at[total, :, columns]))
        copies.append((source.at[per_dev - 1], cross.at[:, columns]))
    started = []
    for i, (source, target) in enumerate(copies):
        copy = pltpu.make_async_copy(source, target, sems.at[i])
        copy.start()
        started.append(copy)
    for copy in started:
        copy.wait()
    started = []
    for i, (buffer, target) in enumerate(zip(buffers, targets)):
        copy = pltpu.make_async_copy(buffer, target, out_sems.at[i])
        copy.start()
        started.append(copy)
    for copy in started:
        copy.wait()


def pack(inverse, basis, coupling):
    per_dev, rows, node_size = inverse.shape
    rank = basis.shape[2]
    width = node_size + 2 * rank
    levels, total = half_levels(per_dev)
    shapes = [
        (total, rows, node_size + rank),
        (rows, total * rank),
        (total + 1, rows, width),
        (rows, width),
    ]
    return pl.pallas_call(
        functools.partial(pack_kernel, per_dev),
        in_specs=[pl.BlockSpec(memory_space=pl.ANY)] * 3,
        out_specs=[pl.BlockSpec(memory_space=pl.ANY)] * 4,
        out_shape=[jax.ShapeDtypeStruct(shape, inverse.dtype) for shape in shapes],
        scratch_shapes=[pltpu.VMEM(shape, inverse.dtype) for shape in shapes]
        + [pltpu.SemaphoreType.DMA((6 + 5 * len(levels) + total,)), pltpu.SemaphoreType.DMA((4,))],
        compiler_params=params(63),
        cost_estimate=cost(0, 4 * per_dev * rows * width),
    )(inverse, basis, coupling)


def climb_kernel(level, count, mine_ref, other_ref, *refs):
    extras, (ancestor_ref, *outs) = refs[:count], refs[count:]
    carrier_refs, passed = outs[: len(outs) - count], outs[len(outs) - count :]
    for ref, extra in zip(passed, extras):
        ref[...] = extra[...]
    right = (lax.axis_index("leaf") // (1 << level)) % 2 == 1

    @pl.when(right)
    def _():
        ancestor_ref[...] = mine_ref[...]
        for ref in carrier_refs:
            ref[...] = other_ref[:, : ref.shape[1]]

    @pl.when(jnp.logical_not(right))
    def _():
        ancestor_ref[...] = other_ref[...]
        for ref in carrier_refs:
            ref[...] = mine_ref[:, : ref.shape[1]]


def climb(level, mine, other, keep, extras=()):
    return pl.pallas_call(
        functools.partial(climb_kernel, level, len(extras)),
        out_shape=[pltpu.VMEM(mine.shape, mine.dtype)]
        + [pltpu.VMEM((mine.shape[0], size), mine.dtype) for size in keep]
        + [pltpu.VMEM(extra.shape, extra.dtype) for extra in extras],
        compiler_params=params(),
        cost_estimate=cost(0, 4 * mine.size),
    )(mine, other, *extras)


def join_kernel(cuts, *refs):
    *blocks, _, out_ref = refs
    start = 0
    for ref, (first, width) in zip(blocks, cuts):
        out_ref[:, start : start + width] = ref[:, first : first + width]
        start += width


def join(blocks, anchor, cuts=None):
    rows = blocks[0].shape[0]
    cuts = cuts or [(0, block.shape[1]) for block in blocks]
    width = sum(size for _, size in cuts)
    return pl.pallas_call(
        functools.partial(join_kernel, cuts),
        out_shape=pltpu.VMEM((rows, width), blocks[0].dtype),
        compiler_params=params(),
        cost_estimate=cost(0, 4 * rows * width),
    )(*blocks, anchor)


def hop_kernel(level, top_ref, tail_ref, _, out_ref):
    node_size = top_ref.shape[1]
    side = (lax.axis_index("leaf") // (1 << level)) % 2
    here = lax.axis_index("rhs") // CORES == side
    out_ref[:, node_size:] = tail_ref[:, node_size:]

    @pl.when(here)
    def _():
        out_ref[:, :node_size] = top_ref[...]

    @pl.when(jnp.logical_not(here))
    def _():
        out_ref[:, :node_size] = tail_ref[:, :node_size]


def hop(level, top, tail, anchor):
    return pl.pallas_call(
        functools.partial(hop_kernel, level),
        out_shape=pltpu.VMEM(tail.shape, tail.dtype),
        compiler_params=params(),
        cost_estimate=cost(0, 4 * tail.size),
    )(top, tail, anchor)


def leaf_kernel(count, side_ref, *refs):
    points, refs = refs[:count], refs[count:]
    order_ref, inverse_ref, basis_ref, values_ref, same_ref, cross_ref, *rest = refs
    targets = values_ref.shape[1]
    stacked = rest[0] if rest else points[0]
    chunks, pieces = stacked.shape[:2]

    if rest:

        @pl.when(pl.program_id(0) == 0)
        def _():
            place = lax.axis_index("rhs")
            for flip, points_ref in zip(PIECES, points):
                for w in range(pieces):
                    stacked[place ^ flip, w] = points_ref[:, w * LANES : (w + 1) * LANES]

    order = order_ref[...]
    high = order // LANES
    low = order % LANES
    rows = lax.broadcasted_iota(jnp.int32, (LANES, order.shape[1]), 0)
    pick = jnp.where(rows == low, 1.0, 0.0).astype(jnp.bfloat16)
    spread = jnp.dot(
        stacked[...].reshape(-1, LANES), pick, preferred_element_type=jnp.float32
    )
    ordered = jnp.zeros((targets, order.shape[1]), jnp.float32)
    for k in range(chunks * pieces):
        ordered = jnp.where(high == k, spread[k * targets : (k + 1) * targets, :], ordered)
    values = dot_rows(ordered.astype(jnp.bfloat16), inverse_ref[0])
    values_ref[0] = values
    partial = jnp.dot(
        values.astype(jnp.bfloat16), basis_ref[0], preferred_element_type=jnp.float32
    ).astype(jnp.bfloat16)
    share = targets // CORES
    for core in range(CORES):

        @pl.when(side_ref[1] == core)
        def _():
            same_ref[0] = partial[core * share : (core + 1) * share]
            cross_ref[0] = partial[(1 - core) * share : (2 - core) * share]


def leaf_up(side, points, point_order, leaf_inverse, leaf_basis):
    leaves, rows, leaf_size = leaf_inverse.shape
    rank = leaf_basis.shape[2]
    half = leaves // 2
    joined = points[0].ndim == 4
    if joined:
        shape = points[0].shape
    else:
        targets, width = points[0].shape
        shape = (len(points), width // LANES, targets, LANES)
    targets = shape[2]
    share = targets // CORES
    sent = jax.ShapeDtypeStruct((half, share, rank), jnp.bfloat16)
    out_specs = [
        pl.BlockSpec((1, targets, rows), lambda i, side: (i, 0, 0)),
        pl.BlockSpec((1, share, rank), lambda i, side: (i, 0, 0)),
        pl.BlockSpec((1, share, rank), lambda i, side: (i, 0, 0)),
    ]
    out_shape = [jax.ShapeDtypeStruct((half, targets, rows), jnp.float32), sent, sent]
    if not joined:
        out_specs.append(pl.BlockSpec(shape, lambda i, side: (0, 0, 0, 0)))
        out_shape.append(pltpu.VMEM(shape, jnp.bfloat16))
    point_specs = [
        pl.BlockSpec(block.shape, lambda i, side, rank=block.ndim: (0,) * rank) for block in points
    ]
    return pl.pallas_call(
        functools.partial(leaf_kernel, len(points)),
        grid_spec=pltpu.PrefetchScalarGridSpec(
            num_scalar_prefetch=1,
            grid=(half,),
            in_specs=[
                *point_specs,
                pl.BlockSpec((1, leaf_size), lambda i, side: (0, side[0] * half + i)),
                pl.BlockSpec((1, rows, leaf_size), lambda i, side: (side[0] * half + i, 0, 0)),
                pl.BlockSpec((1, rows, rank), lambda i, side: (side[0] * half + i, 0, 0)),
            ],
            out_specs=out_specs,
        ),
        out_shape=out_shape,
        compiler_params=params(),
        cost_estimate=cost(
            leaves * targets * leaf_size * (shape[0] * shape[1] * LANES + 2 * rows),
            leaves * rows * (leaf_size + rank + 3 * targets),
        ),
    )(side, *points, point_order.reshape(1, -1), leaf_inverse, leaf_basis)


def solve_node(stacked, inverses, bases, solved_ref):
    mine = lax.axis_index("rhs")
    total = None
    for flip, inverse, basis in zip(PIECES, inverses, bases):
        solved = dot_rows(stacked, inverse)
        solved_ref[mine ^ flip] = solved
        term = jnp.dot(solved.astype(jnp.bfloat16), basis, preferred_element_type=jnp.float32)
        total = term if total is None else total + term
    return total


def group_up_kernel(per_dev, *refs):
    *refs, solved_ref, out_ref = refs
    parts, packs = refs[: 2 * CORES], refs[2 * CORES :]
    levels, _ = half_levels(per_dev)
    rank = parts[0].shape[2]

    def pieces(node, start, width):
        return [ref[node, :, pl.ds(start, width)] for ref in packs]

    sums = sum(ref[...].astype(jnp.float32) for ref in parts).astype(jnp.bfloat16)
    current = [sums[i] for i in range(sums.shape[0])]
    for base, count, _ in levels:
        following = []
        for n in range(count):
            node = base + n
            compressed = solve_node(
                jnp.concatenate([current[2 * n], current[2 * n + 1]], axis=1),
                pieces(node, 0, 2 * rank),
                pieces(node, 2 * rank, rank),
                solved_ref.at[node],
            )
            following.append(compressed.astype(jnp.bfloat16))
        current = following
    out_ref[...] = current[0]


def group_up(per_dev, parts, packs):
    leaves, share, rank = parts[0].shape
    _, total = half_levels(per_dev)
    _, rows, width = packs[0].shape
    return pl.pallas_call(
        functools.partial(group_up_kernel, per_dev),
        out_shape=[
            jax.ShapeDtypeStruct((total, 2 * CORES, share, rows), jnp.float32),
            jax.ShapeDtypeStruct((share, rank), jnp.bfloat16),
        ],
        compiler_params=params(),
        cost_estimate=cost(24 * total * share * rows * rank, 8 * total * rows * width),
    )(*parts, *packs)


def order_pair(right, mine, other):
    return jnp.concatenate([jnp.where(right, other, mine), jnp.where(right, mine, other)], axis=1)


def half_up_kernel(mine_ref, other_ref, own_ref, near_ref, solved_ref, out_ref):
    rank = mine_ref.shape[1]
    place = lax.axis_index("rhs")
    stacked = order_pair(place // CORES == 1, mine_ref[...], other_ref[...])
    total = 0.0
    for flip, ref in enumerate((own_ref, near_ref)):
        solved = dot_rows(stacked, ref[0, :, : 2 * rank])
        solved_ref[(place ^ flip) % CORES] = solved
        total += jnp.dot(
            solved.astype(jnp.bfloat16),
            ref[0, :, 2 * rank : 3 * rank],
            preferred_element_type=jnp.float32,
        )
    out_ref[...] = total.astype(jnp.bfloat16)


def half_up(mine, other, own, near):
    share, rank = mine.shape
    nodes, rows, width = own.shape
    last = pl.BlockSpec((1, rows, width), lambda i: (nodes - 1, 0, 0))
    whole = pl.BlockSpec((share, rank), lambda i: (0, 0))
    return pl.pallas_call(
        half_up_kernel,
        grid=(1,),
        in_specs=[whole, whole, last, last],
        out_specs=[pl.BlockSpec((CORES, share, rows), lambda i: (0, 0, 0)), whole],
        out_shape=[
            jax.ShapeDtypeStruct((CORES, share, rows), jnp.float32),
            jax.ShapeDtypeStruct((share, rank), jnp.bfloat16),
        ],
        compiler_params=params(),
        cost_estimate=cost(12 * share * rows * rank, 4 * rows * width),
    )(mine, other, own, near)


def total_of(refs):
    if len(refs) == 1:
        return refs[0][...]
    return sum(ref[...].astype(jnp.float32) for ref in refs).astype(jnp.bfloat16)


def cross_pair(level, refs):
    half = len(refs) // 2
    refs = refs[::-1] if half > 1 else refs
    is_right = (lax.axis_index("leaf") // (1 << level)) % 2 == 1
    return order_pair(is_right, total_of(refs[:half]), total_of(refs[half:]))


def from_cores(packs):
    if len(packs[-1].shape) == 2:
        return packs
    return [*packs[:-1], packs[-1].at[(lax.axis_index("rhs") + 1) % CORES]]


def cross_up_kernel(level, *refs):
    *refs, solved_ref, out_ref = refs
    inputs, packs = refs[: -2 * CORES], from_cores(refs[-2 * CORES :])
    rank = out_ref.shape[1]
    compressed = solve_node(
        cross_pair(level, inputs),
        [ref[:, : 2 * rank] for ref in packs],
        [ref[:, 2 * rank : 3 * rank] for ref in packs],
        solved_ref,
    )
    out_ref[...] = compressed.astype(jnp.bfloat16)


def cross_up(level, inputs, packs):
    share, rank = inputs[0].shape[-2:]
    rows, width = packs[0].shape
    return pl.pallas_call(
        functools.partial(cross_up_kernel, level),
        out_shape=[
            jax.ShapeDtypeStruct((2 * CORES, share, rows), jnp.float32),
            jax.ShapeDtypeStruct((share, rank), jnp.bfloat16),
        ],
        compiler_params=params(),
        cost_estimate=cost(24 * share * rows * rank, 8 * rows * width),
    )(*inputs, *packs)


def down_kernel(per_dev, cross_levels, input_count, *refs):
    *refs, out_ref, value = refs
    inputs, refs = refs[:input_count], refs[input_count:]
    solved_cross, refs = refs[: cross_levels - 1], refs[cross_levels - 1 :]
    solved_top, solved_half, refs = refs[0], refs[1], refs[2:]
    count = 2 * CORES * (cross_levels - 1)
    cross_packs, (both, keep, keep_near) = refs[:count], refs[count:]
    levels, total = half_levels(per_dev)
    rank = out_ref.shape[2]
    node_size = 2 * rank
    place = lax.axis_index("rhs")
    tail, near_tail = both.at[place % CORES], both.at[(place + 1) % CORES]

    def choose(which):
        return jnp.concatenate([value[2 * which], value[2 * which + 1]], axis=1)

    def side(level):
        return (lax.axis_index("leaf") // (1 << level)) % 2

    def columns(ref):
        width = ref.shape[-1]
        return pl.ds(width - rank, rank)

    stacked = cross_pair(cross_levels - 1, inputs)
    half = side(cross_levels - 1)
    for flip, ref in ((0, tail), (1, near_tail)):
        core = (place ^ flip) % CORES
        value[2 * half + core] = dot_rows(stacked, ref[:, :node_size]).astype(jnp.bfloat16)
    incoming = choose(half)
    for level in range(cross_levels - 2, -1, -1):
        packs = from_cores(cross_packs[2 * CORES * level : 2 * CORES * (level + 1)])
        couplings = [ref[:, columns(ref)] for ref in packs]
        for flip, coupling in zip(PIECES, couplings):
            piece = place ^ flip
            solved = solved_cross[level][piece]
            value[piece] = (solved - dot_rows(incoming, coupling)).astype(jnp.bfloat16)
        incoming = choose(side(level))

    for flip, ref in ((0, keep), (1, keep_near)):
        piece = (place ^ flip) % CORES
        coupling = ref[total, :, columns(ref)]
        value[piece] = (solved_top[piece] - dot_rows(incoming, coupling)).astype(jnp.bfloat16)
    current = [choose(0)]
    for base, count, _ in reversed(levels):
        following = []
        for n in range(count):
            node = base + n
            start = node_size + node * rank
            couplings = (
                keep[node, :, columns(keep)],
                tail[:, start : start + rank],
                keep_near[node, :, columns(keep)],
                near_tail[:, start : start + rank],
            )
            for flip, coupling in zip(PIECES, couplings):
                piece = place ^ flip
                value[piece] = (
                    solved_half[node, piece] - dot_rows(current[n], coupling)
                ).astype(jnp.bfloat16)
            following += [choose(0), choose(1)]
        current = following
    for i, block in enumerate(current):
        out_ref[i] = block


def way_down(per_dev, inputs, solved_cross, solved_top, solved_half, cross_packs, others):
    share, rank = inputs[0].shape[-2:]
    rows = solved_half.shape[3]
    operands = [*inputs, *solved_cross, solved_top, solved_half]
    for packs in cross_packs:
        operands += packs
    operands += others
    return pl.pallas_call(
        functools.partial(down_kernel, per_dev, len(cross_packs) + 1, len(inputs)),
        out_shape=jax.ShapeDtypeStruct((per_dev // 2, share, rank), jnp.bfloat16),
        scratch_shapes=[pltpu.VMEM((2 * CORES, share, rows), jnp.bfloat16)],
        compiler_params=params(18),
        cost_estimate=cost(8 * share * rows * rank * per_dev, 4 * 1024 * 1024),
    )(*operands)


def finish_kernel(far_ref, own_ref, incoming_ref, coupling_ref, out_ref):
    half = own_ref.shape[0]
    high = lax.axis_index("rhs") // CORES
    for values_ref, side in ((far_ref, 1 - high), (own_ref, high)):
        for i in range(half):
            leaf = side * half + i
            incoming = jnp.concatenate(
                [incoming_ref[side * CORES + core, i] for core in range(CORES)], axis=0
            )
            out_ref[leaf] = values_ref[i] - dot_rows(incoming, coupling_ref[leaf])


def finish(far, own, incoming, coupling):
    half, targets, rows = own.shape
    return pl.pallas_call(
        finish_kernel,
        out_shape=jax.ShapeDtypeStruct((2 * half, targets, rows), jnp.float32),
        compiler_params=params(),
        cost_estimate=cost(4 * half * targets * rows * coupling.shape[2], 16 * own.size),
    )(far, own, incoming, coupling)


def swap(block, axis, bit):
    return lax.ppermute(block, axis, [(i, i ^ bit) for i in range(lax.axis_size(axis))])


def gather_cores(block):
    shares = lax.axis_size("rhs")
    cores = [[i + core for core in range(CORES)] for i in range(0, shares, CORES)]
    return lax.all_gather(block, "rhs", axis_index_groups=cores)


def far_swap(block, leaf_bit, rhs_bit):
    shares = lax.axis_size("rhs")
    flip = leaf_bit * shares + rhs_bit
    count = lax.axis_size("leaf") * shares
    return lax.ppermute(block, ("leaf", "rhs"), [(i, i ^ flip) for i in range(count)])


def after(value, anchor):
    return lax.optimization_barrier((value, anchor))[0]


def body(
    right_side,
    point_order,
    leaf_inverse,
    leaf_basis,
    leaf_coupling,
    node_inverse,
    node_basis,
    node_coupling,
):
    devices = lax.axis_size("leaf")
    per_dev = leaf_inverse.shape[0]
    node_size = node_inverse.shape[2]
    rank = leaf_basis.shape[2]
    cross_levels = devices.bit_length() - 1
    place = lax.axis_index("rhs")
    high, low = place // CORES, place % CORES

    def rise(carrier, level, anchor, extras=()):
        other = after(swap(carrier, "leaf", 1 << level), anchor)
        width = node_size if level == cross_levels - 2 else carrier.shape[1]
        keep = [width] * (level < cross_levels - 1)
        ancestor, *carriers = climb(level, carrier, other, keep, extras)
        return (ancestor, *(carriers or [None]))

    send, send_coupling, keep, carrier = pack(node_inverse, node_basis, node_coupling)
    across, beside = after(
        [swap(right_side, "rhs", CORES), swap(right_side, "rhs", 1)], send
    )
    points = [across, beside, swap(after(across, beside), "rhs", 1)]
    half_far = swap(send, "rhs", CORES)
    keep_near = swap(after(keep, points[:2]), "rhs", 1)
    carrier = after(carrier, points[:2])
    points = [right_side, *points]

    leaves = (point_order, leaf_inverse, leaf_basis)
    far_values, far_same, far_cross, joined = leaf_up(
        jnp.stack([1 - high, low]), points, *leaves
    )
    keep_near = after(keep_near, far_same)
    own_values, own_same, own_cross = leaf_up(
        jnp.stack([high, low]), [after(joined, keep_near)], *leaves
    )
    ancestor, carrier, send_coupling = rise(carrier, 0, own_same, [send_coupling])
    ancestors = [ancestor]
    far_same = after(swap(far_same, "rhs", CORES), own_same)
    far_cross = after(swap(far_cross, "rhs", CORES + 1), own_same)
    parts = [own_same, far_same, swap(own_cross, "rhs", 1), far_cross]
    half_far = after(half_far, (parts, carrier))
    half_near = swap(half_far, "rhs", 1)
    fars = [swap(after(ancestors[0], half_far), "rhs", CORES)]

    solved_half, current = group_up(per_dev, parts, [keep, half_far, keep_near, half_near])
    own_near = swap(join([ancestors[0]], current), "rhs", 1)
    other = swap(current, "rhs", CORES)
    ancestor, carrier = rise(carrier, 1, other)
    ancestors.append(ancestor)
    solved_top, current = half_up(current, after(other, own_near), keep, keep_near)
    fars[0] = after(fars[0], other)
    near_far = swap(fars[0], "rhs", 1)
    cross_packs = [[ancestors[0], fars[0], own_near, near_far]]
    fars.append(swap(join([ancestors[1]], current), "rhs", CORES))
    current = after(current, near_far)
    diagonal = far_swap(current, 1, CORES)
    beside = swap(current, "leaf", 1)
    across = swap(current, "rhs", CORES)
    inputs = after([diagonal, beside, across, current], fars[1])

    solved_cross = []
    for level in range(cross_levels - 1):
        if level > 0:
            own, far = ancestors[level], fars[level]
            own_near = swap(join([own], current), "rhs", 1)
            far_near = gather_cores(join([far], current))
            cross_packs.append([own, far, own_near, far_near])
        solved, current = cross_up(level, inputs, cross_packs[level])
        solved_cross.append(solved)
        inputs = [current, swap(current, "leaf", 2 << level)]
        if level == 0:
            for later in range(2, cross_levels):
                ancestor, carrier = rise(carrier, later, current)
                ancestors.append(ancestor)
            for later in range(2, cross_levels - 1):
                fars.append(swap(join([ancestors[later]], current), "rhs", CORES))
            tail = swap(join([ancestors[-1], send_coupling], current), "rhs", CORES)

    tail = hop(cross_levels - 1, ancestors[-1], tail, current)
    others = [gather_cores(tail), keep, keep_near]
    shares = way_down(per_dev, inputs, solved_cross, solved_top, solved_half, cross_packs, others)
    incoming = lax.all_gather(shares, "rhs", axis=0)
    return finish(far_values, own_values, incoming, leaf_coupling)


def solution(mesh):
    placed = (P(None, ("leaf", "rhs")), P("leaf")) + (P("leaf", "rhs", None),) * 6
    return jax.shard_map(
        body, mesh=mesh, in_specs=placed, out_specs=P("leaf", None, "rhs"), check_vma=False
    )
```
